512 devices in a mesh: traj: 8 (over y), blk: 64 (over z, x, core).
Axes of the slice: x: 4, y: 8, z: 8, core: 2. Of those that a mesh axis runs over, the one named last changes fastest.
Arguments:
- codes: bfloat16 [8, 16384, 512], P('traj', 'blk'), may hold values from -127 to 127, as said below
- row_scale: float32 [8, 16384], P('traj', 'blk'), may hold values from 0.1 to 1
- valid: int32 [8], P('traj'), may hold values from 8192 to 16384, as said below
Outputs:
- whitened: bfloat16 [8, 16384, 512], P('traj', 'blk')
- koopman: float32 [512, 512], replicated
The draws below stay inside these ranges and needn't reach their ends.
Inputs may be any that keep to these rules, and one draw needn't show every extreme that they name: `codes`: integer levels. One trajectory has all 16384 frames valid.
All inputs are finite; a program needn't handle non-finite values.
Results may differ from the reference program's by a relative error of at most 0.004.
The reference program's roundings to bfloat16 on the way (of `dequant`, `lead_rows` and `trail_rows`) count: a program that leaves them out, or rounds other values in their place, can miss the bound.
Values may be sent and summed in bfloat16 or wider, within the bound.
A program may use at most 64 MiB of HBM per device.

```python
import math
import jax
import jax.numpy as jnp
from jax import lax

FEAT = 512
LAG = 64
FRAMES = 16384
TRAJ = 8


def draw_codes(key, part):
    key = jax.random.fold_in(key, 11)
    subkeys = jax.random.split(key, 4)
    amplitude = jax.random.randint(subkeys[0], (1, 1, FEAT), 3, 31)
    jitter = jax.random.randint(subkeys[1], (TRAJ, FRAMES, FEAT), -64, 65) * amplitude // 64
    shared_reach = 24
    segment = 2 * LAG
    shared = jax.random.randint(subkeys[2], (TRAJ, FRAMES // segment, 1, FEAT // 16, 1), -shared_reach, shared_reach + 1)
    shared = jnp.broadcast_to(shared, (TRAJ, FRAMES // segment, segment, FEAT // 16, 16)).reshape(TRAJ, FRAMES, FEAT)
    slopes = jax.random.randint(subkeys[3], (TRAJ, 1, FEAT), -30, 31)
    position = jnp.arange(FRAMES, dtype=jnp.int32)[None, :, None]
    trend_part = slopes * (FRAMES + 2 * position) // FRAMES
    levels = jnp.clip(jitter + shared + trend_part, -127, 127)
    return levels.astype(jnp.float32).astype(jnp.bfloat16)


def draw_valid(key, part):
    key = jax.random.fold_in(key, 23)
    subkeys = jax.random.split(key, 2)
    counts = jax.random.randint(subkeys[0], (TRAJ,), FRAMES // 2, FRAMES + 1)
    chosen = jax.random.randint(subkeys[1], (), 0, TRAJ)
    return jnp.where(jnp.arange(TRAJ, dtype=jnp.int32) == chosen, FRAMES, counts).astype(jnp.int32)


def level_of(stream_key, dims, cuts, low, high):
    loudness = 1.0
    for dim, shards_of in cuts:
        steps = jax.random.uniform(jax.random.fold_in(jax.random.fold_in(stream_key, 6), dim), (shards_of,), jnp.float32, low / len(cuts), high / len(cuts))
        loudness = loudness * jnp.repeat(jnp.exp(steps), dims[dim] // shards_of).reshape((-1,) + (1,) * (len(dims) - 1 - dim))
    return loudness


def setup_inputs(seed: int = 0) -> dict:
    splits = jax.random.split(jax.random.key(seed), 4)
    codes = draw_codes(jax.random.fold_in(splits[3], 71), 0)
    row_scale = jnp.clip(jnp.exp(math.log(1.0) - 2.3025851 * jax.random.uniform(splits[1], (TRAJ, FRAMES), jnp.float32) ** level_of(splits[1], (TRAJ, FRAMES), ((0, 8), (1, 64)), -0.2, 0.2)), 0.1, 1.0)
    valid = draw_valid(jax.random.fold_in(splits[3], 71), 0)
    return dict(codes=codes, row_scale=row_scale, valid=valid)


def dequantize(codes_one, scale_one):
    return (codes_one.astype(jnp.float32) * scale_one[:, None]).astype(jnp.bfloat16)

def trajectory_stats(codes_one, scale_one, count_one):
    dequant = dequantize(codes_one, scale_one)
    frames = dequant.shape[0]
    width = dequant.shape[1]
    position = jnp.arange(frames, dtype=jnp.int32)
    paired = position + LAG < count_one
    shifted = jnp.concatenate([dequant[LAG:], jnp.zeros((LAG, width), jnp.bfloat16)], axis=0)
    lead_rows = jnp.where(paired[:, None], dequant, jnp.zeros_like(dequant))
    trail_rows = jnp.where(paired[:, None], shifted, jnp.zeros_like(shifted))
    instant = jnp.dot(lead_rows.T.astype(jnp.float32), lead_rows.astype(jnp.float32), preferred_element_type=jnp.float32) + jnp.dot(trail_rows.T.astype(jnp.float32), trail_rows.astype(jnp.float32), preferred_element_type=jnp.float32)
    crossed = jnp.dot(lead_rows.T.astype(jnp.float32), trail_rows.astype(jnp.float32), preferred_element_type=jnp.float32)
    totals = jnp.sum(lead_rows.astype(jnp.float32), axis=0) + jnp.sum(trail_rows.astype(jnp.float32), axis=0)
    samples = 2.0 * jnp.sum(paired.astype(jnp.float32))
    return (samples, totals, instant, crossed)

def reference(codes, row_scale, valid):
    stacked = lax.map(lambda inputs: trajectory_stats(inputs[0], inputs[1], inputs[2]), (codes, row_scale, valid))
    samples = jnp.sum(stacked[0])
    totals = jnp.sum(stacked[1], axis=0)
    instant = jnp.sum(stacked[2], axis=0)
    crossed = jnp.sum(stacked[3], axis=0)
    average = totals / samples
    outer_mean = jnp.outer(average, average)
    instant_cov = instant / samples - outer_mean
    lagged_cov = (crossed + crossed.T) / samples - outer_mean
    width = instant_cov.shape[0]
    factor = jnp.linalg.cholesky(instant_cov)
    whitener = jax.scipy.linalg.solve_triangular(factor, jnp.eye(width, dtype=jnp.float32), lower=True)
    highest = lax.Precision.HIGHEST
    koopman = jnp.dot(jnp.dot(whitener.astype(jnp.float32), lagged_cov.astype(jnp.float32), precision=highest, preferred_element_type=jnp.float32).astype(jnp.float32), whitener.T.astype(jnp.float32), precision=highest, preferred_element_type=jnp.float32)

    def project(inputs):
        dequant = dequantize(inputs[0], inputs[1])
        centered = dequant.astype(jnp.float32) - average[None, :]
        return jnp.dot(centered.astype(jnp.float32), whitener.T.astype(jnp.float32), precision=highest, preferred_element_type=jnp.float32).astype(jnp.bfloat16)
    whitened = lax.map(project, (codes, row_scale))
    return (whitened, koopman)
```

```python
import functools

import jax
import jax.numpy as jnp
from jax import lax
from jax.experimental import pallas as pl
from jax.experimental.pallas import tpu as pltpu
from jax.sharding import PartitionSpec as P

MESH = pl.DeviceIdType.MESH
LAG = 64
HALF = 1088
PARTS = (
    (0, 512, "x", (("rs", "y"), ("ar", "z"), ("ag", "y"))),
    (512, 256, "y", (("ar", "z"), ("ar", "x"))),
    (768, 320, "z", (("ar", "x"), ("ar", "y"))),
)
SIZE = {"x": 4, "y": 8, "z": 8}


def all_steps(part):
    return (("rs", part[2]),) + part[3] + (("ag", part[2]),)


def sum_kernel(p_ref, out_ref, acc, rcore, *rest):
    n_bufs = sum(kind != "ag" for part in PARTS for kind, _ in all_steps(part))
    bufs, sums, (send, recv, csend, crecv) = rest[:n_bufs], rest[n_bufs:-4], rest[-4:]
    traj, blk = lax.axis_index("traj"), lax.axis_index("blk")
    core = lax.rem(blk, 2)
    at = {"x": lax.rem(lax.div(blk, 2), 4), "y": traj, "z": lax.div(blk, 8)}

    def device(axis, index):
        if axis == "x":
            return (traj, at["z"] * 8 + index * 2 + core)
        if axis == "y":
            return (index, blk)
        return (traj, index * 8 + at["x"] * 2 + core)

    partner = (traj, blk + 1 - 2 * core)
    other = 1 - core

    barrier = pltpu.get_barrier_semaphore()
    pl.semaphore_signal(barrier, inc=1, device_id=partner, device_id_type=MESH)
    for axis, size in SIZE.items():
        for d in range(1, size):
            pl.semaphore_signal(
                barrier, inc=1, device_id=device(axis, lax.rem(at[axis] + d, size)), device_id_type=MESH
            )
    pl.semaphore_wait(barrier, 1 + sum(size - 1 for size in SIZE.values()))

    def copy(src, dst, s, r, to):
        return pltpu.make_async_remote_copy(
            src_ref=src, dst_ref=dst, send_sem=s, recv_sem=r, device_id=to, device_id_type=MESH
        )

    waiting = []
    swaps = []
    for k, (base, rows, _, _) in enumerate(PARTS):
        c = copy(
            p_ref.at[other, pl.ds(base, rows)],
            rcore.at[pl.ds(base, rows)],
            csend.at[0, k],
            crecv.at[0, k],
            partner,
        )
        c.start()
        swaps.append(c)

    class Run:
        pass

    runs = []
    sem_at = 0
    buf_at = 0
    for k, part in enumerate(PARTS):
        run = Run()
        run.base, run.rows = part[0], part[1]
        run.steps = []
        for kind, axis in all_steps(part):
            step = Run()
            step.kind, step.axis, step.sem = kind, axis, sem_at
            sem_at += SIZE[axis]
            if kind != "ag":
                step.buf, step.sum = bufs[buf_at], sums[buf_at]
                buf_at += 1
            run.steps.append(step)
        runs.append(run)

    def begin(run, n):
        step = run.steps[n]
        axis, size = step.axis, SIZE[step.axis]
        me = at[axis]
        step.copies = []
        if step.kind == "rs":
            rows = run.now_rows // size
            for d in range(1, size):
                to = lax.rem(me + d, size)
                src = run.now.at[pl.ds(pl.multiple_of(run.now_at + to * rows, 8), rows)]
                c = copy(src, step.buf.at[d - 1], send.at[step.sem + d], recv.at[step.sem + d], device(axis, to))
                c.start()
                step.copies.append(c)
        elif step.kind == "ar":
            rows = run.now_rows
            for d in range(1, size):
                to = lax.rem(me + d, size)
                c = copy(
                    run.now.at[pl.ds(run.now_at, rows)],
                    step.buf.at[me],
                    send.at[step.sem + d],
                    recv.at[step.sem + me],
                    device(axis, to),
                )
                c.start()
                step.copies.append(c)
            step.buf[me] = run.now[pl.ds(run.now_at, rows)]
        else:
            rows = run.now_rows
            place = out_ref.at[core, pl.ds(run.home, rows)]
            for d in range(1, size):
                to = lax.rem(me + d, size)
                c = copy(place, place, send.at[step.sem + d], recv.at[step.sem + d], device(axis, to))
                c.start()
                step.copies.append(c)

    def finish(run, n):
        step = run.steps[n]
        axis, size = step.axis, SIZE[step.axis]
        me = at[axis]
        if step.kind == "rs":
            rows = run.now_rows // size
            mine = pl.multiple_of(run.now_at + me * rows, 8)
            total = run.now[pl.ds(mine, rows)]
            for d in range(1, size):
                step.copies[d - 1].wait_recv()
                total = total + step.buf[d - 1]
            step.sum[...] = total
            run.place.append((axis, rows))
            run.now, run.now_at, run.now_rows = step.sum, 0, rows
            run.home = run.home + me * rows
        elif step.kind == "ar":
            rows = run.now_rows
            for d in range(1, size):
                come = lax.rem(me + d, size)
                copy(
                    run.now.at[pl.ds(run.now_at, rows)],
                    step.buf.at[come],
                    send.at[step.sem + d],
                    recv.at[step.sem + come],
                    device(axis, come),
                ).wait_recv()
            total = step.buf[0]
            for j in range(1, size):
                total = total + step.buf[j]
            step.sum[...] = total
            run.now, run.now_at = step.sum, 0
        else:
            for c in step.copies:
                c.wait_recv()
            run.place.pop()
            run.home = run.home - me * run.now_rows
            run.now_rows = run.now_rows * size
        waiting.extend(step.copies)
        if n + 1 < len(run.steps) and run.steps[n + 1].kind == "ag" and step.kind != "ag":
            run.home = pl.multiple_of(run.home, 8)
            out_ref[core, pl.ds(run.home, run.now_rows)] = run.now[...]

    for k, run in enumerate(runs):
        swaps[k].wait_recv()
        rows = pl.ds(run.base, run.rows)
        acc[rows] = p_ref[core, rows] + rcore[rows]
        run.now, run.now_at, run.now_rows = acc, run.base, run.rows
        run.home, run.place = run.base, []
        begin(run, 0)
    last = []
    for n in range(max(len(run.steps) for run in runs)):
        for k, run in enumerate(runs):
            if n < len(run.steps):
                finish(run, n)
                if n + 1 < len(run.steps):
                    begin(run, n + 1)
                else:
                    place = out_ref.at[core, pl.ds(run.base, run.rows)]
                    c = copy(place, place, csend.at[1, k], crecv.at[1, k], partner)
                    c.start()
                    last.append(c)
    for c in last:
        c.wait_recv()
    for c in swaps + waiting + last:
        c.wait_send()


def sum_over_devices(packed):
    bufs, sums, sems = [], [], 0
    for part in PARTS:
        rows = part[1]
        for kind, axis in all_steps(part):
            size = SIZE[axis]
            sems += size
            if kind == "rs":
                rows //= size
                bufs.append(pltpu.VMEM((size - 1, rows, 128), jnp.float32))
                sums.append(pltpu.VMEM((rows, 128), jnp.float32))
            elif kind == "ar":
                bufs.append(pltpu.VMEM((size, rows, 128), jnp.float32))
                sums.append(pltpu.VMEM((rows, 128), jnp.float32))
    return pl.pallas_call(
        sum_kernel,
        out_shape=jax.ShapeDtypeStruct(packed.shape, jnp.float32),
        in_specs=[pl.BlockSpec(memory_space=pltpu.VMEM)],
        out_specs=pl.BlockSpec(memory_space=pltpu.VMEM),
        scratch_shapes=[
            pltpu.VMEM((HALF, 128), jnp.float32),
            pltpu.VMEM((HALF, 128), jnp.float32),
            *bufs,
            *sums,
            pltpu.SemaphoreType.DMA((sems,)),
            pltpu.SemaphoreType.DMA((sems,)),
            pltpu.SemaphoreType.DMA((2, len(PARTS))),
            pltpu.SemaphoreType.DMA((2, len(PARTS))),
        ],
        compiler_params=pltpu.CompilerParams(
            collective_id=0, has_side_effects=True, vmem_limit_bytes=40 * 2**20
        ),
        name="sum_over_devices",
    )(packed)


def passed_along(shard, axis, by):
    size = lax.axis_size(axis)
    pairs = [(i, i + by) for i in range(size) if 0 <= i + by < size]
    return lax.ppermute(shard, axis, pairs)


def gram_matrix(left_rows, right_rows):
    return lax.dot_general(
        left_rows, right_rows, (((0,), (0,)), ((), ())), preferred_element_type=jnp.float32
    )


def panels(matrix):
    return [matrix[:, 128 * j : 128 * (j + 1)] for j in range(4)]


def on_device(codes, row_scale, valid):
    frames = codes.shape[1]
    width = codes.shape[2]
    highest = lax.Precision.HIGHEST
    dequant = (codes[0].astype(jnp.float32) * row_scale[0][:, None]).astype(jnp.bfloat16)
    incoming = passed_along(dequant[:LAG], "blk", -1)
    shifted = jnp.concatenate([dequant[LAG:], incoming], axis=0)
    position = lax.axis_index("blk") * frames + jnp.arange(frames, dtype=jnp.int32)
    paired = position + LAG < valid[0]
    lead_rows = jnp.where(paired[:, None], dequant, jnp.zeros_like(dequant))
    trail_rows = jnp.where(paired[:, None], shifted, jnp.zeros_like(shifted))
    both = jnp.concatenate([lead_rows, trail_rows], axis=0)
    swapped = jnp.concatenate([trail_rows, lead_rows], axis=0)
    instant = gram_matrix(both, both)
    lagged = gram_matrix(both, swapped)
    totals = jnp.sum(both, axis=0, dtype=jnp.float32)
    samples = 2.0 * jnp.sum(paired.astype(jnp.float32))

    lower = jnp.arange(width)[:, None] >= jnp.arange(width)[None, :]
    mixed = panels(jnp.where(lower, instant, lagged))
    diagonal = jnp.sum(jnp.where(jnp.eye(width, dtype=bool), lagged, 0.0), axis=0)
    vectors = jnp.concatenate([diagonal.reshape(4, 128), totals.reshape(4, 128)], axis=0)
    count = jnp.full((8, 128), samples)
    rest = jnp.zeros((56, 128), jnp.float32)
    packed = jnp.stack(
        [
            jnp.concatenate([mixed[0], mixed[1], vectors, rest], axis=0),
            jnp.concatenate([mixed[2], mixed[3], count, rest], axis=0),
        ]
    )
    summed = sum_over_devices(packed)
    mixed = jnp.concatenate(
        [summed[0, :512], summed[0, 512:1024], summed[1, :512], summed[1, 512:1024]], axis=1
    )
    diagonal = summed[0, 1024:1028].reshape(width)
    totals = summed[0, 1028:1032].reshape(width)
    samples = summed[1, 1024, 0]
    instant = jnp.where(lower, mixed, mixed.T)
    lagged_sum = jnp.where(lower, mixed.T, mixed)
    lagged_sum = jnp.where(jnp.eye(width, dtype=bool), diagonal[None, :], lagged_sum)

    average = totals / samples
    outer_mean = jnp.outer(average, average)
    instant_cov = instant / samples - outer_mean
    lagged_cov = lagged_sum / samples - outer_mean
    factor = jnp.linalg.cholesky(instant_cov)
    whitener = jax.scipy.linalg.solve_triangular(
        factor, jnp.eye(width, dtype=jnp.float32), lower=True
    )
    koopman = jnp.dot(
        jnp.dot(whitener, lagged_cov, precision=highest, preferred_element_type=jnp.float32),
        whitener.T,
        precision=highest,
        preferred_element_type=jnp.float32,
    )
    centered = dequant.astype(jnp.float32) - average[None, :]
    projected = lax.dot_general(
        centered,
        whitener,
        (((1,), (1,)), ((), ())),
        precision=highest,
        preferred_element_type=jnp.float32,
    )
    return (projected.astype(jnp.bfloat16)[None], koopman)


def solution(mesh):
    return jax.shard_map(
        on_device,
        mesh=mesh,
        in_specs=(P("traj", "blk", None), P("traj", "blk"), P("traj")),
        out_specs=(P("traj", "blk", None), P()),
        check_vma=False,
    )
```

```python
import functools

import jax
import jax.numpy as jnp
from jax import lax
from jax.experimental import pallas as pl
from jax.experimental.pallas import tpu as pltpu
from jax.sharding import PartitionSpec as P

MESH = pl.DeviceIdType.MESH
LAG = 64
HALF = 1088
PARTS = (
    (0, 512, "x", (("rs", "y"), ("ar", "z"), ("ag", "y"))),
    (512, 256, "y", (("ar", "z"), ("ar", "x"))),
    (768, 320, "z", (("ar", "x"), ("ar", "y"))),
)
SIZE = {"x": 4, "y": 8, "z": 8}


def all_steps(part):
    return (("rs", part[2]),) + part[3] + (("ag", part[2]),)


def sum_kernel(p_ref, out_ref, acc, rcore, *rest):
    n_bufs = sum(kind != "ag" for part in PARTS for kind, _ in all_steps(part))
    bufs, sums, (send, recv, csend, crecv) = rest[:n_bufs], rest[n_bufs:-4], rest[-4:]
    traj, blk = lax.axis_index("traj"), lax.axis_index("blk")
    core = lax.rem(blk, 2)
    at = {"x": lax.rem(lax.div(blk, 2), 4), "y": traj, "z": lax.div(blk, 8)}

    def device(axis, index):
        if axis == "x":
            return (traj, at["z"] * 8 + index * 2 + core)
        if axis == "y":
            return (index, blk)
        return (traj, index * 8 + at["x"] * 2 + core)

    partner = (traj, blk + 1 - 2 * core)
    other = 1 - core

    barrier = pltpu.get_barrier_semaphore()
    pl.semaphore_signal(barrier, inc=1, device_id=partner, device_id_type=MESH)
    for axis, size in SIZE.items():
        for d in range(1, size):
            pl.semaphore_signal(
                barrier, inc=1, device_id=device(axis, lax.rem(at[axis] + d, size)), device_id_type=MESH
            )
    pl.semaphore_wait(barrier, 1 + sum(size - 1 for size in SIZE.values()))

    def copy(src, dst, s, r, to):
        return pltpu.make_async_remote_copy(
            src_ref=src, dst_ref=dst, send_sem=s, recv_sem=r, device_id=to, device_id_type=MESH
        )

    waiting = []
    swaps = []
    for k, (base, rows, _, _) in enumerate(PARTS):
        c = copy(
            p_ref.at[other, pl.ds(base, rows)],
            rcore.at[pl.ds(base, rows)],
            csend.at[0, k],
            crecv.at[0, k],
            partner,
        )
        c.start()
        swaps.append(c)

    class Run:
        pass

    runs = []
    sem_at = 0
    buf_at = 0
    for k, part in enumerate(PARTS):
        run = Run()
        run.base, run.rows = part[0], part[1]
        run.steps = []
        for kind, axis in all_steps(part):
            step = Run()
            step.kind, step.axis, step.sem = kind, axis, sem_at
            sem_at += SIZE[axis]
            if kind != "ag":
                step.buf, step.sum = bufs[buf_at], sums[buf_at]
                buf_at += 1
            run.steps.append(step)
        runs.append(run)

    def begin(run, n):
        step = run.steps[n]
        axis, size = step.axis, SIZE[step.axis]
        me = at[axis]
        step.copies = []
        if step.kind == "rs":
            rows = run.now_rows // size
            for d in range(1, size):
                to = lax.rem(me + d, size)
                src = run.now.at[pl.ds(pl.multiple_of(run.now_at + to * rows, 8), rows)]
                c = copy(src, step.buf.at[d - 1], send.at[step.sem + d], recv.at[step.sem + d], device(axis, to))
                c.start()
                step.copies.append(c)
        elif step.kind == "ar":
            rows = run.now_rows
            for d in range(1, size):
                to = lax.rem(me + d, size)
                c = copy(
                    run.now.at[pl.ds(run.now_at, rows)],
                    step.buf.at[me],
                    send.at[step.sem + d],
                    recv.at[step.sem + me],
                    device(axis, to),
                )
                c.start()
                step.copies.append(c)
            step.buf[me] = run.now[pl.ds(run.now_at, rows)]
        else:
            rows = run.now_rows
            place = out_ref.at[core, pl.ds(run.home, rows)]
            for d in range(1, size):
                to = lax.rem(me + d, size)
                c = copy(place, place, send.at[step.sem + d], recv.at[step.sem + d], device(axis, to))
                c.start()
                step.copies.append(c)

    def finish(run, n):
        step = run.steps[n]
        axis, size = step.axis, SIZE[step.axis]
        me = at[axis]
        if step.kind == "rs":
            rows = run.now_rows // size
            mine = pl.multiple_of(run.now_at + me * rows, 8)
            total = run.now[pl.ds(mine, rows)]
            for d in range(1, size):
                step.copies[d - 1].wait_recv()
                total = total + step.buf[d - 1]
            step.sum[...] = total
            run.place.append((axis, rows))
            run.now, run.now_at, run.now_rows = step.sum, 0, rows
            run.home = run.home + me * rows
        elif step.kind == "ar":
            rows = run.now_rows
            for d in range(1, size):
                come = lax.rem(me + d, size)
                copy(
                    run.now.at[pl.ds(run.now_at, rows)],
                    step.buf.at[come],
                    send.at[step.sem + d],
                    recv.at[step.sem + come],
                    device(axis, come),
                ).wait_recv()
            total = step.buf[0]
            for j in range(1, size):
                total = total + step.buf[j]
            step.sum[...] = total
            run.now, run.now_at = step.sum, 0
        else:
            for c in step.copies:
                c.wait_recv()
            run.place.pop()
            run.home = run.home - me * run.now_rows
            run.now_rows = run.now_rows * size
        waiting.extend(step.copies)
        if n + 1 < len(run.steps) and run.steps[n + 1].kind == "ag" and step.kind != "ag":
            run.home = pl.multiple_of(run.home, 8)
            out_ref[core, pl.ds(run.home, run.now_rows)] = run.now[...]

    for k, run in enumerate(runs):
        swaps[k].wait_recv()
        rows = pl.ds(run.base, run.rows)
        acc[rows] = p_ref[core, rows] + rcore[rows]
        run.now, run.now_at, run.now_rows = acc, run.base, run.rows
        run.home, run.place = run.base, []
        begin(run, 0)
    last = []
    for n in range(max(len(run.steps) for run in runs)):
        for k, run in enumerate(runs):
            if n < len(run.steps):
                finish(run, n)
                if n + 1 < len(run.steps):
                    begin(run, n + 1)
                else:
                    place = out_ref.at[core, pl.ds(run.base, run.rows)]
                    c = copy(place, place, csend.at[1, k], crecv.at[1, k], partner)
                    c.start()
                    last.append(c)
    for c in last:
        c.wait_recv()
    for c in swaps + waiting + last:
        c.wait_send()


def sum_over_devices(packed):
    bufs, sums, sems = [], [], 0
    for part in PARTS:
        rows = part[1]
        for kind, axis in all_steps(part):
            size = SIZE[axis]
            sems += size
            if kind == "rs":
                rows //= size
                bufs.append(pltpu.VMEM((size - 1, rows, 128), jnp.float32))
                sums.append(pltpu.VMEM((rows, 128), jnp.float32))
            elif kind == "ar":
                bufs.append(pltpu.VMEM((size, rows, 128), jnp.float32))
                sums.append(pltpu.VMEM((rows, 128), jnp.float32))
    return pl.pallas_call(
        sum_kernel,
        out_shape=jax.ShapeDtypeStruct(packed.shape, jnp.float32),
        in_specs=[pl.BlockSpec(memory_space=pltpu.VMEM)],
        out_specs=pl.BlockSpec(memory_space=pltpu.VMEM),
        scratch_shapes=[
            pltpu.VMEM((HALF, 128), jnp.float32),
            pltpu.VMEM((HALF, 128), jnp.float32),
            *bufs,
            *sums,
            pltpu.SemaphoreType.DMA((sems,)),
            pltpu.SemaphoreType.DMA((sems,)),
            pltpu.SemaphoreType.DMA((2, len(PARTS))),
            pltpu.SemaphoreType.DMA((2, len(PARTS))),
        ],
        compiler_params=pltpu.CompilerParams(
            collective_id=0, has_side_effects=True, vmem_limit_bytes=40 * 2**20
        ),
        name="sum_over_devices",
    )(packed)


HIGHEST = lax.Precision.HIGHEST
ROWS = (((1,), (0,)), ((), ()))
LANES = (((1,), (1,)), ((), ()))
SUBLANES = (((0,), (0,)), ((), ()))


def dot(left, right, dims, precision=HIGHEST):
    return lax.dot_general(left, right, dims, precision=precision, preferred_element_type=jnp.float32)


def reciprocal(x):
    r = pl.reciprocal(x, approx=True)
    return r * (2.0 - x * r)


def one_row(x, k):
    return jnp.broadcast_to(x[k : k + 1, :], (8, 128))


def one_lane(x, k):
    return jnp.broadcast_to(x[:, k : k + 1], (8, 128))


def inverse_factor(block):
    rows = list(block)
    n = len(rows)
    sub = lax.broadcasted_iota(jnp.int32, (8, 128), 0)
    lane = lax.broadcasted_iota(jnp.int32, (8, 128), 1)
    pivots = [None] * n
    for r in range(n):
        first = 8 * r
        columns = [[one_lane(rows[q], first + k) for q in range(r, n)] for k in range(8)]
        inside = (lane >= first) & (lane < first + 8)
        panel = jnp.where(inside, jnp.where(lane - first == sub, 1.0, 0.0), rows[r])
        factors = []
        for k in range(8):
            pivot = reciprocal(one_row(columns[k][0], k))
            pivots[r] = pivot if k == 0 else jnp.where(sub == k, pivot, pivots[r])
            factor = [column * pivot for column in columns[k]]
            factor[0] = jnp.where(sub > k, factor[0], 0.0)
            factors.append(factor)
            for m in range(k + 1, 8):
                entry = one_row(columns[k][0], m)
                columns[m] = [x - f * entry for x, f in zip(columns[m], factor)]
            panel = panel - factor[0] * one_row(panel, k)
        rows[r] = panel
        panel_rows = [one_row(panel, k) for k in range(8)]
        for q in range(r + 1, n):
            x = jnp.where(inside, 0.0, rows[q])
            for k in range(8):
                x = x - factors[k][q - r] * panel_rows[k]
            rows[q] = x
    return [jnp.where(lane <= sub + 8 * q, rows[q], 0.0) * jnp.sqrt(pivots[q]) for q in range(n)]


def split3(x):
    high = x.astype(jnp.bfloat16)
    rest = x - high.astype(jnp.float32)
    middle = rest.astype(jnp.bfloat16)
    return high, middle, (rest - middle.astype(jnp.float32)).astype(jnp.bfloat16)


def finish_kernel(sum_ref, x_ref, white_ref, koop_ref, A, S, lhs):
    f32 = jnp.float32
    ri = lax.broadcasted_iota(jnp.int32, (128, 128), 0)
    ci = lax.broadcasted_iota(jnp.int32, (128, 128), 1)
    inv = 1.0 / sum_ref[1, 1024:1025, :]
    avg = [sum_ref[0, 1028+j:1029+j, :] * inv for j in range(4)]
    avgT = [jnp.transpose(jnp.broadcast_to(a, (128,128))) for a in avg]
    lagdiag = [sum_ref[0, 1024+j:1025+j, :] * inv for j in range(4)]
    def packed(i, j):
        return sum_ref[j//2, (j%2)*512+128*i:(j%2)*512+128*i+128, :] * inv
    def blk(i): return slice(128*i, 128*i+128)
    for i in range(4):
        for j in range(4):
            outer = avgT[i] * avg[j]
            p = packed(i, j)
            if i < j:
                A[blk(i), blk(j)] = p - outer
            elif i > j:
                S[blk(i), blk(j)] = p - outer
                A[blk(i), blk(j)] = jnp.zeros((128,128), f32)
            else:
                t = jnp.transpose(p)
                A[blk(i), blk(i)] = jnp.where(ri <= ci, p, t) - outer
                half = 0.5 * (lagdiag[i] - avg[i] * avg[i])
                S[blk(i), blk(i)] = jnp.where(ri > ci, p - outer, jnp.where(ri == ci, half, 0.0))
    for k in range(4):
        V = [A[128*k+8*q:128*k+8*q+8, blk(k)] for q in range(16)]
        W = jnp.concatenate(inverse_factor(V), axis=0)
        if k == 0:
            R = dot(W, A[blk(0), 128:], ROWS)
            A[blk(0), 128:] = R
        else:
            R = dot(W, A[blk(k), :], ROWS)
            A[blk(k), :] = R
        A[blk(k), blk(k)] = W
        if k < 3:
            Rr = A[blk(k), 128*(k+1):]
            upd = dot(Rr, A[blk(k), :], SUBLANES)
            A[128*(k+1):, blk(k)] = -upd[:, blk(k)]
            if k > 0:
                A[128*(k+1):, 0:128*k] = A[128*(k+1):, 0:128*k] - upd[:, 0:128*k]
            A[128*(k+1):, 128*(k+1):] = A[128*(k+1):, 128*(k+1):] - upd[:, 128*(k+1):]
    z = jnp.zeros((128,128), f32)
    A[blk(0), blk(1)] = z
    A[blk(2), blk(3)] = z
    S[blk(0), blk(1)] = z
    S[blk(2), blk(3)] = z
    a = [A[0:256, 0:256], A[256:512, 0:256], A[256:512, 256:512]]
    s = [S[0:256, 0:256], S[256:512, 0:256], S[256:512, 256:512]]
    x = x_ref[...]
    lhs[0:256, :] = x
    am = [jnp.concatenate([t[m] for t in [split3(q) for q in avg]], axis=1) for m in range(3)]
    lhs[256:272, :] = jnp.concatenate(am + [jnp.zeros((13, 512), jnp.bfloat16)], axis=0)
    y = [None, None]
    for t in split3(a[0]):
        v = dot(lhs[:, 0:256], t, LANES, None)
        y[0] = v if y[0] is None else y[0] + v
    for t, u in zip(split3(a[1]), split3(a[2])):
        v = dot(lhs[:, 0:256], t, LANES, None) + dot(lhs[:, 256:512], u, LANES, None)
        y[1] = v if y[1] is None else y[1] + v
    for h in range(2):
        m = y[h][256:257] + y[h][257:258] + y[h][258:259]
        white_ref[:, 256*h:256*h+256] = (y[h][0:256] - m).astype(jnp.bfloat16)
    nn = ROWS; nt = LANES
    t00 = dot(a[0], s[0], nn)
    t10 = dot(a[1], s[0], nn) + dot(a[2], s[1], nn)
    t11 = dot(a[2], s[2], nn)
    k00 = dot(t00, a[0], nt)
    k01 = dot(t00, a[1], nt)
    k10 = dot(t10, a[0], nt)
    k11 = dot(t10, a[1], nt) + dot(t11, a[2], nt)
    koop_ref[0:256, 0:256] = k00 + jnp.transpose(k00)
    koop_ref[256:512, 256:512] = k11 + jnp.transpose(k11)
    k10 = k10 + jnp.transpose(k01)
    koop_ref[256:512, 0:256] = k10
    koop_ref[0:256, 256:512] = jnp.transpose(k10)


def finish(summed, x):
    width = x.shape[1]
    return pl.pallas_call(
        finish_kernel,
        out_shape=(
            jax.ShapeDtypeStruct(x.shape, jnp.bfloat16),
            jax.ShapeDtypeStruct((width, width), jnp.float32),
        ),
        in_specs=[pl.BlockSpec(memory_space=pltpu.VMEM)] * 2,
        out_specs=(pl.BlockSpec(memory_space=pltpu.VMEM),) * 2,
        scratch_shapes=[
            pltpu.VMEM((width, width), jnp.float32),
            pltpu.VMEM((width, width), jnp.float32),
            pltpu.VMEM((x.shape[0] + 16, width), jnp.bfloat16),
        ],
        compiler_params=pltpu.CompilerParams(vmem_limit_bytes=40 * 2**20),
        name="finish",
    )(summed, x)


def passed_along(shard, axis, by):
    size = lax.axis_size(axis)
    pairs = [(i, i + by) for i in range(size) if 0 <= i + by < size]
    return lax.ppermute(shard, axis, pairs)


def gram_matrix(left_rows, right_rows):
    return lax.dot_general(
        left_rows, right_rows, (((0,), (0,)), ((), ())), preferred_element_type=jnp.float32
    )


def panels(matrix):
    return [matrix[:, 128 * j : 128 * (j + 1)] for j in range(4)]


def on_device(codes, row_scale, valid):
    frames = codes.shape[1]
    width = codes.shape[2]
    dequant = (codes[0].astype(jnp.float32) * row_scale[0][:, None]).astype(jnp.bfloat16)
    incoming = passed_along(dequant[:LAG], "blk", -1)
    shifted = jnp.concatenate([dequant[LAG:], incoming], axis=0)
    position = lax.axis_index("blk") * frames + jnp.arange(frames, dtype=jnp.int32)
    paired = position + LAG < valid[0]
    lead_rows = jnp.where(paired[:, None], dequant, jnp.zeros_like(dequant))
    trail_rows = jnp.where(paired[:, None], shifted, jnp.zeros_like(shifted))
    both = jnp.concatenate([lead_rows, trail_rows], axis=0)
    swapped = jnp.concatenate([trail_rows, lead_rows], axis=0)
    instant = gram_matrix(both, both)
    lagged = gram_matrix(both, swapped)
    totals = jnp.sum(both, axis=0, dtype=jnp.float32)
    samples = 2.0 * jnp.sum(paired.astype(jnp.float32))

    upper = jnp.arange(width)[:, None] <= jnp.arange(width)[None, :]
    mixed = panels(jnp.where(upper, instant, lagged))
    diagonal = jnp.sum(jnp.where(jnp.eye(width, dtype=bool), lagged, 0.0), axis=0)
    vectors = jnp.concatenate([diagonal.reshape(4, 128), totals.reshape(4, 128)], axis=0)
    count = jnp.full((8, 128), samples)
    rest = jnp.zeros((56, 128), jnp.float32)
    packed = jnp.stack(
        [
            jnp.concatenate([mixed[0], mixed[1], vectors, rest], axis=0),
            jnp.concatenate([mixed[2], mixed[3], count, rest], axis=0),
        ]
    )
    summed = sum_over_devices(packed)
    projected, koopman = finish(summed, dequant)
    return (projected[None], koopman)


def solution(mesh):
    return jax.shard_map(
        on_device,
        mesh=mesh,
        in_specs=(P("traj", "blk", None), P("traj", "blk"), P("traj")),
        out_specs=(P("traj", "blk", None), P()),
        check_vma=False,
    )
```

```python
import jax
import jax.numpy as jnp
from jax import lax
from jax.experimental import pallas as pl
from jax.experimental.pallas import tpu as pltpu
from jax.sharding import PartitionSpec as P

MESH = pl.DeviceIdType.MESH
LAG = 64
HALF = 576
PARTS = (
    (0, 256, "x", (("rs", "y"), ("ar", "z"), ("ag", "y"))),
    (256, 128, "y", (("ar", "z"), ("ar", "x"))),
    (384, 192, "z", (("ar", "x"), ("ar", "y"))),
)
SIZE = {"x": 4, "y": 8, "z": 8}
FAR = {4: (2, 1, 3), 8: (4, 3, 5, 2, 6, 1, 7)}
BLOCKS = (((0, 1), (1, 2)), ((0, 2), (1, 3)), ((0, 3), (2, 3)), ((0, 0), (2, 2)), ((1, 1), (3, 3)))


def all_steps(part):
    return (("rs", part[2]),) + part[3] + (("ag", part[2]),)


class Record:
    pass


class Place:
    def __init__(self):
        self.traj, self.blk = lax.axis_index("traj"), lax.axis_index("blk")
        self.core = lax.rem(self.blk, 2)
        self.chip = lax.div(self.blk, 2)
        self.at = {"x": lax.rem(self.chip, 4), "y": self.traj, "z": lax.div(self.blk, 8)}
        self.partner = (self.traj, self.blk + 1 - 2 * self.core)

    def device(self, axis, index):
        if axis == "x":
            return (self.traj, self.at["z"] * 8 + index * 2 + self.core)
        if axis == "y":
            return (index, self.blk)
        return (self.traj, index * 8 + self.at["x"] * 2 + self.core)


def remote(src, dst, send, recv, to):
    return pltpu.make_async_remote_copy(
        src_ref=src, dst_ref=dst, send_sem=send, recv_sem=recv, device_id=to, device_id_type=MESH
    )


class Stream:
    def __init__(self, place, acc, out, bufs, sums, send, recv, core_send, core_recv):
        self.place, self.acc, self.out = place, acc, out
        self.send, self.recv = send, recv
        self.core_send, self.core_recv = core_send, core_recv
        self.waiting, self.last, self.runs = [], [], []
        sem_at = buf_at = 0
        for part in PARTS:
            run = Record()
            run.base, run.rows = part[0], part[1]
            run.steps = []
            for kind, axis in all_steps(part):
                step = Record()
                step.kind, step.axis, step.sem = kind, axis, sem_at
                sem_at += SIZE[axis]
                if kind != "ag":
                    step.buf, step.sum = bufs[buf_at], sums[buf_at]
                    buf_at += 1
                run.steps.append(step)
            self.runs.append(run)
        self.n_steps = max(len(run.steps) for run in self.runs)

    def start(self):
        for run in self.runs:
            run.now, run.now_at, run.now_rows = self.acc, run.base, run.rows
            run.home = run.base
        for run in self.runs[::-1]:
            self.begin(run, 0)

    def advance(self, n):
        for k, run in enumerate(self.runs):
            if n < len(run.steps):
                self.finish(run, n)
                if n + 1 < len(run.steps):
                    self.begin(run, n + 1)
                else:
                    rows = self.out.at[self.place.core, pl.ds(run.base, run.rows)]
                    c = remote(rows, rows, self.core_send.at[k], self.core_recv.at[k], self.place.partner)
                    c.start()
                    self.last.append(c)

    def arrive(self):
        for c in self.last:
            c.wait_recv()

    def close(self):
        for c in self.waiting + self.last:
            c.wait_send()

    def begin(self, run, n):
        step = run.steps[n]
        axis, size = step.axis, SIZE[step.axis]
        me = self.place.at[axis]
        step.copies = {}
        for d in FAR[size]:
            to = lax.rem(me + d, size)
            if step.kind == "rs":
                rows = run.now_rows // size
                src = run.now.at[pl.ds(pl.multiple_of(run.now_at + to * rows, 8), rows)]
                dst, slot = step.buf.at[d - 1], d
            elif step.kind == "ar":
                src = run.now.at[pl.ds(run.now_at, run.now_rows)]
                dst, slot = step.buf.at[me], me
            else:
                src = dst = self.out.at[self.place.core, pl.ds(run.home, run.now_rows)]
                slot = d
            step.copies[d] = remote(
                src, dst, self.send.at[step.sem + d], self.recv.at[step.sem + slot], self.place.device(axis, to)
            )
            step.copies[d].start()
        if step.kind == "ar":
            step.buf[me] = run.now[pl.ds(run.now_at, run.now_rows)]
        self.waiting.extend(step.copies.values())

    def finish(self, run, n):
        step = run.steps[n]
        axis, size = step.axis, SIZE[step.axis]
        me = self.place.at[axis]
        near = FAR[size][::-1]
        if step.kind == "rs":
            rows = run.now_rows // size
            total = run.now[pl.ds(pl.multiple_of(run.now_at + me * rows, 8), rows)]
            for d in near:
                step.copies[d].wait_recv()
                total = total + step.buf[d - 1]
            step.sum[...] = total
            run.now, run.now_at, run.now_rows = step.sum, 0, rows
            run.home = run.home + me * rows
        elif step.kind == "ar":
            for d in near:
                come = lax.rem(me + d, size)
                remote(
                    run.now.at[pl.ds(run.now_at, run.now_rows)],
                    step.buf.at[come],
                    self.send.at[step.sem + d],
                    self.recv.at[step.sem + come],
                    self.place.device(axis, come),
                ).wait_recv()
            total = step.buf[0]
            for j in range(1, size):
                total = total + step.buf[j]
            step.sum[...] = total
            run.now, run.now_at = step.sum, 0
        else:
            for d in near:
                step.copies[d].wait_recv()
            run.home = run.home - me * run.now_rows
            run.now_rows = run.now_rows * size
        if n + 1 < len(run.steps) and run.steps[n + 1].kind == "ag":
            run.home = pl.multiple_of(run.home, 8)
            if step.kind != "ag":
                self.out[self.place.core, pl.ds(run.home, run.now_rows)] = run.now[...]


def moments_kernel(codes_ref, scale_ref, valid_ref, inst_ref, lag_ref, frames, turned, weighted, trailing, acc, *rest):
    (frame_send, frame_recv), rest = rest[:2], rest[2:]
    n = sum(kind != "ag" for part in PARTS for kind, _ in all_steps(part))
    place = Place()
    core = place.core
    streams = []
    for s, out in enumerate((inst_ref, lag_ref)):
        bufs, sums, sems = rest[:n], rest[n : 2 * n], rest[2 * n : 2 * n + 4]
        rest = rest[2 * n + 4 :]
        streams.append(Stream(place, acc.at[s], out, bufs, sums, *sems))
    instant, lagged = streams

    chips = 32
    before = lax.rem(place.chip + chips - 1, chips)
    after = lax.rem(place.chip + 1, chips)
    barrier = pltpu.get_barrier_semaphore()
    greeted = [place.partner, (place.traj, after * 2)]
    for axis, size in SIZE.items():
        greeted += [place.device(axis, lax.rem(place.at[axis] + d, size)) for d in range(1, size)]
    for device in greeted:
        pl.semaphore_signal(barrier, inc=1, device_id=device, device_id_type=MESH)

    rows_of = lax.broadcasted_iota(jnp.int32, (128, 128), 0)
    lanes_of = lax.broadcasted_iota(jnp.int32, (128, 128), 1)
    bf16, f32 = jnp.bfloat16, jnp.float32
    mine = pl.multiple_of(core * 256, 256)
    for i in range(2):
        scale = jnp.transpose(jnp.broadcast_to(scale_ref[:, 128 * i : 128 * i + 128], (128, 128)))
        at = pl.ds(pl.multiple_of(mine + 128 * i, 128), 128)
        for p in range(4):
            codes = codes_ref[128 * i : 128 * i + 128, 128 * p : 128 * p + 128]
            frames[p, at, :] = (codes.astype(f32) * scale).astype(bf16)

    pl.semaphore_wait(barrier, len(greeted) - 1 + 2 * (1 - core))
    own = frames.at[:, pl.ds(mine, 256), :]
    swap = remote(own, own, frame_send.at[0], frame_recv.at[0], place.partner)
    swap.start()
    first, halo = frames.at[:, pl.ds(0, LAG), :], frames.at[:, pl.ds(512, LAG), :]
    heads = [
        remote(first, halo, frame_send.at[1 + c], frame_recv.at[1], (place.traj, before * 2 + c)) for c in range(2)
    ]

    @pl.when(core == 0)
    def _():
        for c in heads:
            c.start()

    start = place.chip * 512
    valid = valid_ref[0]

    def prepare(block):
        at = pl.ds(pl.multiple_of(block * 128, 128), 128)
        t = rows_of + (start + block * 128)
        weight = jnp.where(t + LAG < valid, 1.0, 0.0) + jnp.where((t >= LAG) & (t < valid), 1.0, 0.0)
        for p in range(4):
            x = frames[p, at, :].astype(f32)
            turned[p, block] = jnp.transpose(x).astype(bf16)
            weighted[p, at, :] = (x * weight).astype(bf16)

    def block_of(k):
        (a0, b0), (a1, b1) = BLOCKS[k]
        return a0 + core * (a1 - a0), b0 + core * (b1 - b0)

    def product(a, right):
        return sum(
            dot(turned[a, i], right[128 * i : 128 * i + 128], ROWS, None) for i in range(4)
        )

    prepare(2 * core)
    prepare(2 * core + 1)
    swap.wait_recv()
    prepare(2 - 2 * core)
    prepare(3 - 2 * core)

    row8 = lax.broadcasted_iota(jnp.int32, (8, 128), 0)
    for k in range(3):
        a, b = block_of(k)
        acc[0, 128 * k : 128 * k + 128] = product(a, weighted[b])
    on = [product(block_of(k)[0], weighted[block_of(k)[0]]) for k in (3, 4)]
    acc[0, 384:512] = jnp.where(rows_of <= lanes_of, on[0], on[1])
    diagonal = jnp.sum(jnp.where(rows_of == lanes_of, on[1], 0.0), axis=0, keepdims=True)
    ones = jnp.ones((16, 512), bf16)
    totals = jnp.concatenate(
        [jnp.zeros((4, 128), f32)] + [dot(ones, weighted[p], ROWS, None)[:1] for p in range(4)], axis=0
    )
    count = jnp.clip(valid - LAG - start, 0, 512).astype(f32) * 2.0
    extra = jnp.where(core == 0, totals, jnp.full((8, 128), count))
    acc[0, 512:520] = jnp.where(row8 == 0, diagonal, extra)
    acc[0, 520:576] = jnp.zeros((56, 128), f32)
    instant.start()

    remote(first, halo, frame_send.at[1], frame_recv.at[1], (place.traj, after * 2)).wait_recv()
    for block in range(4):
        t = rows_of + (start + block * 128)
        for p in range(4):
            x = frames[p, 128 * block + LAG : 128 * block + LAG + 128, :].astype(f32)
            trailing[p, 128 * block : 128 * block + 128, :] = jnp.where(t + LAG < valid, x, 0.0).astype(bf16)
    for k in range(3):
        a, b = block_of(k)
        acc[1, 128 * k : 128 * k + 128] = product(b, trailing[a]) + jnp.transpose(product(a, trailing[b]))
    on = [product(block_of(k)[0], trailing[block_of(k)[0]]) for k in (3, 4)]
    on = [x + jnp.transpose(x) for x in on]
    acc[1, 384:512] = jnp.where(rows_of >= lanes_of, on[0], on[1])
    diagonal = jnp.sum(jnp.where(rows_of == lanes_of, on[1], 0.0), axis=0, keepdims=True)
    acc[1, 512:520] = jnp.where(row8 == 0, diagonal, 0.0)
    acc[1, 520:576] = jnp.zeros((56, 128), f32)

    instant.advance(0)
    lagged.start()
    for n in range(1, instant.n_steps):
        instant.advance(n)
        lagged.advance(n - 1)
    lagged.advance(lagged.n_steps - 1)
    instant.arrive()
    lagged.arrive()
    instant.close()
    lagged.close()
    swap.wait_send()

    @pl.when(core == 0)
    def _():
        for c in heads:
            c.wait_send()


def sum_scratch():
    bufs, sums, sems = [], [], 0
    for part in PARTS:
        rows = part[1]
        for kind, axis in all_steps(part):
            size = SIZE[axis]
            sems += size
            if kind == "rs":
                rows //= size
                bufs.append(pltpu.VMEM((size - 1, rows, 128), jnp.float32))
                sums.append(pltpu.VMEM((rows, 128), jnp.float32))
            elif kind == "ar":
                bufs.append(pltpu.VMEM((size, rows, 128), jnp.float32))
                sums.append(pltpu.VMEM((rows, 128), jnp.float32))
    return [
        *bufs,
        *sums,
        pltpu.SemaphoreType.DMA((sems,)),
        pltpu.SemaphoreType.DMA((sems,)),
        pltpu.SemaphoreType.DMA((len(PARTS),)),
        pltpu.SemaphoreType.DMA((len(PARTS),)),
    ]


def moments(codes, row_scale, valid):
    vmem = pl.BlockSpec(memory_space=pltpu.VMEM)
    out = jax.ShapeDtypeStruct((2, HALF, 128), jnp.float32)
    return pl.pallas_call(
        moments_kernel,
        out_shape=(out, out),
        in_specs=[vmem, vmem, pl.BlockSpec(memory_space=pltpu.SMEM)],
        out_specs=(vmem, vmem),
        scratch_shapes=[
            pltpu.VMEM((4, 512 + LAG, 128), jnp.bfloat16),
            pltpu.VMEM((4, 4, 128, 128), jnp.bfloat16),
            pltpu.VMEM((4, 512, 128), jnp.bfloat16),
            pltpu.VMEM((4, 512, 128), jnp.bfloat16),
            pltpu.VMEM((2, HALF, 128), jnp.float32),
            pltpu.SemaphoreType.DMA((3,)),
            pltpu.SemaphoreType.DMA((2,)),
            *sum_scratch(),
            *sum_scratch(),
        ],
        compiler_params=pltpu.CompilerParams(
            collective_id=0, has_side_effects=True, vmem_limit_bytes=40 * 2**20
        ),
        name="moments",
    )(codes, row_scale, valid)


HIGHEST = lax.Precision.HIGHEST
ROWS = (((1,), (0,)), ((), ()))
LANES = (((1,), (1,)), ((), ()))
SUBLANES = (((0,), (0,)), ((), ()))


def dot(left, right, dims, precision=HIGHEST):
    return lax.dot_general(left, right, dims, precision=precision, preferred_element_type=jnp.float32)


def one_row(x, k):
    return jnp.broadcast_to(x[k : k + 1, :], (8, 128))


def one_lane(x, k):
    return jnp.broadcast_to(x[:, k : k + 1], (8, 128))


def inverse_factor(block):
    rows = list(block)
    n, size = len(rows), 8
    sub = lax.broadcasted_iota(jnp.int32, (8, 128), 0)
    lane = lax.broadcasted_iota(jnp.int32, (8, 128), 1)
    pivots = [None] * n
    for group in range(0, n, size):
        end = group + size
        coming = [one_lane(rows[group], 8 * group + k) for k in range(8)]
        for r in range(group, end):
            first = 8 * r
            last = r == end - 1
            columns = [[coming[k]] + [one_lane(rows[q], first + k) for q in range(r + 1, end)] for k in range(8)]
            if not last:
                coming = [one_lane(rows[r + 1], first + 8 + k) for k in range(8)]
            inside = (lane >= first) & (lane < first + 8)
            panel = jnp.where(inside, jnp.where(lane - first == sub, 1.0, 0.0), rows[r])
            for q in range(r + 1, end):
                rows[q] = jnp.where(inside, 0.0, rows[q])
            for k in range(8):
                entry = one_row(columns[k][0], k)
                rough = pl.reciprocal(entry, approx=True)
                mend = 2.0 - entry * rough
                pivot = rough * mend
                pivots[r] = pivot if k == 0 else jnp.where(sub == k, pivot, pivots[r])
                below = jnp.where(sub > k, columns[k][0], 0.0)
                factor = [below * pivot] + [column * pivot for column in columns[k][1:]]
                for m in range(k + 1, 8):
                    entry = one_row(columns[k][0], m)
                    columns[m] = [columns[m][0] - ((below * entry) * rough) * mend] + [
                        x - f * entry for x, f in zip(columns[m][1:], factor[1:])
                    ]
                if not last:
                    coming = [coming[m] - factor[1] * one_row(columns[k][1], m) for m in range(8)]
                row = one_row(panel, k)
                panel = panel - factor[0] * row
                for q in range(r + 1, end):
                    rows[q] = rows[q] - factor[q - r] * row
            rows[r] = panel
        if end < n:
            done = jnp.concatenate(rows[group:end], axis=0)
            factors = jnp.concatenate([rows[r] * pivots[r] for r in range(group, end)], axis=0)
            down = lax.broadcasted_iota(jnp.int32, done.shape, 0) + 8 * group
            along = lax.broadcasted_iota(jnp.int32, done.shape, 1)
            done = jnp.where((along > down) & (along < 8 * end), 0.0, done)
            change = dot(factors, done, SUBLANES)
            inside = (lane >= 8 * group) & (lane < 8 * end)
            for q in range(end, n):
                rows[q] = jnp.where(inside, 0.0, rows[q]) - change[8 * q : 8 * q + 8]
    return [jnp.where(lane <= sub + 8 * q, rows[q], 0.0) * jnp.sqrt(pivots[q]) for q in range(n)]


def split3(x):
    high = x.astype(jnp.bfloat16)
    rest = x - high.astype(jnp.float32)
    middle = rest.astype(jnp.bfloat16)
    return high, middle, (rest - middle.astype(jnp.float32)).astype(jnp.bfloat16)


def at_block(i):
    return slice(128 * i, 128 * i + 128)


def finish_kernel(inst_ref, lag_ref, x_ref, white_ref, koop_ref, A, S, lhs):
    f32 = jnp.float32
    ri = lax.broadcasted_iota(jnp.int32, (128, 128), 0)
    ci = lax.broadcasted_iota(jnp.int32, (128, 128), 1)
    inv = 1.0 / inst_ref[1, 516:517, :]
    avg = [inst_ref[0, 516 + j : 517 + j, :] * inv for j in range(4)]
    avg_down = [jnp.transpose(jnp.broadcast_to(a, (128, 128))) for a in avg]

    def on_diagonal(ref, i):
        stored = ref[i // 2, 384:512] * inv
        turned = jnp.transpose(stored)
        if i % 2 == 0:
            return stored, turned, stored
        return turned, stored, ref[i // 2, 512:513] * inv

    for k, pair in enumerate(BLOCKS[:3]):
        for c, (i, j) in enumerate(pair):
            A[at_block(i), at_block(j)] = inst_ref[c, at_block(k)] * inv - avg_down[i] * avg[j]
            S[at_block(j), at_block(i)] = lag_ref[c, at_block(k)] * inv - avg_down[j] * avg[i]
    for i in range(4):
        outer = avg_down[i] * avg[i]
        own, turned, diagonal = on_diagonal(inst_ref, i)
        whole = jnp.where(ri < ci, own, jnp.where(ri > ci, turned, diagonal))
        A[at_block(i), at_block(i)] = whole - outer
        own, _, diagonal = on_diagonal(lag_ref, i)
        S[at_block(i), at_block(i)] = jnp.where(
            ri > ci, own - outer, jnp.where(ri == ci, 0.5 * (diagonal - outer), 0.0)
        )
    for k in range(4):
        V = [A[128*k+8*q:128*k+8*q+8, at_block(k)] for q in range(16)]
        W = jnp.concatenate(inverse_factor(V), axis=0)
        if k == 0:
            R = dot(W, A[at_block(0), 128:], ROWS)
            A[at_block(0), 128:] = R
        else:
            R = dot(W, A[at_block(k), :], ROWS)
            A[at_block(k), :] = R
        A[at_block(k), at_block(k)] = W
        if k < 3:
            Rr = A[at_block(k), 128*(k+1):]
            upd = dot(Rr, A[at_block(k), :], SUBLANES)
            A[128*(k+1):, at_block(k)] = -upd[:, at_block(k)]
            if k > 0:
                A[128*(k+1):, 0:128*k] = A[128*(k+1):, 0:128*k] - upd[:, 0:128*k]
            A[128*(k+1):, 128*(k+1):] = A[128*(k+1):, 128*(k+1):] - upd[:, 128*(k+1):]
    z = jnp.zeros((128,128), f32)
    A[at_block(0), at_block(1)] = z
    A[at_block(2), at_block(3)] = z
    S[at_block(0), at_block(1)] = z
    S[at_block(2), at_block(3)] = z
    a = [A[0:256, 0:256], A[256:512, 0:256], A[256:512, 256:512]]
    s = [S[0:256, 0:256], S[256:512, 0:256], S[256:512, 256:512]]
    x = x_ref[...]
    lhs[0:256, :] = x
    am = [jnp.concatenate([t[m] for t in [split3(q) for q in avg]], axis=1) for m in range(3)]
    lhs[256:272, :] = jnp.concatenate(am + [jnp.zeros((13, 512), jnp.bfloat16)], axis=0)
    y = [None, None]
    for t in split3(a[0]):
        v = dot(lhs[:, 0:256], t, LANES, None)
        y[0] = v if y[0] is None else y[0] + v
    for t, u in zip(split3(a[1]), split3(a[2])):
        v = dot(lhs[:, 0:256], t, LANES, None) + dot(lhs[:, 256:512], u, LANES, None)
        y[1] = v if y[1] is None else y[1] + v
    for h in range(2):
        m = y[h][256:257] + y[h][257:258] + y[h][258:259]
        white_ref[:, 256*h:256*h+256] = (y[h][0:256] - m).astype(jnp.bfloat16)
    nn = ROWS; nt = LANES
    t00 = dot(a[0], s[0], nn)
    t10 = dot(a[1], s[0], nn) + dot(a[2], s[1], nn)
    t11 = dot(a[2], s[2], nn)
    k00 = dot(t00, a[0], nt)
    k01 = dot(t00, a[1], nt)
    k10 = dot(t10, a[0], nt)
    k11 = dot(t10, a[1], nt) + dot(t11, a[2], nt)
    koop_ref[0:256, 0:256] = k00 + jnp.transpose(k00)
    koop_ref[256:512, 256:512] = k11 + jnp.transpose(k11)
    k10 = k10 + jnp.transpose(k01)
    koop_ref[256:512, 0:256] = k10
    koop_ref[0:256, 256:512] = jnp.transpose(k10)


def finish(instant, lagged, x):
    width = x.shape[1]
    return pl.pallas_call(
        finish_kernel,
        out_shape=(
            jax.ShapeDtypeStruct(x.shape, jnp.bfloat16),
            jax.ShapeDtypeStruct((width, width), jnp.float32),
        ),
        in_specs=[pl.BlockSpec(memory_space=pltpu.VMEM)] * 3,
        out_specs=(pl.BlockSpec(memory_space=pltpu.VMEM),) * 2,
        scratch_shapes=[
            pltpu.VMEM((width, width), jnp.float32),
            pltpu.VMEM((width, width), jnp.float32),
            pltpu.VMEM((x.shape[0] + 16, width), jnp.bfloat16),
        ],
        compiler_params=pltpu.CompilerParams(vmem_limit_bytes=40 * 2**20),
        name="finish",
    )(instant, lagged, x)


def on_device(codes, row_scale, valid):
    instant, lagged = moments(codes[0], row_scale, valid)
    dequant = (codes[0].astype(jnp.float32) * row_scale[0][:, None]).astype(jnp.bfloat16)
    projected, koopman = finish(instant, lagged, dequant)
    return (projected[None], koopman)


def solution(mesh):
    return jax.shard_map(
        on_device,
        mesh=mesh,
        in_specs=(P("traj", "blk", None), P("traj", "blk"), P("traj")),
        out_specs=(P("traj", "blk", None), P()),
        check_vma=False,
    )
```

```python
import jax
import jax.numpy as jnp
from jax import lax
from jax.experimental import pallas as pl
from jax.experimental.pallas import tpu as pltpu
from jax.sharding import PartitionSpec as P

MESH = pl.DeviceIdType.MESH
LAG = 64
HALF = 544
PARTS = (
    (0, 96, "x", (("ar", "y"), ("ar", "z"))),
    (96, 192, "y", (("ar", "z"), ("ar", "x"))),
    (288, 256, "z", (("ar", "x"), ("ar", "y"))),
)
SIZE = {"x": 4, "y": 8, "z": 8}
FAR = {4: (2, 1, 3), 8: (4, 3, 5, 2, 6, 1, 7)}
BLOCKS = (((0, 1), (1, 2)), ((0, 2), (1, 3)), ((0, 3), (2, 3)), ((0, 0), (2, 2)), ((1, 1), (3, 3)))


def all_steps(part):
    return (("rs", part[2]),) + part[3] + (("ag", part[2]),)


class Record:
    pass


class Place:
    def __init__(self):
        self.traj, self.blk = lax.axis_index("traj"), lax.axis_index("blk")
        self.core = lax.rem(self.blk, 2)
        self.chip = lax.div(self.blk, 2)
        self.at = {"x": lax.rem(self.chip, 4), "y": self.traj, "z": lax.div(self.blk, 8)}
        self.partner = (self.traj, self.blk + 1 - 2 * self.core)

    def device(self, axis, index):
        if axis == "x":
            return (self.traj, self.at["z"] * 8 + index * 2 + self.core)
        if axis == "y":
            return (index, self.blk)
        return (self.traj, index * 8 + self.at["x"] * 2 + self.core)


def remote(src, dst, send, recv, to):
    return pltpu.make_async_remote_copy(
        src_ref=src, dst_ref=dst, send_sem=send, recv_sem=recv, device_id=to, device_id_type=MESH
    )


class Stream:
    def __init__(self, place, acc, out, bufs, sums, send, recv, core_send, core_recv):
        self.place, self.acc, self.out = place, acc, out
        self.send, self.recv = send, recv
        self.core_send, self.core_recv = core_send, core_recv
        self.waiting, self.last, self.runs = [], [], []
        sem_at = buf_at = 0
        for part in PARTS:
            run = Record()
            run.base, run.rows = part[0], part[1]
            run.steps = []
            for kind, axis in all_steps(part):
                step = Record()
                step.kind, step.axis, step.sem = kind, axis, sem_at
                sem_at += SIZE[axis]
                if kind != "ag":
                    step.buf, step.sum = bufs[buf_at], sums[buf_at]
                    buf_at += 1
                run.steps.append(step)
            self.runs.append(run)
        self.n_steps = max(len(run.steps) for run in self.runs)

    def start(self):
        for run in self.runs:
            run.now, run.now_at, run.now_rows = self.acc, run.base, run.rows
            run.home = run.base
        for run in self.runs[::-1]:
            self.begin(run, 0)

    def advance(self, n):
        for k, run in enumerate(self.runs):
            if n < len(run.steps):
                self.finish(run, n)
                if n + 1 < len(run.steps):
                    self.begin(run, n + 1)
                else:
                    rows = self.out.at[self.place.core, pl.ds(run.base, run.rows)]
                    c = remote(rows, rows, self.core_send.at[k], self.core_recv.at[k], self.place.partner)
                    c.start()
                    self.last.append(c)

    def arrive(self):
        for c in self.last:
            c.wait_recv()

    def close(self):
        for c in self.waiting + self.last:
            c.wait_send()

    def begin(self, run, n):
        step = run.steps[n]
        axis, size = step.axis, SIZE[step.axis]
        me = self.place.at[axis]
        step.copies = {}
        for d in FAR[size]:
            to = lax.rem(me + d, size)
            if step.kind == "rs":
                rows = run.now_rows // size
                src = run.now.at[pl.ds(pl.multiple_of(run.now_at + to * rows, 8), rows)]
                dst, slot = step.buf.at[d - 1], d
            elif step.kind == "ar":
                src = run.now.at[pl.ds(run.now_at, run.now_rows)]
                dst, slot = step.buf.at[me], me
            else:
                src = dst = self.out.at[self.place.core, pl.ds(run.home, run.now_rows)]
                slot = d
            step.copies[d] = remote(
                src, dst, self.send.at[step.sem + d], self.recv.at[step.sem + slot], self.place.device(axis, to)
            )
            step.copies[d].start()
        if step.kind == "ar":
            step.buf[me] = run.now[pl.ds(run.now_at, run.now_rows)]
        self.waiting.extend(step.copies.values())

    def finish(self, run, n):
        step = run.steps[n]
        axis, size = step.axis, SIZE[step.axis]
        me = self.place.at[axis]
        near = FAR[size][::-1]
        if step.kind == "rs":
            rows = run.now_rows // size
            total = run.now[pl.ds(pl.multiple_of(run.now_at + me * rows, 8), rows)]
            for d in near:
                step.copies[d].wait_recv()
                total = total + step.buf[d - 1]
            step.sum[...] = total
            run.now, run.now_at, run.now_rows = step.sum, 0, rows
            run.home = run.home + me * rows
        elif step.kind == "ar":
            for d in near:
                come = lax.rem(me + d, size)
                remote(
                    run.now.at[pl.ds(run.now_at, run.now_rows)],
                    step.buf.at[come],
                    self.send.at[step.sem + d],
                    self.recv.at[step.sem + come],
                    self.place.device(axis, come),
                ).wait_recv()
            total = step.buf[0]
            for j in range(1, size):
                total = total + step.buf[j]
            step.sum[...] = total
            run.now, run.now_at = step.sum, 0
        else:
            for d in near:
                step.copies[d].wait_recv()
            run.home = run.home - me * run.now_rows
            run.now_rows = run.now_rows * size
        if n + 1 < len(run.steps) and run.steps[n + 1].kind == "ag":
            run.home = pl.multiple_of(run.home, 8)
            if step.kind != "ag":
                self.out[self.place.core, pl.ds(run.home, run.now_rows)] = run.now[...]


def moments_kernel(
    codes_ref, scale_ref, valid_ref, A, S, avg_ref, x_ref, frames, turned, weighted, trailing, acc, summed, *rest
):
    (frame_send, frame_recv), rest = rest[:2], rest[2:]
    n = sum(kind != "ag" for part in PARTS for kind, _ in all_steps(part))
    place = Place()
    core = place.core
    streams = []
    for s, out in enumerate((summed.at[0], summed.at[1])):
        bufs, sums, sems = rest[:n], rest[n : 2 * n], rest[2 * n : 2 * n + 4]
        rest = rest[2 * n + 4 :]
        streams.append(Stream(place, acc.at[s], out, bufs, sums, *sems))
    instant, lagged = streams

    chips = 32
    before = lax.rem(place.chip + chips - 1, chips)
    after = lax.rem(place.chip + 1, chips)
    barrier = pltpu.get_barrier_semaphore()
    greeted = [place.partner, (place.traj, after * 2)]
    for axis, size in SIZE.items():
        greeted += [place.device(axis, lax.rem(place.at[axis] + d, size)) for d in range(1, size)]
    for device in greeted:
        pl.semaphore_signal(barrier, inc=1, device_id=device, device_id_type=MESH)

    rows_of = lax.broadcasted_iota(jnp.int32, (128, 128), 0)
    lanes_of = lax.broadcasted_iota(jnp.int32, (128, 128), 1)
    bf16, f32 = jnp.bfloat16, jnp.float32
    mine = pl.multiple_of(core * 256, 256)
    for i in range(2):
        scale = jnp.transpose(jnp.broadcast_to(scale_ref[:, 128 * i : 128 * i + 128], (128, 128)))
        at = pl.ds(pl.multiple_of(mine + 128 * i, 128), 128)
        for p in range(4):
            codes = codes_ref[128 * i : 128 * i + 128, 128 * p : 128 * p + 128]
            x = (codes.astype(f32) * scale).astype(bf16)
            frames[p, at, :] = x
            x_ref[128 * i : 128 * i + 128, 128 * p : 128 * p + 128] = x

    pl.semaphore_wait(barrier, len(greeted) - 1 + 2 * (1 - core))
    own = frames.at[:, pl.ds(mine, 256), :]
    swap = remote(own, own, frame_send.at[0], frame_recv.at[0], place.partner)
    swap.start()
    first, halo = frames.at[:, pl.ds(0, LAG), :], frames.at[:, pl.ds(512, LAG), :]
    heads = [
        remote(first, halo, frame_send.at[1 + c], frame_recv.at[1], (place.traj, before * 2 + c)) for c in range(2)
    ]

    @pl.when(core == 0)
    def _():
        for c in heads:
            c.start()

    start = place.chip * 512
    valid = valid_ref[0]

    def prepare(block):
        at = pl.ds(pl.multiple_of(block * 128, 128), 128)
        t = rows_of + (start + block * 128)
        weight = jnp.where(t + LAG < valid, 1.0, 0.0) + jnp.where((t >= LAG) & (t < valid), 1.0, 0.0)
        for p in range(4):
            x = frames[p, at, :].astype(f32)
            turned[p, block] = jnp.transpose(x).astype(bf16)
            weighted[p, at, :] = (x * weight).astype(bf16)

    def block_of(k):
        (a0, b0), (a1, b1) = BLOCKS[k]
        return a0 + core * (a1 - a0), b0 + core * (b1 - b0)

    def product(a, right):
        return sum(
            dot(turned[a, i], right[128 * i : 128 * i + 128], ROWS, None) for i in range(4)
        )

    prepare(2 * core)
    prepare(2 * core + 1)
    swap.wait_recv()
    prepare(2 - 2 * core)
    prepare(3 - 2 * core)

    row8 = lax.broadcasted_iota(jnp.int32, (8, 128), 0)
    for k in range(3):
        a, b = block_of(k)
        acc[0, 128 * k : 128 * k + 128] = product(a, weighted[b])
    on = [product(block_of(k)[0], weighted[block_of(k)[0]]) for k in (3, 4)]
    acc[0, 384:512] = jnp.where(rows_of <= lanes_of, on[0], on[1])
    diagonal = jnp.sum(jnp.where(rows_of == lanes_of, on[1], 0.0), axis=0, keepdims=True)
    ones = jnp.ones((16, 512), bf16)
    totals = jnp.concatenate(
        [jnp.zeros((4, 128), f32)] + [dot(ones, weighted[p], ROWS, None)[:1] for p in range(4)], axis=0
    )
    count = jnp.clip(valid - LAG - start, 0, 512).astype(f32) * 2.0
    extra = jnp.where(core == 0, totals, jnp.full((8, 128), count))
    acc[0, 512:520] = jnp.where(row8 == 0, diagonal, extra)
    acc[0, 520:HALF] = jnp.zeros((HALF - 520, 128), f32)
    instant.start()

    remote(first, halo, frame_send.at[1], frame_recv.at[1], (place.traj, after * 2)).wait_recv()
    for block in range(4):
        t = rows_of + (start + block * 128)
        for p in range(4):
            x = frames[p, 128 * block + LAG : 128 * block + LAG + 128, :].astype(f32)
            trailing[p, 128 * block : 128 * block + 128, :] = jnp.where(t + LAG < valid, x, 0.0).astype(bf16)
    for k in range(3):
        a, b = block_of(k)
        acc[1, 128 * k : 128 * k + 128] = product(b, trailing[a]) + jnp.transpose(product(a, trailing[b]))
    on = [product(block_of(k)[0], trailing[block_of(k)[0]]) for k in (3, 4)]
    on = [x + jnp.transpose(x) for x in on]
    acc[1, 384:512] = jnp.where(rows_of >= lanes_of, on[0], on[1])
    diagonal = jnp.sum(jnp.where(rows_of == lanes_of, on[1], 0.0), axis=0, keepdims=True)
    acc[1, 512:520] = jnp.where(row8 == 0, diagonal, 0.0)
    acc[1, 520:HALF] = jnp.zeros((HALF - 520, 128), f32)

    instant.advance(0)
    instant.advance(1)
    lagged.start()
    instant.advance(2)
    instant.advance(3)
    instant.arrive()
    lagged.advance(0)
    means = Means(summed.at[0], summed.at[1])
    means.instant_cov(A)
    D = A[at_block(0), at_block(0)]
    for k in range(4):
        D = eliminate(A, k, D)
        if k < 3:
            lagged.advance(k + 1)
    A[at_block(0), at_block(1)] = jnp.zeros((128, 128), f32)
    A[at_block(2), at_block(3)] = jnp.zeros((128, 128), f32)
    avg_ref[...] = jnp.concatenate(means.avg + means.avg, axis=0)
    lagged.arrive()
    means.lagged_cov(S)
    instant.close()
    lagged.close()
    swap.wait_send()

    @pl.when(core == 0)
    def _():
        for c in heads:
            c.wait_send()


def sum_scratch():
    bufs, sums, sems = [], [], 0
    for part in PARTS:
        rows = part[1]
        for kind, axis in all_steps(part):
            size = SIZE[axis]
            sems += size
            if kind == "rs":
                rows //= size
                bufs.append(pltpu.VMEM((size - 1, rows, 128), jnp.float32))
                sums.append(pltpu.VMEM((rows, 128), jnp.float32))
            elif kind == "ar":
                bufs.append(pltpu.VMEM((size, rows, 128), jnp.float32))
                sums.append(pltpu.VMEM((rows, 128), jnp.float32))
    return [
        *bufs,
        *sums,
        pltpu.SemaphoreType.DMA((sems,)),
        pltpu.SemaphoreType.DMA((sems,)),
        pltpu.SemaphoreType.DMA((len(PARTS),)),
        pltpu.SemaphoreType.DMA((len(PARTS),)),
    ]


def moments(codes, row_scale, valid):
    vmem = pl.BlockSpec(memory_space=pltpu.VMEM)
    square = jax.ShapeDtypeStruct((codes.shape[1], codes.shape[1]), jnp.float32)
    average = jax.ShapeDtypeStruct((8, 128), jnp.float32)
    return pl.pallas_call(
        moments_kernel,
        out_shape=(square, square, average, jax.ShapeDtypeStruct(codes.shape, codes.dtype)),
        in_specs=[vmem, vmem, pl.BlockSpec(memory_space=pltpu.SMEM)],
        out_specs=(vmem,) * 4,
        scratch_shapes=[
            pltpu.VMEM((4, 512 + LAG, 128), jnp.bfloat16),
            pltpu.VMEM((4, 4, 128, 128), jnp.bfloat16),
            pltpu.VMEM((4, 512, 128), jnp.bfloat16),
            pltpu.VMEM((4, 512, 128), jnp.bfloat16),
            pltpu.VMEM((2, HALF, 128), jnp.float32),
            pltpu.VMEM((2, 2, HALF, 128), jnp.float32),
            pltpu.SemaphoreType.DMA((3,)),
            pltpu.SemaphoreType.DMA((2,)),
            *sum_scratch(),
            *sum_scratch(),
        ],
        compiler_params=pltpu.CompilerParams(
            collective_id=0, has_side_effects=True, vmem_limit_bytes=40 * 2**20
        ),
        name="moments",
    )(codes, row_scale, valid)


HIGHEST = lax.Precision.HIGHEST
ROWS = (((1,), (0,)), ((), ()))
LANES = (((1,), (1,)), ((), ()))
SUBLANES = (((0,), (0,)), ((), ()))


def dot(left, right, dims, precision=HIGHEST):
    return lax.dot_general(left, right, dims, precision=precision, preferred_element_type=jnp.float32)


def one_row(x, k):
    return jnp.broadcast_to(x[k : k + 1, :], (8, 128))


def one_lane(x, k):
    return jnp.broadcast_to(x[:, k : k + 1], (8, 128))


def inverse_factor(block):
    rows = list(block)
    n, size = len(rows), 8
    sub = lax.broadcasted_iota(jnp.int32, (8, 128), 0)
    lane = lax.broadcasted_iota(jnp.int32, (8, 128), 1)
    even = (sub % 2) == 0
    for group in range(0, n, size):
        end = group + size
        coming = [one_lane(rows[group], 8 * group + k) for k in range(8)]
        pivots = []
        for r in range(group, end):
            first = 8 * r
            last = r == end - 1
            columns = [[coming[k]] + [one_lane(rows[q], first + k) for q in range(r + 1, end)] for k in range(8)]
            if not last:
                coming = [one_lane(rows[r + 1], first + 8 + k) for k in range(8)]
            inside = (lane >= first) & (lane < first + 8)
            panel = jnp.where(inside, jnp.where(lane - first == sub, 1.0, 0.0), rows[r])
            for q in range(r + 1, end):
                rows[q] = jnp.where(inside, 0.0, rows[q])
            for k in range(0, 8, 2):
                left, right = columns[k], columns[k + 1]
                a, b, d = one_row(left[0], k), one_row(left[0], k + 1), one_row(right[0], k + 1)
                det = a * d - b * b
                rough = pl.reciprocal(det, approx=True)
                mend = 2.0 - det * rough
                inv = rough * mend
                a_inv, b_inv, d_inv = a * inv, b * inv, d * inv
                low, high = jnp.where(sub > k + 1, left[0], 0.0), jnp.where(sub > k + 1, right[0], 0.0)
                g, h = low * d - high * b, high * a - low * b
                f0 = [g * inv] + [x * d_inv - y * b_inv for x, y in zip(left[1:], right[1:])]
                f1 = [h * inv] + [y * a_inv - x * b_inv for x, y in zip(left[1:], right[1:])]
                for m in range(k + 2, 8):
                    e0, e1 = one_row(left[0], m), one_row(right[0], m)
                    columns[m] = [columns[m][0] - ((g * e0 + h * e1) * rough) * mend] + [
                        x - (u * e0 + v * e1) for x, u, v in zip(columns[m][1:], f0[1:], f1[1:])
                    ]
                if not last:
                    coming = [
                        coming[m] - (f0[1] * one_row(left[1], m) + f1[1] * one_row(right[1], m)) for m in range(8)
                    ]
                row0, row1 = one_row(panel, k), one_row(panel, k + 1)
                panel = panel - (f0[0] * row0 + f1[0] * row1)
                for q in range(r + 1, end):
                    rows[q] = rows[q] - (f0[q - r] * row0 + f1[q - r] * row1)
                if k == 0:
                    pivot = (a, b, det)
                else:
                    pivot = tuple(jnp.where(sub >= k, x, y) for x, y in zip((a, b, det), pivot))
            rows[r] = panel
            pivots.append(pivot)
        for r in range(group, end):
            a, b, det = pivots[r - group]
            above = pltpu.roll(rows[r], 1, 0)
            rows[r] = jnp.where(even, rows[r], rows[r] * a - above * b) * lax.rsqrt(jnp.where(even, a, a * det))
        if end < n:
            done = jnp.concatenate(rows[group:end], axis=0)
            down = lax.broadcasted_iota(jnp.int32, done.shape, 0) + 8 * group
            along = lax.broadcasted_iota(jnp.int32, done.shape, 1)
            change = dot(done, jnp.where((along > down) & (along < 8 * end), 0.0, done), SUBLANES)
            inside = (lane >= 8 * group) & (lane < 8 * end)
            for q in range(end, n):
                rows[q] = jnp.where(inside, 0.0, rows[q]) - change[8 * q : 8 * q + 8]
    return [jnp.where(lane <= sub + 8 * q, rows[q], 0.0) for q in range(n)]


def split3(x):
    high = x.astype(jnp.bfloat16)
    rest = x - high.astype(jnp.float32)
    middle = rest.astype(jnp.bfloat16)
    return high, middle, (rest - middle.astype(jnp.float32)).astype(jnp.bfloat16)


def at_block(i):
    return slice(128 * i, 128 * i + 128)


def eliminate(A, k, D):
    W = jnp.concatenate(inverse_factor([D[8 * q : 8 * q + 8, :] for q in range(16)]), axis=0)
    A[at_block(k), at_block(k)] = W
    if k < 3:
        near = dot(W, A[at_block(k), at_block(k + 1)], ROWS)
        D = A[at_block(k + 1), at_block(k + 1)] - dot(near, near, SUBLANES)
        A[at_block(k), at_block(k + 1)] = near
    for lo, hi in ((0, 128 * k), (128 * (k + 2), 512)):
        if lo < hi:
            A[at_block(k), lo:hi] = dot(W, A[at_block(k), lo:hi], ROWS)
    if k < 3:
        below = 128 * (k + 1)
        change = dot(A[at_block(k), below:], A[at_block(k), :], SUBLANES)
        A[below:, at_block(k)] = -change[:, at_block(k)]
        if k > 0:
            A[below:, 0 : 128 * k] = A[below:, 0 : 128 * k] - change[:, 0 : 128 * k]
        if k < 2:
            A[below:, below + 128 :] = A[below:, below + 128 :] - change[:, below + 128 :]
    return D


class Means:
    def __init__(self, inst_ref, lag_ref):
        self.inst, self.lag = inst_ref, lag_ref
        self.inv = 1.0 / inst_ref[1, 516:517, :]
        self.avg = [inst_ref[0, 516 + j : 517 + j, :] * self.inv for j in range(4)]
        self.down = [jnp.transpose(jnp.broadcast_to(a, (128, 128))) for a in self.avg]
        self.ri = lax.broadcasted_iota(jnp.int32, (128, 128), 0)
        self.ci = lax.broadcasted_iota(jnp.int32, (128, 128), 1)

    def on_diagonal(self, ref, i):
        stored = ref[i // 2, 384:512] * self.inv
        turned = jnp.transpose(stored)
        if i % 2 == 0:
            return stored, turned, stored
        return turned, stored, ref[i // 2, 512:513] * self.inv

    def instant_cov(self, A):
        for k, pair in enumerate(BLOCKS[:3]):
            for c, (i, j) in enumerate(pair):
                A[at_block(i), at_block(j)] = self.inst[c, at_block(k)] * self.inv - self.down[i] * self.avg[j]
        for i in range(4):
            own, turned, diagonal = self.on_diagonal(self.inst, i)
            whole = jnp.where(self.ri < self.ci, own, jnp.where(self.ri > self.ci, turned, diagonal))
            A[at_block(i), at_block(i)] = whole - self.down[i] * self.avg[i]

    def lagged_cov(self, S):
        zero = jnp.zeros((128, 128), jnp.float32)
        S[at_block(0), at_block(1)] = zero
        S[at_block(2), at_block(3)] = zero
        for k, pair in enumerate(BLOCKS[:3]):
            for c, (i, j) in enumerate(pair):
                S[at_block(j), at_block(i)] = self.lag[c, at_block(k)] * self.inv - self.down[j] * self.avg[i]
        for i in range(4):
            outer = self.down[i] * self.avg[i]
            own, _, diagonal = self.on_diagonal(self.lag, i)
            S[at_block(i), at_block(i)] = jnp.where(
                self.ri > self.ci, own - outer, jnp.where(self.ri == self.ci, 0.5 * (diagonal - outer), 0.0)
            )


def finish_kernel(A, S, avg_ref, x_ref, white_ref, koop_ref, lhs):
    f32 = jnp.float32
    avg = [avg_ref[j : j + 1, :] for j in range(4)]
    a = [A[0:256, 0:256], A[256:512, 0:256], A[256:512, 256:512]]
    s = [S[0:256, 0:256], S[256:512, 0:256], S[256:512, 256:512]]
    x = x_ref[...]
    lhs[0:256, :] = x
    am = [jnp.concatenate([t[m] for t in [split3(q) for q in avg]], axis=1) for m in range(3)]
    lhs[256:272, :] = jnp.concatenate(am + [jnp.zeros((13, 512), jnp.bfloat16)], axis=0)
    y = [None, None]
    for t in split3(a[0]):
        v = dot(lhs[:, 0:256], t, LANES, None)
        y[0] = v if y[0] is None else y[0] + v
    for t, u in zip(split3(a[1]), split3(a[2])):
        v = dot(lhs[:, 0:256], t, LANES, None) + dot(lhs[:, 256:512], u, LANES, None)
        y[1] = v if y[1] is None else y[1] + v
    for h in range(2):
        m = y[h][256:257] + y[h][257:258] + y[h][258:259]
        white_ref[:, 256*h:256*h+256] = (y[h][0:256] - m).astype(jnp.bfloat16)
    nn = ROWS; nt = LANES
    t00 = dot(a[0], s[0], nn)
    t10 = dot(a[1], s[0], nn) + dot(a[2], s[1], nn)
    t11 = dot(a[2], s[2], nn)
    k00 = dot(t00, a[0], nt)
    k01 = dot(t00, a[1], nt)
    k10 = dot(t10, a[0], nt)
    k11 = dot(t10, a[1], nt) + dot(t11, a[2], nt)
    koop_ref[0:256, 0:256] = k00 + jnp.transpose(k00)
    koop_ref[256:512, 256:512] = k11 + jnp.transpose(k11)
    k10 = k10 + jnp.transpose(k01)
    koop_ref[256:512, 0:256] = k10
    koop_ref[0:256, 256:512] = jnp.transpose(k10)


def finish(whitener, lagged_cov, average, x):
    width = x.shape[1]
    return pl.pallas_call(
        finish_kernel,
        out_shape=(
            jax.ShapeDtypeStruct(x.shape, jnp.bfloat16),
            jax.ShapeDtypeStruct((width, width), jnp.float32),
        ),
        in_specs=[pl.BlockSpec(memory_space=pltpu.VMEM)] * 4,
        out_specs=(pl.BlockSpec(memory_space=pltpu.VMEM),) * 2,
        scratch_shapes=[pltpu.VMEM((x.shape[0] + 16, width), jnp.bfloat16)],
        compiler_params=pltpu.CompilerParams(vmem_limit_bytes=40 * 2**20),
        name="finish",
    )(whitener, lagged_cov, average, x)


def on_device(codes, row_scale, valid):
    projected, koopman = finish(*moments(codes[0], row_scale, valid))
    return (projected[None], koopman)


def solution(mesh):
    return jax.shard_map(
        on_device,
        mesh=mesh,
        in_specs=(P("traj", "blk", None), P("traj", "blk"), P("traj")),
        out_specs=(P("traj", "blk", None), P()),
        check_vma=False,
    )
```

```python
import jax
import jax.numpy as jnp
from jax import lax
from jax.experimental import pallas as pl
from jax.experimental.pallas import tpu as pltpu
from jax.sharding import PartitionSpec as P

MESH = pl.DeviceIdType.MESH
LAG = 64
HALF = 544
PARTS = (
    (0, 96, "x", (("ar", "y"), ("ar", "z"))),
    (96, 192, "y", (("ar", "z"), ("ar", "x"))),
    (288, 256, "z", (("ar", "x"), ("ar", "y"))),
)
SIZE = {"x": 4, "y": 8, "z": 8}
FAR = {4: (2, 1, 3), 8: (4, 3, 5, 2, 6, 1, 7)}
UPPER = (((0, 1), (2, 1)), ((0, 2), (2, 3)), ((0, 3), (3, 1)))
BLOCKS = (((0, 1), (1, 2)), ((0, 2), (1, 3)), ((0, 3), (2, 3)))


def all_steps(part):
    return (("rs", part[2]),) + part[3] + (("ag", part[2]),)


class Record:
    pass


class Place:
    def __init__(self):
        self.traj, self.blk = lax.axis_index("traj"), lax.axis_index("blk")
        self.core = lax.rem(self.blk, 2)
        self.chip = lax.div(self.blk, 2)
        self.at = {"x": lax.rem(self.chip, 4), "y": self.traj, "z": lax.div(self.blk, 8)}
        self.partner = (self.traj, self.blk + 1 - 2 * self.core)

    def device(self, axis, index):
        if axis == "x":
            return (self.traj, self.at["z"] * 8 + index * 2 + self.core)
        if axis == "y":
            return (index, self.blk)
        return (self.traj, index * 8 + self.at["x"] * 2 + self.core)


def remote(src, dst, send, recv, to):
    return pltpu.make_async_remote_copy(
        src_ref=src, dst_ref=dst, send_sem=send, recv_sem=recv, device_id=to, device_id_type=MESH
    )


class Stream:
    def __init__(self, place, acc, out, bufs, sums, send, recv, core_send, core_recv):
        self.place, self.acc, self.out = place, acc, out
        self.send, self.recv = send, recv
        self.core_send, self.core_recv = core_send, core_recv
        self.waiting, self.last, self.runs = [], [], []
        sem_at = buf_at = 0
        for part in PARTS:
            run = Record()
            run.base, run.rows = part[0], part[1]
            run.steps = []
            for kind, axis in all_steps(part):
                step = Record()
                step.kind, step.axis, step.sem = kind, axis, sem_at
                sem_at += SIZE[axis]
                if kind != "ag":
                    step.buf, step.sum = bufs[buf_at], sums[buf_at]
                    buf_at += 1
                run.steps.append(step)
            self.runs.append(run)
        self.n_steps = max(len(run.steps) for run in self.runs)

    def start(self):
        for run in self.runs:
            run.now, run.now_at, run.now_rows = self.acc, run.base, run.rows
            run.home = run.base
        for run in self.runs[::-1]:
            self.begin(run, 0)

    def advance(self, n):
        for k, run in enumerate(self.runs):
            if n < len(run.steps):
                self.finish(run, n)
                if n + 1 < len(run.steps):
                    self.begin(run, n + 1)
                else:
                    rows = self.out.at[self.place.core, pl.ds(run.base, run.rows)]
                    c = remote(rows, rows, self.core_send.at[k], self.core_recv.at[k], self.place.partner)
                    c.start()
                    self.last.append(c)

    def arrive(self):
        for c in self.last:
            c.wait_recv()

    def close(self):
        for c in self.waiting + self.last:
            c.wait_send()

    def begin(self, run, n):
        step = run.steps[n]
        axis, size = step.axis, SIZE[step.axis]
        me = self.place.at[axis]
        step.copies = {}
        for d in FAR[size]:
            to = lax.rem(me + d, size)
            if step.kind == "rs":
                rows = run.now_rows // size
                src = run.now.at[pl.ds(pl.multiple_of(run.now_at + to * rows, 8), rows)]
                dst, slot = step.buf.at[d - 1], d
            elif step.kind == "ar":
                src = run.now.at[pl.ds(run.now_at, run.now_rows)]
                dst, slot = step.buf.at[me], me
            else:
                src = dst = self.out.at[self.place.core, pl.ds(run.home, run.now_rows)]
                slot = d
            step.copies[d] = remote(
                src, dst, self.send.at[step.sem + d], self.recv.at[step.sem + slot], self.place.device(axis, to)
            )
            step.copies[d].start()
        if step.kind == "ar":
            step.buf[me] = run.now[pl.ds(run.now_at, run.now_rows)]
        self.waiting.extend(step.copies.values())

    def finish(self, run, n):
        step = run.steps[n]
        axis, size = step.axis, SIZE[step.axis]
        me = self.place.at[axis]
        near = FAR[size][::-1]
        if step.kind == "rs":
            rows = run.now_rows // size
            total = run.now[pl.ds(pl.multiple_of(run.now_at + me * rows, 8), rows)]
            for d in near:
                step.copies[d].wait_recv()
                total = total + step.buf[d - 1]
            step.sum[...] = total
            run.now, run.now_at, run.now_rows = step.sum, 0, rows
            run.home = run.home + me * rows
        elif step.kind == "ar":
            for d in near:
                come = lax.rem(me + d, size)
                remote(
                    run.now.at[pl.ds(run.now_at, run.now_rows)],
                    step.buf.at[come],
                    self.send.at[step.sem + d],
                    self.recv.at[step.sem + come],
                    self.place.device(axis, come),
                ).wait_recv()
            total = step.buf[0]
            for j in range(1, size):
                total = total + step.buf[j]
            step.sum[...] = total
            run.now, run.now_at = step.sum, 0
        else:
            for d in near:
                step.copies[d].wait_recv()
            run.home = run.home - me * run.now_rows
            run.now_rows = run.now_rows * size
        if n + 1 < len(run.steps) and run.steps[n + 1].kind == "ag":
            run.home = pl.multiple_of(run.home, 8)
            if step.kind != "ag":
                self.out[self.place.core, pl.ds(run.home, run.now_rows)] = run.now[...]


def moments_kernel(
    codes_in, scale_in, valid_ref, A, S, avg_ref, x_ref, codes_ref, scale_ref, load_sem, frames, turned, weighted, trailing, acc, summed, *rest
):
    (frame_send, frame_recv), rest = rest[:2], rest[2:]
    n = sum(kind != "ag" for part in PARTS for kind, _ in all_steps(part))
    loads = [
        pltpu.make_async_copy(scale_in, scale_ref, load_sem.at[0]),
        pltpu.make_async_copy(codes_in, codes_ref, load_sem.at[1]),
    ]
    for load in loads:
        load.start()
    place = Place()
    core = place.core
    streams = []
    for s, out in enumerate((summed.at[0], summed.at[1])):
        bufs, sums, sems = rest[:n], rest[n : 2 * n], rest[2 * n : 2 * n + 4]
        rest = rest[2 * n + 4 :]
        streams.append(Stream(place, acc.at[s], out, bufs, sums, *sems))
    instant, lagged = streams

    chips = 32
    before = lax.rem(place.chip + chips - 1, chips)
    after = lax.rem(place.chip + 1, chips)
    barrier = pltpu.get_barrier_semaphore()
    greeted = [place.partner, (place.traj, after * 2)]
    for axis, size in SIZE.items():
        greeted += [place.device(axis, lax.rem(place.at[axis] + d, size)) for d in range(1, size)]
    for device in greeted:
        pl.semaphore_signal(barrier, inc=1, device_id=device, device_id_type=MESH)

    rows_of = lax.broadcasted_iota(jnp.int32, (128, 128), 0)
    lanes_of = lax.broadcasted_iota(jnp.int32, (128, 128), 1)
    bf16, f32 = jnp.bfloat16, jnp.float32
    mine = pl.multiple_of(core * 256, 256)
    for load in loads:
        load.wait()
    for i in range(2):
        scale = jnp.transpose(jnp.broadcast_to(scale_ref[:, 128 * i : 128 * i + 128], (128, 128)))
        at = pl.ds(pl.multiple_of(mine + 128 * i, 128), 128)
        for p in range(4):
            codes = codes_ref[128 * i : 128 * i + 128, 128 * p : 128 * p + 128]
            x = (codes.astype(f32) * scale).astype(bf16)
            frames[p, at, :] = x
            x_ref[128 * i : 128 * i + 128, 128 * p : 128 * p + 128] = x

    pl.semaphore_wait(barrier, len(greeted) - 1 + 2 * (1 - core))
    own = frames.at[:, pl.ds(mine, 256), :]
    swap = remote(own, own, frame_send.at[0], frame_recv.at[0], place.partner)
    swap.start()
    first, halo = frames.at[:, pl.ds(0, LAG), :], frames.at[:, pl.ds(512, LAG), :]
    heads = [
        remote(first, halo, frame_send.at[1 + c], frame_recv.at[1], (place.traj, before * 2 + c)) for c in range(2)
    ]

    @pl.when(core == 0)
    def _():
        for c in heads:
            c.start()

    start = place.chip * 512
    valid = valid_ref[0]

    def rows_at(block):
        return pl.ds(pl.multiple_of(block * 128, 128), 128)

    def turn(block, panels):
        for p in panels:
            turned[p, block] = jnp.transpose(frames[p, rows_at(block), :].astype(f32)).astype(bf16)

    def prepare(block):
        t = rows_of + (start + block * 128)
        weight = jnp.where(t + LAG < valid, 1.0, 0.0) + jnp.where((t >= LAG) & (t < valid), 1.0, 0.0)
        for p in range(4):
            weighted[p, rows_at(block), :] = (frames[p, rows_at(block), :].astype(f32) * weight).astype(bf16)
        turn(block, (2 * core, 2 * core + 1))

    def product(a, *rights):
        left = jnp.concatenate([turned[a, i] for i in range(4)], axis=1)
        full = dot(left, jnp.concatenate([right[...] for right in rights], axis=1), ROWS, None)
        return [full[:, at_block(k)] for k in range(len(rights))]

    prepare(2 * core)
    prepare(2 * core + 1)
    swap.wait_recv()
    prepare(2 - 2 * core)
    prepare(3 - 2 * core)

    row8 = lax.broadcasted_iota(jnp.int32, (8, 128), 0)
    first_core = core == 0
    upper = product(2 * core, *[weighted.at[p] for p in range(4)])
    lower = product(2 * core + 1, weighted.at[1], weighted.at[3])
    acc[0, at_block(0)] = upper[1]
    acc[0, at_block(1)] = jnp.where(first_core, upper[2], upper[3])
    acc[0, at_block(2)] = jnp.where(first_core, upper[3], lower[0])
    on = [jnp.where(first_core, upper[0], upper[2]), jnp.where(first_core, lower[0], lower[1])]
    acc[0, 384:512] = jnp.where(rows_of <= lanes_of, on[0], on[1])
    diagonal = jnp.sum(jnp.where(rows_of == lanes_of, on[1], 0.0), axis=0, keepdims=True)
    ones = jnp.ones((16, 512), bf16)
    totals = jnp.concatenate(
        [jnp.zeros((4, 128), f32)] + [dot(ones, weighted[p], ROWS, None)[:1] for p in range(4)], axis=0
    )
    count = jnp.clip(valid - LAG - start, 0, 512).astype(f32) * 2.0
    extra = jnp.where(core == 0, totals, jnp.full((8, 128), count))
    acc[0, 512:520] = jnp.where(row8 == 0, diagonal, extra)
    acc[0, 520:HALF] = jnp.zeros((HALF - 520, 128), f32)
    instant.start()

    remote(first, halo, frame_send.at[1], frame_recv.at[1], (place.traj, after * 2)).wait_recv()
    for block in range(4):
        t = rows_of + (start + block * 128)
        for p in range(4):
            x = frames[p, 128 * block + LAG : 128 * block + LAG + 128, :].astype(f32)
            trailing[p, 128 * block : 128 * block + 128, :] = jnp.where(t + LAG < valid, x, 0.0).astype(bf16)
    for block in range(4):
        turn(block, (2 - 2 * core, 3 - 2 * core))
    full = [product(a, *[trailing.at[b] for b in range(4)]) for a in range(4)]
    for k in range(3):
        pair = [full[b][a] + jnp.transpose(full[a][b]) for a, b in BLOCKS[k]]
        acc[1, at_block(k)] = jnp.where(first_core, *pair)
    on = [jnp.where(first_core, full[i][i], full[i + 2][i + 2]) for i in range(2)]
    on = [x + jnp.transpose(x) for x in on]
    acc[1, 384:512] = jnp.where(rows_of >= lanes_of, on[0], on[1])
    diagonal = jnp.sum(jnp.where(rows_of == lanes_of, on[1], 0.0), axis=0, keepdims=True)
    acc[1, 512:520] = jnp.where(row8 == 0, diagonal, 0.0)
    acc[1, 520:HALF] = jnp.zeros((HALF - 520, 128), f32)

    instant.advance(0)
    lagged.start()
    instant.advance(1)
    instant.advance(2)
    lagged.advance(0)
    instant.advance(3)
    lagged.advance(1)
    instant.arrive()
    means = Means(summed.at[0], summed.at[1])
    means.instant_cov(A)
    D = A[at_block(0), at_block(0)]
    D = eliminate(A, 0, D)
    D = eliminate(A, 1, D, lambda: lagged.advance(2))
    D = eliminate(A, 2, D)
    eliminate(A, 3, D, lambda: lagged.advance(3))
    A[at_block(0), at_block(1)] = jnp.zeros((128, 128), f32)
    A[at_block(2), at_block(3)] = jnp.zeros((128, 128), f32)
    avg_ref[...] = jnp.concatenate(means.avg + means.avg, axis=0)
    lagged.arrive()
    means.lagged_cov(S)
    instant.close()
    lagged.close()
    swap.wait_send()

    @pl.when(core == 0)
    def _():
        for c in heads:
            c.wait_send()


def sum_scratch():
    bufs, sums, sems = [], [], 0
    for part in PARTS:
        rows = part[1]
        for kind, axis in all_steps(part):
            size = SIZE[axis]
            sems += size
            if kind == "rs":
                rows //= size
                bufs.append(pltpu.VMEM((size - 1, rows, 128), jnp.float32))
                sums.append(pltpu.VMEM((rows, 128), jnp.float32))
            elif kind == "ar":
                bufs.append(pltpu.VMEM((size, rows, 128), jnp.float32))
                sums.append(pltpu.VMEM((rows, 128), jnp.float32))
    return [
        *bufs,
        *sums,
        pltpu.SemaphoreType.DMA((sems,)),
        pltpu.SemaphoreType.DMA((sems,)),
        pltpu.SemaphoreType.DMA((len(PARTS),)),
        pltpu.SemaphoreType.DMA((len(PARTS),)),
    ]


def moments(codes, row_scale, valid):
    vmem = pl.BlockSpec(memory_space=pltpu.VMEM)
    hbm = pl.BlockSpec(memory_space=pltpu.HBM)
    square = jax.ShapeDtypeStruct((codes.shape[1], codes.shape[1]), jnp.float32)
    average = jax.ShapeDtypeStruct((8, 128), jnp.float32)
    return pl.pallas_call(
        moments_kernel,
        out_shape=(square, square, average, jax.ShapeDtypeStruct(codes.shape, codes.dtype)),
        in_specs=[hbm, hbm, pl.BlockSpec(memory_space=pltpu.SMEM)],
        out_specs=(vmem,) * 4,
        scratch_shapes=[
            pltpu.VMEM(codes.shape, codes.dtype),
            pltpu.VMEM(row_scale.shape, row_scale.dtype),
            pltpu.SemaphoreType.DMA((2,)),
            pltpu.VMEM((4, 512 + LAG, 128), jnp.bfloat16),
            pltpu.VMEM((4, 4, 128, 128), jnp.bfloat16),
            pltpu.VMEM((4, 512, 128), jnp.bfloat16),
            pltpu.VMEM((4, 512, 128), jnp.bfloat16),
            pltpu.VMEM((2, HALF, 128), jnp.float32),
            pltpu.VMEM((2, 2, HALF, 128), jnp.float32),
            pltpu.SemaphoreType.DMA((3,)),
            pltpu.SemaphoreType.DMA((2,)),
            *sum_scratch(),
            *sum_scratch(),
        ],
        compiler_params=pltpu.CompilerParams(
            collective_id=0, has_side_effects=True, vmem_limit_bytes=40 * 2**20
        ),
        name="moments",
    )(codes, row_scale, valid)


HIGHEST = lax.Precision.HIGHEST
ROWS = (((1,), (0,)), ((), ()))
LANES = (((1,), (1,)), ((), ()))
SUBLANES = (((0,), (0,)), ((), ()))


def dot(left, right, dims, precision=HIGHEST):
    return lax.dot_general(left, right, dims, precision=precision, preferred_element_type=jnp.float32)


def one_row(x, k):
    return jnp.broadcast_to(x[k : k + 1, :], (8, 128))


def one_lane(x, k):
    return jnp.broadcast_to(x[:, k : k + 1], (8, 128))


def inverse_factor(block, halfway=None):
    rows = list(block)
    n, size = len(rows), 8
    sub = lax.broadcasted_iota(jnp.int32, (8, 128), 0)
    lane = lax.broadcasted_iota(jnp.int32, (8, 128), 1)
    even = (sub % 2) == 0
    for group in range(0, n, size):
        end = group + size
        coming = [one_lane(rows[group], 8 * group + k) for k in range(8)]
        pivots = []
        for r in range(group, end):
            first = 8 * r
            last = r == end - 1
            columns = [[coming[k]] + [one_lane(rows[q], first + k) for q in range(r + 1, end)] for k in range(8)]
            if not last:
                coming = [one_lane(rows[r + 1], first + 8 + k) for k in range(8)]
            inside = (lane >= first) & (lane < first + 8)
            panel = jnp.where(inside, jnp.where(lane - first == sub, 1.0, 0.0), rows[r])
            for q in range(r + 1, end):
                rows[q] = jnp.where(inside, 0.0, rows[q])
            for k in range(0, 8, 2):
                left, right = columns[k], columns[k + 1]
                a, b, d = one_row(left[0], k), one_row(left[0], k + 1), one_row(right[0], k + 1)
                det = a * d - b * b
                rough = pl.reciprocal(det, approx=True)
                mend = 2.0 - det * rough
                inv = rough * mend
                a_inv, b_inv, d_inv = a * inv, b * inv, d * inv
                low, high = jnp.where(sub > k + 1, left[0], 0.0), jnp.where(sub > k + 1, right[0], 0.0)
                g, h = low * d - high * b, high * a - low * b
                f0 = [g * inv] + [x * d_inv - y * b_inv for x, y in zip(left[1:], right[1:])]
                f1 = [h * inv] + [y * a_inv - x * b_inv for x, y in zip(left[1:], right[1:])]
                for m in range(k + 2, 8):
                    e0, e1 = one_row(left[0], m), one_row(right[0], m)
                    columns[m] = [columns[m][0] - ((g * e0 + h * e1) * rough) * mend] + [
                        x - (u * e0 + v * e1) for x, u, v in zip(columns[m][1:], f0[1:], f1[1:])
                    ]
                if not last:
                    coming = [
                        coming[m] - (f0[1] * one_row(left[1], m) + f1[1] * one_row(right[1], m)) for m in range(8)
                    ]
                row0, row1 = one_row(panel, k), one_row(panel, k + 1)
                panel = panel - (f0[0] * row0 + f1[0] * row1)
                for q in range(r + 1, end):
                    rows[q] = rows[q] - (f0[q - r] * row0 + f1[q - r] * row1)
                if k == 0:
                    pivot = (a, b, det)
                else:
                    pivot = tuple(jnp.where(sub >= k, x, y) for x, y in zip((a, b, det), pivot))
            rows[r] = panel
            pivots.append(pivot)
        for r in range(group, end):
            a, b, det = pivots[r - group]
            above = pltpu.roll(rows[r], 1, 0)
            rows[r] = jnp.where(even, rows[r], rows[r] * a - above * b) * lax.rsqrt(jnp.where(even, a, a * det))
        if end < n:
            done = jnp.concatenate(rows[group:end], axis=0)
            down = lax.broadcasted_iota(jnp.int32, done.shape, 0) + 8 * group
            along = lax.broadcasted_iota(jnp.int32, done.shape, 1)
            change = dot(done, jnp.where((along > down) & (along < 8 * end), 0.0, done), SUBLANES)
            inside = (lane >= 8 * group) & (lane < 8 * end)
            for q in range(end, n):
                rows[q] = jnp.where(inside, 0.0, rows[q]) - change[8 * q : 8 * q + 8]
            if halfway is not None:
                halfway()
    return [jnp.where(lane <= sub + 8 * q, rows[q], 0.0) for q in range(n)]


def split3(x):
    high = x.astype(jnp.bfloat16)
    rest = x - high.astype(jnp.float32)
    middle = rest.astype(jnp.bfloat16)
    return high, middle, (rest - middle.astype(jnp.float32)).astype(jnp.bfloat16)


def at_block(i):
    return slice(128 * i, 128 * i + 128)


def eliminate(A, k, D, halfway=None):
    W = jnp.concatenate(inverse_factor([D[8 * q : 8 * q + 8, :] for q in range(16)], halfway), axis=0)
    A[at_block(k), at_block(k)] = W
    if k < 3:
        near = dot(W, A[at_block(k), at_block(k + 1)], ROWS)
        D = A[at_block(k + 1), at_block(k + 1)] - dot(near, near, SUBLANES)
        A[at_block(k), at_block(k + 1)] = near
    for lo, hi in ((0, 128 * k), (128 * (k + 2), 512)):
        if lo < hi:
            A[at_block(k), lo:hi] = dot(W, A[at_block(k), lo:hi], ROWS)
    if k < 3:
        below = 128 * (k + 1)
        change = dot(A[at_block(k), below:], A[at_block(k), :], SUBLANES)
        A[below:, at_block(k)] = -change[:, at_block(k)]
        if k > 0:
            A[below:, 0 : 128 * k] = A[below:, 0 : 128 * k] - change[:, 0 : 128 * k]
        if k < 2:
            A[below:, below + 128 :] = A[below:, below + 128 :] - change[:, below + 128 :]
    return D


class Means:
    def __init__(self, inst_ref, lag_ref):
        self.inst, self.lag = inst_ref, lag_ref
        self.inv = 1.0 / inst_ref[1, 516:517, :]
        self.avg = [inst_ref[0, 516 + j : 517 + j, :] * self.inv for j in range(4)]
        self.down = [jnp.transpose(jnp.broadcast_to(a, (128, 128))) for a in self.avg]
        self.ri = lax.broadcasted_iota(jnp.int32, (128, 128), 0)
        self.ci = lax.broadcasted_iota(jnp.int32, (128, 128), 1)

    def on_diagonal(self, ref, i):
        stored = ref[i // 2, 384:512] * self.inv
        turned = jnp.transpose(stored)
        if i % 2 == 0:
            return stored, turned, stored
        return turned, stored, ref[i // 2, 512:513] * self.inv

    def instant_cov(self, A):
        for k, pair in enumerate(UPPER):
            for c, (i, j) in enumerate(pair):
                block = self.inst[c, at_block(k)] * self.inv - self.down[i] * self.avg[j]
                if i < j:
                    A[at_block(i), at_block(j)] = block
                else:
                    A[at_block(j), at_block(i)] = jnp.transpose(block)
        for i in range(4):
            own, turned, diagonal = self.on_diagonal(self.inst, i)
            whole = jnp.where(self.ri < self.ci, own, jnp.where(self.ri > self.ci, turned, diagonal))
            A[at_block(i), at_block(i)] = whole - self.down[i] * self.avg[i]

    def lagged_cov(self, S):
        zero = jnp.zeros((128, 128), jnp.float32)
        S[at_block(0), at_block(1)] = zero
        S[at_block(2), at_block(3)] = zero
        for k, pair in enumerate(BLOCKS):
            for c, (i, j) in enumerate(pair):
                S[at_block(j), at_block(i)] = self.lag[c, at_block(k)] * self.inv - self.down[j] * self.avg[i]
        for i in range(4):
            outer = self.down[i] * self.avg[i]
            own, _, diagonal = self.on_diagonal(self.lag, i)
            S[at_block(i), at_block(i)] = jnp.where(
                self.ri > self.ci, own - outer, jnp.where(self.ri == self.ci, 0.5 * (diagonal - outer), 0.0)
            )


def finish_kernel(A, S, avg_ref, x_ref, white_ref, koop_ref, lhs):
    f32 = jnp.float32
    avg = [avg_ref[j : j + 1, :] for j in range(4)]
    a = [A[0:256, 0:256], A[256:512, 0:256], A[256:512, 256:512]]
    s = [S[0:256, 0:256], S[256:512, 0:256], S[256:512, 256:512]]
    x = x_ref[...]
    lhs[0:256, :] = x
    am = [jnp.concatenate([t[m] for t in [split3(q) for q in avg]], axis=1) for m in range(3)]
    lhs[256:272, :] = jnp.concatenate(am + [jnp.zeros((13, 512), jnp.bfloat16)], axis=0)
    y = [None, None]
    for t in split3(a[0]):
        v = dot(lhs[:, 0:256], t, LANES, None)
        y[0] = v if y[0] is None else y[0] + v
    for t, u in zip(split3(a[1]), split3(a[2])):
        v = dot(lhs[:, 0:256], t, LANES, None) + dot(lhs[:, 256:512], u, LANES, None)
        y[1] = v if y[1] is None else y[1] + v
    for h in range(2):
        m = y[h][256:257] + y[h][257:258] + y[h][258:259]
        white_ref[:, 256*h:256*h+256] = (y[h][0:256] - m).astype(jnp.bfloat16)
    nn = ROWS; nt = LANES
    t00 = dot(a[0], s[0], nn)
    t10 = dot(a[1], s[0], nn) + dot(a[2], s[1], nn)
    t11 = dot(a[2], s[2], nn)
    k00 = dot(t00, a[0], nt)
    k01 = dot(t00, a[1], nt)
    k10 = dot(t10, a[0], nt)
    k11 = dot(t10, a[1], nt) + dot(t11, a[2], nt)
    koop_ref[0:256, 0:256] = k00 + jnp.transpose(k00)
    koop_ref[256:512, 256:512] = k11 + jnp.transpose(k11)
    k10 = k10 + jnp.transpose(k01)
    koop_ref[256:512, 0:256] = k10
    koop_ref[0:256, 256:512] = jnp.transpose(k10)


def finish(whitener, lagged_cov, average, x):
    width = x.shape[1]
    return pl.pallas_call(
        finish_kernel,
        out_shape=(
            jax.ShapeDtypeStruct(x.shape, jnp.bfloat16),
            jax.ShapeDtypeStruct((width, width), jnp.float32),
        ),
        in_specs=[pl.BlockSpec(memory_space=pltpu.VMEM)] * 4,
        out_specs=(pl.BlockSpec(memory_space=pltpu.VMEM),) * 2,
        scratch_shapes=[pltpu.VMEM((x.shape[0] + 16, width), jnp.bfloat16)],
        compiler_params=pltpu.CompilerParams(vmem_limit_bytes=40 * 2**20),
        name="finish",
    )(whitener, lagged_cov, average, x)


def on_device(codes, row_scale, valid):
    projected, koopman = finish(*moments(codes[0], row_scale, valid))
    return (projected[None], koopman)


def solution(mesh):
    return jax.shard_map(
        on_device,
        mesh=mesh,
        in_specs=(P("traj", "blk", None), P("traj", "blk"), P("traj")),
        out_specs=(P("traj", "blk", None), P()),
        check_vma=False,
    )
```

```python
import jax
import jax.numpy as jnp
from jax import lax
from jax.experimental import pallas as pl
from jax.experimental.pallas import tpu as pltpu
from jax.sharding import PartitionSpec as P

MESH = pl.DeviceIdType.MESH
LAG = 64
HALF = 576
PARTS = (
    (0, 128, "x", (("ar", "y"), ("ar", "z"))),
    (128, 256, "y", (("ar", "z"), ("ar", "x"))),
    (384, 192, "z", (("ar", "x"), ("ar", "y"))),
)
SIZE = {"x": 4, "y": 8, "z": 8}
FAR = {4: (2, 1, 3), 8: (4, 3, 5, 2, 6, 1, 7)}
UPPER = (((0, 1), (2, 1)), ((0, 2), (2, 3)), ((0, 3), (3, 1)))
BLOCKS = (((0, 1), (1, 2)), ((0, 2), (1, 3)), ((0, 3), (2, 3)))


def all_steps(part):
    return (("rs", part[2]),) + part[3] + (("ag", part[2]),)


class Record:
    pass


class Place:
    def __init__(self):
        self.traj, self.blk = lax.axis_index("traj"), lax.axis_index("blk")
        self.core = lax.rem(self.blk, 2)
        self.chip = lax.div(self.blk, 2)
        self.at = {"x": lax.rem(self.chip, 4), "y": self.traj, "z": lax.div(self.blk, 8)}
        self.partner = (self.traj, self.blk + 1 - 2 * self.core)

    def device(self, axis, index):
        if axis == "x":
            return (self.traj, self.at["z"] * 8 + index * 2 + self.core)
        if axis == "y":
            return (index, self.blk)
        return (self.traj, index * 8 + self.at["x"] * 2 + self.core)


def remote(src, dst, send, recv, to):
    return pltpu.make_async_remote_copy(
        src_ref=src, dst_ref=dst, send_sem=send, recv_sem=recv, device_id=to, device_id_type=MESH
    )


class Stream:
    def __init__(self, place, acc, out, bufs, sums, send, recv, core_send, core_recv):
        self.place, self.acc, self.out = place, acc, out
        self.send, self.recv = send, recv
        self.core_send, self.core_recv = core_send, core_recv
        self.waiting, self.last, self.runs = [], {}, []
        sem_at = buf_at = 0
        for part in PARTS:
            run = Record()
            run.base, run.rows = part[0], part[1]
            run.steps = []
            for kind, axis in all_steps(part):
                step = Record()
                step.kind, step.axis, step.sem = kind, axis, sem_at
                sem_at += SIZE[axis]
                if kind != "ag":
                    step.buf, step.sum = bufs[buf_at], sums[buf_at]
                    buf_at += 1
                run.steps.append(step)
            self.runs.append(run)
        self.n_steps = max(len(run.steps) for run in self.runs)

    def start(self):
        for run in self.runs:
            run.now, run.now_at, run.now_rows = self.acc, run.base, run.rows
            run.home = run.base
        for run in self.runs[::-1]:
            self.begin(run, 0)

    def advance(self, n, parts=(2, 0, 1)):
        for k in parts:
            run = self.runs[k]
            if n < len(run.steps):
                self.finish(run, n)
                if n + 1 < len(run.steps):
                    self.begin(run, n + 1)
                else:
                    rows = self.out.at[self.place.core, pl.ds(run.base, run.rows)]
                    c = remote(rows, rows, self.core_send.at[k], self.core_recv.at[k], self.place.partner)
                    c.start()
                    self.last[k] = c

    def arrive(self, parts=(0, 1, 2)):
        for k in parts:
            self.last[k].wait_recv()

    def close(self):
        for c in self.waiting + list(self.last.values()):
            c.wait_send()

    def begin(self, run, n):
        step = run.steps[n]
        axis, size = step.axis, SIZE[step.axis]
        me = self.place.at[axis]
        step.copies = {}
        for d in FAR[size]:
            to = lax.rem(me + d, size)
            if step.kind == "rs":
                rows = run.now_rows // size
                src = run.now.at[pl.ds(pl.multiple_of(run.now_at + to * rows, 8), rows)]
                dst, slot = step.buf.at[d - 1], d
            elif step.kind == "ar":
                src = run.now.at[pl.ds(run.now_at, run.now_rows)]
                dst, slot = step.buf.at[me], me
            else:
                src = dst = self.out.at[self.place.core, pl.ds(run.home, run.now_rows)]
                slot = d
            step.copies[d] = remote(
                src, dst, self.send.at[step.sem + d], self.recv.at[step.sem + slot], self.place.device(axis, to)
            )
            step.copies[d].start()
        if step.kind == "ar":
            step.buf[me] = run.now[pl.ds(run.now_at, run.now_rows)]
        self.waiting.extend(step.copies.values())

    def finish(self, run, n):
        step = run.steps[n]
        axis, size = step.axis, SIZE[step.axis]
        me = self.place.at[axis]
        near = FAR[size][::-1]
        if step.kind == "rs":
            rows = run.now_rows // size
            total = run.now[pl.ds(pl.multiple_of(run.now_at + me * rows, 8), rows)]
            for d in near:
                step.copies[d].wait_recv()
                total = total + step.buf[d - 1]
            step.sum[...] = total
            run.now, run.now_at, run.now_rows = step.sum, 0, rows
            run.home = run.home + me * rows
        elif step.kind == "ar":
            for d in near:
                come = lax.rem(me + d, size)
                remote(
                    run.now.at[pl.ds(run.now_at, run.now_rows)],
                    step.buf.at[come],
                    self.send.at[step.sem + d],
                    self.recv.at[step.sem + come],
                    self.place.device(axis, come),
                ).wait_recv()
            total = step.buf[0]
            for j in range(1, size):
                total = total + step.buf[j]
            step.sum[...] = total
            run.now, run.now_at = step.sum, 0
        else:
            for d in near:
                step.copies[d].wait_recv()
            run.home = run.home - me * run.now_rows
            run.now_rows = run.now_rows * size
        if n + 1 < len(run.steps) and run.steps[n + 1].kind == "ag":
            run.home = pl.multiple_of(run.home, 8)
            if step.kind != "ag":
                self.out[self.place.core, pl.ds(run.home, run.now_rows)] = run.now[...]


def moments_kernel(
    codes_in, scale_in, valid_ref, A, S, white_ref, codes_ref, scale_ref, load_sem, lhs, frames, turned, weighted, trailing, acc, summed, *rest
):
    (frame_send, frame_recv), rest = rest[:2], rest[2:]
    n = sum(kind != "ag" for part in PARTS for kind, _ in all_steps(part))
    loads = [
        pltpu.make_async_copy(scale_in, scale_ref, load_sem.at[0]),
        pltpu.make_async_copy(codes_in, codes_ref, load_sem.at[1]),
    ]
    for load in loads:
        load.start()
    place = Place()
    core = place.core
    streams = []
    for s, out in enumerate((summed.at[0], summed.at[1])):
        bufs, sums, sems = rest[:n], rest[n : 2 * n], rest[2 * n : 2 * n + 4]
        rest = rest[2 * n + 4 :]
        streams.append(Stream(place, acc.at[s], out, bufs, sums, *sems))
    instant, lagged = streams

    chips = 32
    before = lax.rem(place.chip + chips - 1, chips)
    after = lax.rem(place.chip + 1, chips)
    barrier = pltpu.get_barrier_semaphore()
    greeted = [place.partner, (place.traj, after * 2)]
    for axis, size in SIZE.items():
        greeted += [place.device(axis, lax.rem(place.at[axis] + d, size)) for d in range(1, size)]
    for device in greeted:
        pl.semaphore_signal(barrier, inc=1, device_id=device, device_id_type=MESH)

    rows_of = lax.broadcasted_iota(jnp.int32, (128, 128), 0)
    lanes_of = lax.broadcasted_iota(jnp.int32, (128, 128), 1)
    bf16, f32 = jnp.bfloat16, jnp.float32
    mine = pl.multiple_of(core * 256, 256)
    for load in loads:
        load.wait()
    for i in range(2):
        scale = jnp.transpose(jnp.broadcast_to(scale_ref[:, 128 * i : 128 * i + 128], (128, 128)))
        at = pl.ds(pl.multiple_of(mine + 128 * i, 128), 128)
        for p in range(4):
            codes = codes_ref[128 * i : 128 * i + 128, 128 * p : 128 * p + 128]
            x = (codes.astype(f32) * scale).astype(bf16)
            frames[p, at, :] = x
            lhs[128 * i : 128 * i + 128, 128 * p : 128 * p + 128] = x

    pl.semaphore_wait(barrier, len(greeted) - 1 + 2 * (1 - core))
    own = frames.at[:, pl.ds(mine, 256), :]
    swap = remote(own, own, frame_send.at[0], frame_recv.at[0], place.partner)
    swap.start()
    first, halo = frames.at[:, pl.ds(0, LAG), :], frames.at[:, pl.ds(512, LAG), :]
    heads = [
        remote(first, halo, frame_send.at[1 + c], frame_recv.at[1], (place.traj, before * 2 + c)) for c in range(2)
    ]

    @pl.when(core == 0)
    def _():
        for c in heads:
            c.start()

    start = place.chip * 512
    valid = valid_ref[0]

    def rows_at(block):
        return pl.ds(pl.multiple_of(block * 128, 128), 128)

    def turn(block, panels):
        for p in panels:
            turned[p, block] = jnp.transpose(frames[p, rows_at(block), :].astype(f32)).astype(bf16)

    def prepare(block):
        t = rows_of + (start + block * 128)
        weight = jnp.where(t + LAG < valid, 1.0, 0.0) + jnp.where((t >= LAG) & (t < valid), 1.0, 0.0)
        for p in range(4):
            weighted[p, rows_at(block), :] = (frames[p, rows_at(block), :].astype(f32) * weight).astype(bf16)
        turn(block, (2 * core, 2 * core + 1))

    def product(a, *rights):
        left = jnp.concatenate([turned[a, i] for i in range(4)], axis=1)
        full = dot(left, jnp.concatenate([right[...] for right in rights], axis=1), ROWS, None)
        return [full[:, at_block(k)] for k in range(len(rights))]

    prepare(2 * core)
    prepare(2 * core + 1)
    swap.wait_recv()
    prepare(2 - 2 * core)
    prepare(3 - 2 * core)

    row8 = lax.broadcasted_iota(jnp.int32, (8, 128), 0)
    first_core = core == 0
    upper = product(2 * core, *[weighted.at[p] for p in range(4)])
    lower = product(2 * core + 1, weighted.at[1], weighted.at[3])
    acc[0, at_block(0)] = upper[1]
    acc[0, at_block(1)] = jnp.where(first_core, upper[2], upper[3])
    acc[0, at_block(2)] = jnp.where(first_core, upper[3], lower[0])
    on = [jnp.where(first_core, upper[0], upper[2]), jnp.where(first_core, lower[0], lower[1])]
    acc[0, 384:512] = jnp.where(rows_of <= lanes_of, on[0], on[1])
    diagonal = jnp.sum(jnp.where(rows_of == lanes_of, on[1], 0.0), axis=0, keepdims=True)
    ones = jnp.ones((16, 512), bf16)
    totals = jnp.concatenate(
        [jnp.zeros((4, 128), f32)] + [dot(ones, weighted[p], ROWS, None)[:1] for p in range(4)], axis=0
    )
    count = jnp.clip(valid - LAG - start, 0, 512).astype(f32) * 2.0
    extra = jnp.where(core == 0, totals, jnp.full((8, 128), count))
    acc[0, 512:520] = jnp.where(row8 == 0, diagonal, extra)
    acc[0, 520:HALF] = jnp.zeros((HALF - 520, 128), f32)
    instant.start()

    remote(first, halo, frame_send.at[1], frame_recv.at[1], (place.traj, after * 2)).wait_recv()
    for block in range(4):
        t = rows_of + (start + block * 128)
        for p in range(4):
            x = frames[p, 128 * block + LAG : 128 * block + LAG + 128, :].astype(f32)
            trailing[p, 128 * block : 128 * block + 128, :] = jnp.where(t + LAG < valid, x, 0.0).astype(bf16)
    for block in range(4):
        turn(block, (2 - 2 * core, 3 - 2 * core))
    full = [product(a, *[trailing.at[b] for b in range(4)]) for a in range(4)]
    for k in range(3):
        pair = [full[b][a] + jnp.transpose(full[a][b]) for a, b in BLOCKS[k]]
        acc[1, at_block(k)] = jnp.where(first_core, *pair)
    on = [jnp.where(first_core, full[i][i], full[i + 2][i + 2]) for i in range(2)]
    on = [x + jnp.transpose(x) for x in on]
    acc[1, 384:512] = jnp.where(rows_of >= lanes_of, on[0], on[1])
    diagonal = jnp.sum(jnp.where(rows_of == lanes_of, on[1], 0.0), axis=0, keepdims=True)
    acc[1, 512:520] = jnp.where(row8 == 0, diagonal, 0.0)
    acc[1, 520:HALF] = jnp.zeros((HALF - 520, 128), f32)

    instant.advance(0)
    lagged.start()
    instant.advance(1)
    instant.advance(2)
    lagged.advance(0)
    instant.advance(3, (2,))
    instant.arrive((2,))
    means = Means(summed.at[0], summed.at[1])
    means.instant_diagonal(A)

    def rest():
        instant.advance(3, (0, 1))
        lagged.advance(1)

    def upper_blocks():
        instant.arrive((0, 1))
        means.instant_cov(A)

    D = eliminate(A, 0, A[at_block(0), at_block(0)], rest, upper_blocks)
    D = eliminate(A, 1, D, lambda: lagged.advance(2))
    D = eliminate(A, 2, D)
    eliminate(A, 3, D, lambda: lagged.advance(3))
    A[at_block(0), at_block(1)] = jnp.zeros((128, 128), f32)
    A[at_block(2), at_block(3)] = jnp.zeros((128, 128), f32)
    whiten(A, means.avg, lhs, white_ref)
    lagged.arrive()
    means.lagged_cov(S)
    instant.close()
    lagged.close()
    swap.wait_send()

    @pl.when(core == 0)
    def _():
        for c in heads:
            c.wait_send()


def sum_scratch():
    bufs, sums, sems = [], [], 0
    for part in PARTS:
        rows = part[1]
        for kind, axis in all_steps(part):
            size = SIZE[axis]
            sems += size
            if kind == "rs":
                rows //= size
                bufs.append(pltpu.VMEM((size - 1, rows, 128), jnp.float32))
                sums.append(pltpu.VMEM((rows, 128), jnp.float32))
            elif kind == "ar":
                bufs.append(pltpu.VMEM((size, rows, 128), jnp.float32))
                sums.append(pltpu.VMEM((rows, 128), jnp.float32))
    return [
        *bufs,
        *sums,
        pltpu.SemaphoreType.DMA((sems,)),
        pltpu.SemaphoreType.DMA((sems,)),
        pltpu.SemaphoreType.DMA((len(PARTS),)),
        pltpu.SemaphoreType.DMA((len(PARTS),)),
    ]


def moments(codes, row_scale, valid):
    vmem = pl.BlockSpec(memory_space=pltpu.VMEM)
    hbm = pl.BlockSpec(memory_space=pltpu.HBM)
    square = jax.ShapeDtypeStruct((codes.shape[1], codes.shape[1]), jnp.float32)
    return pl.pallas_call(
        moments_kernel,
        out_shape=(square, square, jax.ShapeDtypeStruct(codes.shape, codes.dtype)),
        in_specs=[hbm, hbm, pl.BlockSpec(memory_space=pltpu.SMEM)],
        out_specs=(vmem,) * 3,
        scratch_shapes=[
            pltpu.VMEM(codes.shape, codes.dtype),
            pltpu.VMEM(row_scale.shape, row_scale.dtype),
            pltpu.SemaphoreType.DMA((2,)),
            pltpu.VMEM((codes.shape[0] + 16, codes.shape[1]), jnp.bfloat16),
            pltpu.VMEM((4, 512 + LAG, 128), jnp.bfloat16),
            pltpu.VMEM((4, 4, 128, 128), jnp.bfloat16),
            pltpu.VMEM((4, 512, 128), jnp.bfloat16),
            pltpu.VMEM((4, 512, 128), jnp.bfloat16),
            pltpu.VMEM((2, HALF, 128), jnp.float32),
            pltpu.VMEM((2, 2, HALF, 128), jnp.float32),
            pltpu.SemaphoreType.DMA((3,)),
            pltpu.SemaphoreType.DMA((2,)),
            *sum_scratch(),
            *sum_scratch(),
        ],
        compiler_params=pltpu.CompilerParams(
            collective_id=0, has_side_effects=True, vmem_limit_bytes=40 * 2**20
        ),
        name="moments",
    )(codes, row_scale, valid)


HIGHEST = lax.Precision.HIGHEST
ROWS = (((1,), (0,)), ((), ()))
LANES = (((1,), (1,)), ((), ()))
SUBLANES = (((0,), (0,)), ((), ()))


def dot(left, right, dims, precision=HIGHEST):
    return lax.dot_general(left, right, dims, precision=precision, preferred_element_type=jnp.float32)


def one_row(x, k):
    return jnp.broadcast_to(x[k : k + 1, :], (8, 128))


def one_lane(x, k):
    return jnp.broadcast_to(x[:, k : k + 1], (8, 128))


def inverse_factor(block, halfway=None):
    rows = list(block)
    n, size = len(rows), 8
    sub = lax.broadcasted_iota(jnp.int32, (8, 128), 0)
    lane = lax.broadcasted_iota(jnp.int32, (8, 128), 1)
    even = (sub % 2) == 0
    for group in range(0, n, size):
        end = group + size
        coming = [one_lane(rows[group], 8 * group + k) for k in range(8)]
        pivots = []
        for r in range(group, end):
            first = 8 * r
            last = r == end - 1
            columns = [[coming[k]] + [one_lane(rows[q], first + k) for q in range(r + 1, end)] for k in range(8)]
            if not last:
                coming = [one_lane(rows[r + 1], first + 8 + k) for k in range(8)]
            inside = (lane >= first) & (lane < first + 8)
            panel = jnp.where(inside, jnp.where(lane - first == sub, 1.0, 0.0), rows[r])
            for q in range(r + 1, end):
                rows[q] = jnp.where(inside, 0.0, rows[q])
            for k in range(0, 8, 2):
                left, right = columns[k], columns[k + 1]
                a, b, d = one_row(left[0], k), one_row(left[0], k + 1), one_row(right[0], k + 1)
                det = a * d - b * b
                rough = pl.reciprocal(det, approx=True)
                mend = 2.0 - det * rough
                inv = rough * mend
                a_inv, b_inv, d_inv = a * inv, b * inv, d * inv
                low, high = jnp.where(sub > k + 1, left[0], 0.0), jnp.where(sub > k + 1, right[0], 0.0)
                g, h = low * d - high * b, high * a - low * b
                f0 = [g * inv] + [x * d_inv - y * b_inv for x, y in zip(left[1:], right[1:])]
                f1 = [h * inv] + [y * a_inv - x * b_inv for x, y in zip(left[1:], right[1:])]
                for m in range(k + 2, 8):
                    e0, e1 = one_row(left[0], m), one_row(right[0], m)
                    columns[m] = [columns[m][0] - ((g * e0 + h * e1) * rough) * mend] + [
                        x - (u * e0 + v * e1) for x, u, v in zip(columns[m][1:], f0[1:], f1[1:])
                    ]
                if not last:
                    coming = [
                        coming[m] - (f0[1] * one_row(left[1], m) + f1[1] * one_row(right[1], m)) for m in range(8)
                    ]
                row0, row1 = one_row(panel, k), one_row(panel, k + 1)
                panel = panel - (f0[0] * row0 + f1[0] * row1)
                for q in range(r + 1, end):
                    rows[q] = rows[q] - (f0[q - r] * row0 + f1[q - r] * row1)
                if k == 0:
                    pivot = (a, b, det)
                else:
                    pivot = tuple(jnp.where(sub >= k, x, y) for x, y in zip((a, b, det), pivot))
            rows[r] = panel
            pivots.append(pivot)
        for r in range(group, end):
            a, b, det = pivots[r - group]
            above = pltpu.roll(rows[r], 1, 0)
            rows[r] = jnp.where(even, rows[r], rows[r] * a - above * b) * lax.rsqrt(jnp.where(even, a, a * det))
        if end < n:
            done = jnp.concatenate(rows[group:end], axis=0)
            down = lax.broadcasted_iota(jnp.int32, done.shape, 0) + 8 * group
            along = lax.broadcasted_iota(jnp.int32, done.shape, 1)
            change = dot(done, jnp.where((along > down) & (along < 8 * end), 0.0, done), SUBLANES)
            inside = (lane >= 8 * group) & (lane < 8 * end)
            for q in range(end, n):
                rows[q] = jnp.where(inside, 0.0, rows[q]) - change[8 * q : 8 * q + 8]
            if halfway is not None:
                halfway()
    return [jnp.where(lane <= sub + 8 * q, rows[q], 0.0) for q in range(n)]


def split3(x):
    high = x.astype(jnp.bfloat16)
    rest = x - high.astype(jnp.float32)
    middle = rest.astype(jnp.bfloat16)
    return high, middle, (rest - middle.astype(jnp.float32)).astype(jnp.bfloat16)


def at_block(i):
    return slice(128 * i, 128 * i + 128)


def eliminate(A, k, D, halfway=None, others=None):
    W = jnp.concatenate(inverse_factor([D[8 * q : 8 * q + 8, :] for q in range(16)], halfway), axis=0)
    if others is not None:
        others()
    A[at_block(k), at_block(k)] = W
    if k < 3:
        near = dot(W, A[at_block(k), at_block(k + 1)], ROWS)
        D = A[at_block(k + 1), at_block(k + 1)] - dot(near, near, SUBLANES)
        A[at_block(k), at_block(k + 1)] = near
    for lo, hi in ((0, 128 * k), (128 * (k + 2), 512)):
        if lo < hi:
            A[at_block(k), lo:hi] = dot(W, A[at_block(k), lo:hi], ROWS)
    if k < 3:
        below = 128 * (k + 1)
        change = dot(A[at_block(k), below:], A[at_block(k), :], SUBLANES)
        A[below:, at_block(k)] = -change[:, at_block(k)]
        if k > 0:
            A[below:, 0 : 128 * k] = A[below:, 0 : 128 * k] - change[:, 0 : 128 * k]
        if k < 2:
            A[below:, below + 128 :] = A[below:, below + 128 :] - change[:, below + 128 :]
    return D


class Means:
    def __init__(self, inst_ref, lag_ref):
        self.inst, self.lag = inst_ref, lag_ref
        self.inv = 1.0 / inst_ref[1, 516:517, :]
        self.avg = [inst_ref[0, 516 + j : 517 + j, :] * self.inv for j in range(4)]
        self.down = [jnp.transpose(jnp.broadcast_to(a, (128, 128))) for a in self.avg]
        self.ri = lax.broadcasted_iota(jnp.int32, (128, 128), 0)
        self.ci = lax.broadcasted_iota(jnp.int32, (128, 128), 1)

    def on_diagonal(self, ref, i):
        stored = ref[i // 2, 384:512] * self.inv
        turned = jnp.transpose(stored)
        if i % 2 == 0:
            return stored, turned, stored
        return turned, stored, ref[i // 2, 512:513] * self.inv

    def instant_cov(self, A):
        for k, pair in enumerate(UPPER):
            for c, (i, j) in enumerate(pair):
                block = self.inst[c, at_block(k)] * self.inv - self.down[i] * self.avg[j]
                if i < j:
                    A[at_block(i), at_block(j)] = block
                else:
                    A[at_block(j), at_block(i)] = jnp.transpose(block)

    def instant_diagonal(self, A):
        for i in range(4):
            own, turned, diagonal = self.on_diagonal(self.inst, i)
            whole = jnp.where(self.ri < self.ci, own, jnp.where(self.ri > self.ci, turned, diagonal))
            A[at_block(i), at_block(i)] = whole - self.down[i] * self.avg[i]

    def lagged_cov(self, S):
        zero = jnp.zeros((128, 128), jnp.float32)
        S[at_block(0), at_block(1)] = zero
        S[at_block(2), at_block(3)] = zero
        for k, pair in enumerate(BLOCKS):
            for c, (i, j) in enumerate(pair):
                S[at_block(j), at_block(i)] = self.lag[c, at_block(k)] * self.inv - self.down[j] * self.avg[i]
        for i in range(4):
            outer = self.down[i] * self.avg[i]
            own, _, diagonal = self.on_diagonal(self.lag, i)
            S[at_block(i), at_block(i)] = jnp.where(
                self.ri > self.ci, own - outer, jnp.where(self.ri == self.ci, 0.5 * (diagonal - outer), 0.0)
            )


def whiten(A, avg, lhs, white_ref):
    a = [A[0:256, 0:256], A[256:512, 0:256], A[256:512, 256:512]]
    am = [jnp.concatenate([t[m] for t in [split3(q) for q in avg]], axis=1) for m in range(3)]
    lhs[256:272, :] = jnp.concatenate(am + [jnp.zeros((13, 512), jnp.bfloat16)], axis=0)
    y = [None, None]
    for t in split3(a[0]):
        v = dot(lhs[:, 0:256], t, LANES, None)
        y[0] = v if y[0] is None else y[0] + v
    for t, u in zip(split3(a[1]), split3(a[2])):
        v = dot(lhs[:, 0:256], t, LANES, None) + dot(lhs[:, 256:512], u, LANES, None)
        y[1] = v if y[1] is None else y[1] + v
    for h in range(2):
        m = y[h][256:257] + y[h][257:258] + y[h][258:259]
        white_ref[:, 256*h:256*h+256] = (y[h][0:256] - m).astype(jnp.bfloat16)


def finish_kernel(A, S, white_in, white_ref, koop_ref, sem):
    handed_on = pltpu.make_async_copy(white_in, white_ref, sem)
    handed_on.start()
    a = [A[0:256, 0:256], A[256:512, 0:256], A[256:512, 256:512]]
    s = [S[0:256, 0:256], S[256:512, 0:256], S[256:512, 256:512]]
    nn = ROWS; nt = LANES
    t00 = dot(a[0], s[0], nn)
    t10 = dot(a[1], s[0], nn) + dot(a[2], s[1], nn)
    t11 = dot(a[2], s[2], nn)
    k00 = dot(t00, a[0], nt)
    k01 = dot(t00, a[1], nt)
    k10 = dot(t10, a[0], nt)
    k11 = dot(t10, a[1], nt) + dot(t11, a[2], nt)
    koop_ref[0:256, 0:256] = k00 + jnp.transpose(k00)
    koop_ref[256:512, 256:512] = k11 + jnp.transpose(k11)
    k10 = k10 + jnp.transpose(k01)
    koop_ref[256:512, 0:256] = k10
    koop_ref[0:256, 256:512] = jnp.transpose(k10)
    handed_on.wait()


def finish(whitener, lagged_cov, whitened):
    return pl.pallas_call(
        finish_kernel,
        out_shape=(
            jax.ShapeDtypeStruct(whitened.shape, whitened.dtype),
            jax.ShapeDtypeStruct(whitener.shape, jnp.float32),
        ),
        in_specs=[pl.BlockSpec(memory_space=pltpu.VMEM)] * 3,
        out_specs=(pl.BlockSpec(memory_space=pltpu.HBM), pl.BlockSpec(memory_space=pltpu.VMEM)),
        scratch_shapes=[pltpu.SemaphoreType.DMA],
        compiler_params=pltpu.CompilerParams(vmem_limit_bytes=40 * 2**20),
        name="finish",
    )(whitener, lagged_cov, whitened)


def on_device(codes, row_scale, valid):
    projected, koopman = finish(*moments(codes[0], row_scale, valid))
    return (projected[None], koopman)


def solution(mesh):
    return jax.shard_map(
        on_device,
        mesh=mesh,
        in_specs=(P("traj", "blk", None), P("traj", "blk"), P("traj")),
        out_specs=(P("traj", "blk", None), P()),
        check_vma=False,
    )
```

```python
import jax
import jax.numpy as jnp
from jax import lax
from jax.experimental import pallas as pl
from jax.experimental.pallas import tpu as pltpu
from jax.sharding import PartitionSpec as P

MESH = pl.DeviceIdType.MESH
LAG = 64
HALF = 544
PARTS = (
    (0, 96, "x", (("ar", "y"), ("ar", "z"))),
    (96, 192, "y", (("ar", "z"), ("ar", "x"))),
    (288, 256, "z", (("ar", "x"), ("ar", "y"))),
)
SIZE = {"x": 4, "y": 8, "z": 8}
FAR = {4: (2, 1, 3), 8: (4, 3, 5, 2, 6, 1, 7)}
UPPER = (((0, 1), (2, 1)), ((0, 2), (2, 3)), ((0, 3), (3, 1)))
BLOCKS = (((0, 1), (1, 2)), ((0, 2), (1, 3)), ((0, 3), (2, 3)))


def all_steps(part):
    return (("rs", part[2]),) + part[3] + (("ag", part[2]),)


class Record:
    pass


class Place:
    def __init__(self):
        self.traj, self.blk = lax.axis_index("traj"), lax.axis_index("blk")
        self.core = lax.rem(self.blk, 2)
        self.chip = lax.div(self.blk, 2)
        self.at = {"x": lax.rem(self.chip, 4), "y": self.traj, "z": lax.div(self.blk, 8)}
        self.partner = (self.traj, self.blk + 1 - 2 * self.core)

    def device(self, axis, index):
        if axis == "x":
            return (self.traj, self.at["z"] * 8 + index * 2 + self.core)
        if axis == "y":
            return (index, self.blk)
        return (self.traj, index * 8 + self.at["x"] * 2 + self.core)


def remote(src, dst, send, recv, to):
    return pltpu.make_async_remote_copy(
        src_ref=src, dst_ref=dst, send_sem=send, recv_sem=recv, device_id=to, device_id_type=MESH
    )


class Stream:
    def __init__(self, place, acc, out, bufs, sums, send, recv, core_send, core_recv):
        self.place, self.acc, self.out = place, acc, out
        self.send, self.recv = send, recv
        self.core_send, self.core_recv = core_send, core_recv
        self.waiting, self.last, self.runs = [], [], []
        sem_at = buf_at = 0
        for part in PARTS:
            run = Record()
            run.base, run.rows = part[0], part[1]
            run.steps = []
            for kind, axis in all_steps(part):
                step = Record()
                step.kind, step.axis, step.sem = kind, axis, sem_at
                sem_at += SIZE[axis]
                if kind != "ag":
                    step.buf, step.sum = bufs[buf_at], sums[buf_at]
                    buf_at += 1
                run.steps.append(step)
            self.runs.append(run)
        self.n_steps = max(len(run.steps) for run in self.runs)

    def start(self):
        for run in self.runs:
            run.now, run.now_at, run.now_rows = self.acc, run.base, run.rows
            run.home = run.base
        for run in self.runs[::-1]:
            self.begin(run, 0)

    def advance(self, n):
        for k, run in enumerate(self.runs):
            if n < len(run.steps):
                self.finish(run, n)
                if n + 1 < len(run.steps):
                    self.begin(run, n + 1)
                else:
                    rows = self.out.at[self.place.core, pl.ds(run.base, run.rows)]
                    c = remote(rows, rows, self.core_send.at[k], self.core_recv.at[k], self.place.partner)
                    c.start()
                    self.last.append(c)

    def arrive(self):
        for c in self.last:
            c.wait_recv()

    def close(self):
        for c in self.waiting + self.last:
            c.wait_send()

    def begin(self, run, n):
        step = run.steps[n]
        axis, size = step.axis, SIZE[step.axis]
        me = self.place.at[axis]
        step.copies = {}
        for d in FAR[size]:
            to = lax.rem(me + d, size)
            if step.kind == "rs":
                rows = run.now_rows // size
                src = run.now.at[pl.ds(pl.multiple_of(run.now_at + to * rows, 8), rows)]
                dst, slot = step.buf.at[d - 1], d
            elif step.kind == "ar":
                src = run.now.at[pl.ds(run.now_at, run.now_rows)]
                dst, slot = step.buf.at[me], me
            else:
                src = dst = self.out.at[self.place.core, pl.ds(run.home, run.now_rows)]
                slot = d
            step.copies[d] = remote(
                src, dst, self.send.at[step.sem + d], self.recv.at[step.sem + slot], self.place.device(axis, to)
            )
            step.copies[d].start()
        if step.kind == "ar":
            step.buf[me] = run.now[pl.ds(run.now_at, run.now_rows)]
        self.waiting.extend(step.copies.values())

    def finish(self, run, n):
        step = run.steps[n]
        axis, size = step.axis, SIZE[step.axis]
        me = self.place.at[axis]
        near = FAR[size][::-1]
        if step.kind == "rs":
            rows = run.now_rows // size
            total = run.now[pl.ds(pl.multiple_of(run.now_at + me * rows, 8), rows)]
            for d in near:
                step.copies[d].wait_recv()
                total = total + step.buf[d - 1]
            step.sum[...] = total
            run.now, run.now_at, run.now_rows = step.sum, 0, rows
            run.home = run.home + me * rows
        elif step.kind == "ar":
            for d in near:
                come = lax.rem(me + d, size)
                remote(
                    run.now.at[pl.ds(run.now_at, run.now_rows)],
                    step.buf.at[come],
                    self.send.at[step.sem + d],
                    self.recv.at[step.sem + come],
                    self.place.device(axis, come),
                ).wait_recv()
            total = step.buf[0]
            for j in range(1, size):
                total = total + step.buf[j]
            step.sum[...] = total
            run.now, run.now_at = step.sum, 0
        else:
            for d in near:
                step.copies[d].wait_recv()
            run.home = run.home - me * run.now_rows
            run.now_rows = run.now_rows * size
        if n + 1 < len(run.steps) and run.steps[n + 1].kind == "ag":
            run.home = pl.multiple_of(run.home, 8)
            if step.kind != "ag":
                self.out[self.place.core, pl.ds(run.home, run.now_rows)] = run.now[...]


def tica_kernel(
    codes_in, scale_in, valid_ref, white_out, koop_out, A, S, white, koop, out_sem, codes_ref, scale_ref, load_sem, lhs, frames, turned, weighted, trailing, acc, summed, *rest
):
    (frame_send, frame_recv), rest = rest[:2], rest[2:]
    n = sum(kind != "ag" for part in PARTS for kind, _ in all_steps(part))
    loads = [
        pltpu.make_async_copy(scale_in, scale_ref, load_sem.at[0]),
        pltpu.make_async_copy(codes_in, codes_ref, load_sem.at[1]),
    ]
    for load in loads:
        load.start()
    place = Place()
    core = place.core
    streams = []
    for s, out in enumerate((summed.at[0], summed.at[1])):
        bufs, sums, sems = rest[:n], rest[n : 2 * n], rest[2 * n : 2 * n + 4]
        rest = rest[2 * n + 4 :]
        streams.append(Stream(place, acc.at[s], out, bufs, sums, *sems))
    instant, lagged = streams

    chips = 32
    before = lax.rem(place.chip + chips - 1, chips)
    after = lax.rem(place.chip + 1, chips)
    barrier = pltpu.get_barrier_semaphore()
    greeted = [place.partner, (place.traj, after * 2)]
    for axis, size in SIZE.items():
        greeted += [place.device(axis, lax.rem(place.at[axis] + d, size)) for d in range(1, size)]
    for device in greeted:
        pl.semaphore_signal(barrier, inc=1, device_id=device, device_id_type=MESH)

    rows_of = lax.broadcasted_iota(jnp.int32, (128, 128), 0)
    lanes_of = lax.broadcasted_iota(jnp.int32, (128, 128), 1)
    bf16, f32 = jnp.bfloat16, jnp.float32
    mine = pl.multiple_of(core * 256, 256)
    for load in loads:
        load.wait()
    for i in range(2):
        scale = jnp.transpose(jnp.broadcast_to(scale_ref[:, 128 * i : 128 * i + 128], (128, 128)))
        at = pl.ds(pl.multiple_of(mine + 128 * i, 128), 128)
        for p in range(4):
            codes = codes_ref[128 * i : 128 * i + 128, 128 * p : 128 * p + 128]
            x = (codes.astype(f32) * scale).astype(bf16)
            frames[p, at, :] = x
            lhs[128 * i : 128 * i + 128, 128 * p : 128 * p + 128] = x

    pl.semaphore_wait(barrier, len(greeted) - 1 + 2 * (1 - core))
    own = frames.at[:, pl.ds(mine, 256), :]
    swap = remote(own, own, frame_send.at[0], frame_recv.at[0], place.partner)
    swap.start()
    first, halo = frames.at[:, pl.ds(0, LAG), :], frames.at[:, pl.ds(512, LAG), :]
    heads = [
        remote(first, halo, frame_send.at[1 + c], frame_recv.at[1], (place.traj, before * 2 + c)) for c in range(2)
    ]

    @pl.when(core == 0)
    def _():
        for c in heads:
            c.start()

    start = place.chip * 512
    valid = valid_ref[0]

    def rows_at(block):
        return pl.ds(pl.multiple_of(block * 128, 128), 128)

    def turn(block, panels):
        for p in panels:
            turned[p, block] = jnp.transpose(frames[p, rows_at(block), :].astype(f32)).astype(bf16)

    def prepare(block):
        t = rows_of + (start + block * 128)
        weight = jnp.where(t + LAG < valid, 1.0, 0.0) + jnp.where((t >= LAG) & (t < valid), 1.0, 0.0)
        for p in range(4):
            weighted[p, rows_at(block), :] = (frames[p, rows_at(block), :].astype(f32) * weight).astype(bf16)
        turn(block, (2 * core, 2 * core + 1))

    def product(a, *rights):
        left = jnp.concatenate([turned[a, i] for i in range(4)], axis=1)
        full = dot(left, jnp.concatenate([right[...] for right in rights], axis=1), ROWS, None)
        return [full[:, at_block(k)] for k in range(len(rights))]

    prepare(2 * core)
    prepare(2 * core + 1)
    swap.wait_recv()
    prepare(2 - 2 * core)
    prepare(3 - 2 * core)

    row8 = lax.broadcasted_iota(jnp.int32, (8, 128), 0)
    first_core = core == 0
    upper = product(2 * core, *[weighted.at[p] for p in range(4)])
    lower = product(2 * core + 1, weighted.at[1], weighted.at[3])
    acc[0, at_block(0)] = upper[1]
    acc[0, at_block(1)] = jnp.where(first_core, upper[2], upper[3])
    acc[0, at_block(2)] = jnp.where(first_core, upper[3], lower[0])
    on = [jnp.where(first_core, upper[0], upper[2]), jnp.where(first_core, lower[0], lower[1])]
    acc[0, 384:512] = jnp.where(rows_of <= lanes_of, on[0], on[1])
    diagonal = jnp.sum(jnp.where(rows_of == lanes_of, on[1], 0.0), axis=0, keepdims=True)
    ones = jnp.ones((16, 512), bf16)
    totals = jnp.concatenate(
        [jnp.zeros((4, 128), f32)] + [dot(ones, weighted[p], ROWS, None)[:1] for p in range(4)], axis=0
    )
    count = jnp.clip(valid - LAG - start, 0, 512).astype(f32) * 2.0
    extra = jnp.where(core == 0, totals, jnp.full((8, 128), count))
    acc[0, 512:520] = jnp.where(row8 == 0, diagonal, extra)
    acc[0, 520:HALF] = jnp.zeros((HALF - 520, 128), f32)
    instant.start()

    remote(first, halo, frame_send.at[1], frame_recv.at[1], (place.traj, after * 2)).wait_recv()
    for block in range(4):
        t = rows_of + (start + block * 128)
        for p in range(4):
            x = frames[p, 128 * block + LAG : 128 * block + LAG + 128, :].astype(f32)
            trailing[p, 128 * block : 128 * block + 128, :] = jnp.where(t + LAG < valid, x, 0.0).astype(bf16)
    for block in range(4):
        turn(block, (2 - 2 * core, 3 - 2 * core))
    full = [product(a, *[trailing.at[b] for b in range(4)]) for a in range(4)]
    for k in range(3):
        pair = [full[b][a] + jnp.transpose(full[a][b]) for a, b in BLOCKS[k]]
        acc[1, at_block(k)] = jnp.where(first_core, *pair)
    on = [jnp.where(first_core, full[i][i], full[i + 2][i + 2]) for i in range(2)]
    on = [x + jnp.transpose(x) for x in on]
    acc[1, 384:512] = jnp.where(rows_of >= lanes_of, on[0], on[1])
    diagonal = jnp.sum(jnp.where(rows_of == lanes_of, on[1], 0.0), axis=0, keepdims=True)
    acc[1, 512:520] = jnp.where(row8 == 0, diagonal, 0.0)
    acc[1, 520:HALF] = jnp.zeros((HALF - 520, 128), f32)

    instant.advance(0)
    lagged.start()
    instant.advance(1)
    instant.advance(2)
    lagged.advance(0)
    instant.advance(3)
    lagged.advance(1)
    instant.arrive()
    means = Means(summed.at[0], summed.at[1])
    means.instant_cov(A)
    D = A[at_block(0), at_block(0)]
    D = eliminate(A, 0, D)
    D = eliminate(A, 1, D, lambda: lagged.advance(2))
    D = eliminate(A, 2, D)
    eliminate(A, 3, D, lambda: lagged.advance(3))
    A[at_block(0), at_block(1)] = jnp.zeros((128, 128), f32)
    A[at_block(2), at_block(3)] = jnp.zeros((128, 128), f32)
    whiten(A, means.avg, lhs, white)
    out_white = pltpu.make_async_copy(white, white_out, out_sem.at[0])
    out_white.start()
    lagged.arrive()
    means.lagged_cov(S)
    out_koop = []

    def written(i):
        half = pl.ds(256 * i, 256)
        out_koop.append(pltpu.make_async_copy(koop.at[half], koop_out.at[half], out_sem.at[1 + i]))
        out_koop[-1].start()

    whiten_lagged(A, S, koop, written)
    instant.close()
    lagged.close()
    swap.wait_send()
    out_white.wait()
    for c in out_koop:
        c.wait()

    @pl.when(core == 0)
    def _():
        for c in heads:
            c.wait_send()


def sum_scratch():
    bufs, sums, sems = [], [], 0
    for part in PARTS:
        rows = part[1]
        for kind, axis in all_steps(part):
            size = SIZE[axis]
            sems += size
            if kind == "rs":
                rows //= size
                bufs.append(pltpu.VMEM((size - 1, rows, 128), jnp.float32))
                sums.append(pltpu.VMEM((rows, 128), jnp.float32))
            elif kind == "ar":
                bufs.append(pltpu.VMEM((size, rows, 128), jnp.float32))
                sums.append(pltpu.VMEM((rows, 128), jnp.float32))
    return [
        *bufs,
        *sums,
        pltpu.SemaphoreType.DMA((sems,)),
        pltpu.SemaphoreType.DMA((sems,)),
        pltpu.SemaphoreType.DMA((len(PARTS),)),
        pltpu.SemaphoreType.DMA((len(PARTS),)),
    ]


def tica(codes, row_scale, valid):
    hbm = pl.BlockSpec(memory_space=pltpu.HBM)
    square = jax.ShapeDtypeStruct((codes.shape[1], codes.shape[1]), jnp.float32)
    return pl.pallas_call(
        tica_kernel,
        out_shape=(jax.ShapeDtypeStruct(codes.shape, codes.dtype), square),
        in_specs=[hbm, hbm, pl.BlockSpec(memory_space=pltpu.SMEM)],
        out_specs=(hbm, hbm),
        scratch_shapes=[
            pltpu.VMEM(square.shape, square.dtype),
            pltpu.VMEM(square.shape, square.dtype),
            pltpu.VMEM(codes.shape, codes.dtype),
            pltpu.VMEM(square.shape, square.dtype),
            pltpu.SemaphoreType.DMA((3,)),
            pltpu.VMEM(codes.shape, codes.dtype),
            pltpu.VMEM(row_scale.shape, row_scale.dtype),
            pltpu.SemaphoreType.DMA((2,)),
            pltpu.VMEM((codes.shape[0] + 16, codes.shape[1]), jnp.bfloat16),
            pltpu.VMEM((4, 512 + LAG, 128), jnp.bfloat16),
            pltpu.VMEM((4, 4, 128, 128), jnp.bfloat16),
            pltpu.VMEM((4, 512, 128), jnp.bfloat16),
            pltpu.VMEM((4, 512, 128), jnp.bfloat16),
            pltpu.VMEM((2, HALF, 128), jnp.float32),
            pltpu.VMEM((2, 2, HALF, 128), jnp.float32),
            pltpu.SemaphoreType.DMA((3,)),
            pltpu.SemaphoreType.DMA((2,)),
            *sum_scratch(),
            *sum_scratch(),
        ],
        compiler_params=pltpu.CompilerParams(
            collective_id=0, has_side_effects=True, vmem_limit_bytes=58 * 2**20
        ),
        name="tica",
    )(codes, row_scale, valid)


HIGHEST = lax.Precision.HIGHEST
ROWS = (((1,), (0,)), ((), ()))
LANES = (((1,), (1,)), ((), ()))
SUBLANES = (((0,), (0,)), ((), ()))


def dot(left, right, dims, precision=HIGHEST):
    return lax.dot_general(left, right, dims, precision=precision, preferred_element_type=jnp.float32)


def one_row(x, k):
    return jnp.broadcast_to(x[k : k + 1, :], (8, 128))


def one_lane(x, k):
    return jnp.broadcast_to(x[:, k : k + 1], (8, 128))


def inverse_factor(block, halfway=None):
    rows = list(block)
    n, size = len(rows), 8
    sub = lax.broadcasted_iota(jnp.int32, (8, 128), 0)
    lane = lax.broadcasted_iota(jnp.int32, (8, 128), 1)
    even = (sub % 2) == 0
    for group in range(0, n, size):
        end = group + size
        coming = [one_lane(rows[group], 8 * group + k) for k in range(8)]
        pivots = []
        for r in range(group, end):
            first = 8 * r
            last = r == end - 1
            columns = [[coming[k]] + [one_lane(rows[q], first + k) for q in range(r + 1, end)] for k in range(8)]
            if not last:
                coming = [one_lane(rows[r + 1], first + 8 + k) for k in range(8)]
            inside = (lane >= first) & (lane < first + 8)
            panel = jnp.where(inside, jnp.where(lane - first == sub, 1.0, 0.0), rows[r])
            for q in range(r + 1, end):
                rows[q] = jnp.where(inside, 0.0, rows[q])
            for k in range(0, 8, 2):
                left, right = columns[k], columns[k + 1]
                a, b, d = one_row(left[0], k), one_row(left[0], k + 1), one_row(right[0], k + 1)
                det = a * d - b * b
                rough = pl.reciprocal(det, approx=True)
                mend = 2.0 - det * rough
                inv = rough * mend
                a_inv, b_inv, d_inv = a * inv, b * inv, d * inv
                low, high = jnp.where(sub > k + 1, left[0], 0.0), jnp.where(sub > k + 1, right[0], 0.0)
                g, h = low * d - high * b, high * a - low * b
                f0 = [g * inv] + [x * d_inv - y * b_inv for x, y in zip(left[1:], right[1:])]
                f1 = [h * inv] + [y * a_inv - x * b_inv for x, y in zip(left[1:], right[1:])]
                for m in range(k + 2, 8):
                    e0, e1 = one_row(left[0], m), one_row(right[0], m)
                    columns[m] = [columns[m][0] - ((g * e0 + h * e1) * rough) * mend] + [
                        x - (u * e0 + v * e1) for x, u, v in zip(columns[m][1:], f0[1:], f1[1:])
                    ]
                if not last:
                    coming = [
                        coming[m] - (f0[1] * one_row(left[1], m) + f1[1] * one_row(right[1], m)) for m in range(8)
                    ]
                row0, row1 = one_row(panel, k), one_row(panel, k + 1)
                panel = panel - (f0[0] * row0 + f1[0] * row1)
                for q in range(r + 1, end):
                    rows[q] = rows[q] - (f0[q - r] * row0 + f1[q - r] * row1)
                if k == 0:
                    pivot = (a, b, det)
                else:
                    pivot = tuple(jnp.where(sub >= k, x, y) for x, y in zip((a, b, det), pivot))
            rows[r] = panel
            pivots.append(pivot)
        for r in range(group, end):
            a, b, det = pivots[r - group]
            above = pltpu.roll(rows[r], 1, 0)
            rows[r] = jnp.where(even, rows[r], rows[r] * a - above * b) * lax.rsqrt(jnp.where(even, a, a * det))
        if end < n:
            done = jnp.concatenate(rows[group:end], axis=0)
            down = lax.broadcasted_iota(jnp.int32, done.shape, 0) + 8 * group
            along = lax.broadcasted_iota(jnp.int32, done.shape, 1)
            change = dot(done, jnp.where((along > down) & (along < 8 * end), 0.0, done), SUBLANES)
            inside = (lane >= 8 * group) & (lane < 8 * end)
            for q in range(end, n):
                rows[q] = jnp.where(inside, 0.0, rows[q]) - change[8 * q : 8 * q + 8]
            if halfway is not None:
                halfway()
    return [jnp.where(lane <= sub + 8 * q, rows[q], 0.0) for q in range(n)]


def split3(x):
    high = x.astype(jnp.bfloat16)
    rest = x - high.astype(jnp.float32)
    middle = rest.astype(jnp.bfloat16)
    return high, middle, (rest - middle.astype(jnp.float32)).astype(jnp.bfloat16)


def at_block(i):
    return slice(128 * i, 128 * i + 128)


def eliminate(A, k, D, halfway=None):
    W = jnp.concatenate(inverse_factor([D[8 * q : 8 * q + 8, :] for q in range(16)], halfway), axis=0)
    A[at_block(k), at_block(k)] = W
    if k < 3:
        near = dot(W, A[at_block(k), at_block(k + 1)], ROWS)
        D = A[at_block(k + 1), at_block(k + 1)] - dot(near, near, SUBLANES)
        A[at_block(k), at_block(k + 1)] = near
    for lo, hi in ((0, 128 * k), (128 * (k + 2), 512)):
        if lo < hi:
            A[at_block(k), lo:hi] = dot(W, A[at_block(k), lo:hi], ROWS)
    if k < 3:
        below = 128 * (k + 1)
        change = dot(A[at_block(k), below:], A[at_block(k), :], SUBLANES)
        A[below:, at_block(k)] = -change[:, at_block(k)]
        if k > 0:
            A[below:, 0 : 128 * k] = A[below:, 0 : 128 * k] - change[:, 0 : 128 * k]
        if k < 2:
            A[below:, below + 128 :] = A[below:, below + 128 :] - change[:, below + 128 :]
    return D


class Means:
    def __init__(self, inst_ref, lag_ref):
        self.inst, self.lag = inst_ref, lag_ref
        self.inv = 1.0 / inst_ref[1, 516:517, :]
        self.avg = [inst_ref[0, 516 + j : 517 + j, :] * self.inv for j in range(4)]
        self.down = [jnp.transpose(jnp.broadcast_to(a, (128, 128))) for a in self.avg]
        self.ri = lax.broadcasted_iota(jnp.int32, (128, 128), 0)
        self.ci = lax.broadcasted_iota(jnp.int32, (128, 128), 1)

    def on_diagonal(self, ref, i):
        stored = ref[i // 2, 384:512] * self.inv
        turned = jnp.transpose(stored)
        if i % 2 == 0:
            return stored, turned, stored
        return turned, stored, ref[i // 2, 512:513] * self.inv

    def instant_cov(self, A):
        for k, pair in enumerate(UPPER):
            for c, (i, j) in enumerate(pair):
                block = self.inst[c, at_block(k)] * self.inv - self.down[i] * self.avg[j]
                if i < j:
                    A[at_block(i), at_block(j)] = block
                else:
                    A[at_block(j), at_block(i)] = jnp.transpose(block)
        for i in range(4):
            own, turned, diagonal = self.on_diagonal(self.inst, i)
            whole = jnp.where(self.ri < self.ci, own, jnp.where(self.ri > self.ci, turned, diagonal))
            A[at_block(i), at_block(i)] = whole - self.down[i] * self.avg[i]

    def lagged_cov(self, S):
        zero = jnp.zeros((128, 128), jnp.float32)
        S[at_block(0), at_block(1)] = zero
        S[at_block(2), at_block(3)] = zero
        for k, pair in enumerate(BLOCKS):
            for c, (i, j) in enumerate(pair):
                S[at_block(j), at_block(i)] = self.lag[c, at_block(k)] * self.inv - self.down[j] * self.avg[i]
        for i in range(4):
            outer = self.down[i] * self.avg[i]
            own, _, diagonal = self.on_diagonal(self.lag, i)
            S[at_block(i), at_block(i)] = jnp.where(
                self.ri > self.ci, own - outer, jnp.where(self.ri == self.ci, 0.5 * (diagonal - outer), 0.0)
            )


def whiten(A, avg, lhs, white_ref):
    a = [A[0:256, 0:256], A[256:512, 0:256], A[256:512, 256:512]]
    am = [jnp.concatenate([t[m] for t in [split3(q) for q in avg]], axis=1) for m in range(3)]
    lhs[256:272, :] = jnp.concatenate(am + [jnp.zeros((13, 512), jnp.bfloat16)], axis=0)
    y = [None, None]
    for t in split3(a[0]):
        v = dot(lhs[:, 0:256], t, LANES, None)
        y[0] = v if y[0] is None else y[0] + v
    for t, u in zip(split3(a[1]), split3(a[2])):
        v = dot(lhs[:, 0:256], t, LANES, None) + dot(lhs[:, 256:512], u, LANES, None)
        y[1] = v if y[1] is None else y[1] + v
    for h in range(2):
        m = y[h][256:257] + y[h][257:258] + y[h][258:259]
        white_ref[:, 256*h:256*h+256] = (y[h][0:256] - m).astype(jnp.bfloat16)


def whiten_lagged(A, S, koop_ref, written):
    a = [A[0:256, 0:256], A[256:512, 0:256], A[256:512, 256:512]]
    s = [S[0:256, 0:256], S[256:512, 0:256], S[256:512, 256:512]]
    nn = ROWS; nt = LANES
    t00 = dot(a[0], s[0], nn)
    t10 = dot(a[1], s[0], nn) + dot(a[2], s[1], nn)
    t11 = dot(a[2], s[2], nn)
    k00 = dot(t00, a[0], nt)
    k01 = dot(t00, a[1], nt)
    k10 = dot(t10, a[0], nt)
    k11 = dot(t10, a[1], nt) + dot(t11, a[2], nt)
    k10 = k10 + jnp.transpose(k01)
    koop_ref[0:256, 0:256] = k00 + jnp.transpose(k00)
    koop_ref[0:256, 256:512] = jnp.transpose(k10)
    written(0)
    koop_ref[256:512, 0:256] = k10
    koop_ref[256:512, 256:512] = k11 + jnp.transpose(k11)
    written(1)


def on_device(codes, row_scale, valid):
    projected, koopman = tica(codes[0], row_scale, valid)
    return (projected[None], koopman)


def solution(mesh):
    return jax.shard_map(
        on_device,
        mesh=mesh,
        in_specs=(P("traj", "blk", None), P("traj", "blk"), P("traj")),
        out_specs=(P("traj", "blk", None), P()),
        check_vma=False,
    )
```

```python
import jax
import jax.numpy as jnp
from jax import lax
from jax.experimental import pallas as pl
from jax.experimental.pallas import tpu as pltpu
from jax.sharding import PartitionSpec as P

MESH = pl.DeviceIdType.MESH
LAG = 64
HALF = 544
PARTS = (
    (0, 96, "x", (("ar", "y"), ("ar", "z"))),
    (96, 192, "y", (("ar", "z"), ("ar", "x"))),
    (288, 256, "z", (("ar", "x"), ("ar", "y"))),
)
SIZE = {"x": 4, "y": 8, "z": 8}
FAR = {4: (2, 1, 3), 8: (4, 3, 5, 2, 6, 1, 7)}
UPPER = (((0, 1), (2, 1)), ((0, 2), (2, 3)), ((0, 3), (3, 1)))
BLOCKS = (((0, 1), (1, 2)), ((0, 2), (1, 3)), ((0, 3), (2, 3)))


def all_steps(part):
    return (("rs", part[2]),) + part[3] + (("ag", part[2]),)


class Record:
    pass


class Place:
    def __init__(self):
        self.traj, self.blk = lax.axis_index("traj"), lax.axis_index("blk")
        self.core = lax.rem(self.blk, 2)
        self.chip = lax.div(self.blk, 2)
        self.at = {"x": lax.rem(self.chip, 4), "y": self.traj, "z": lax.div(self.blk, 8)}
        self.partner = (self.traj, self.blk + 1 - 2 * self.core)

    def device(self, axis, index):
        if axis == "x":
            return (self.traj, self.at["z"] * 8 + index * 2 + self.core)
        if axis == "y":
            return (index, self.blk)
        return (self.traj, index * 8 + self.at["x"] * 2 + self.core)


def remote(src, dst, send, recv, to):
    return pltpu.make_async_remote_copy(
        src_ref=src, dst_ref=dst, send_sem=send, recv_sem=recv, device_id=to, device_id_type=MESH
    )


class Stream:
    def __init__(self, place, acc, out, bufs, sums, send, recv, core_send, core_recv):
        self.place, self.acc, self.out = place, acc, out
        self.send, self.recv = send, recv
        self.core_send, self.core_recv = core_send, core_recv
        self.waiting, self.last, self.runs = [], [], []
        sem_at = buf_at = 0
        for part in PARTS:
            run = Record()
            run.base, run.rows = part[0], part[1]
            run.steps = []
            for kind, axis in all_steps(part):
                step = Record()
                step.kind, step.axis, step.sem = kind, axis, sem_at
                sem_at += SIZE[axis]
                if kind != "ag":
                    step.buf, step.sum = bufs[buf_at], sums[buf_at]
                    buf_at += 1
                run.steps.append(step)
            self.runs.append(run)
        self.n_steps = max(len(run.steps) for run in self.runs)

    def start(self):
        for run in self.runs:
            run.now, run.now_at, run.now_rows = self.acc, run.base, run.rows
            run.home = run.base
        for run in self.runs[::-1]:
            self.begin(run, 0)

    def advance(self, n):
        for k, run in enumerate(self.runs):
            if n < len(run.steps):
                self.finish(run, n)
                if n + 1 < len(run.steps):
                    self.begin(run, n + 1)
                else:
                    rows = self.out.at[self.place.core, pl.ds(run.base, run.rows)]
                    c = remote(rows, rows, self.core_send.at[k], self.core_recv.at[k], self.place.partner)
                    c.start()
                    self.last.append(c)

    def arrive(self):
        for c in self.last:
            c.wait_recv()

    def close(self):
        for c in self.waiting + self.last:
            c.wait_send()

    def begin(self, run, n):
        step = run.steps[n]
        axis, size = step.axis, SIZE[step.axis]
        me = self.place.at[axis]
        step.copies = {}
        for d in FAR[size]:
            to = lax.rem(me + d, size)
            if step.kind == "rs":
                rows = run.now_rows // size
                src = run.now.at[pl.ds(pl.multiple_of(run.now_at + to * rows, 8), rows)]
                dst, slot = step.buf.at[d - 1], d
            elif step.kind == "ar":
                src = run.now.at[pl.ds(run.now_at, run.now_rows)]
                dst, slot = step.buf.at[me], me
            else:
                src = dst = self.out.at[self.place.core, pl.ds(run.home, run.now_rows)]
                slot = d
            step.copies[d] = remote(
                src, dst, self.send.at[step.sem + d], self.recv.at[step.sem + slot], self.place.device(axis, to)
            )
            step.copies[d].start()
        if step.kind == "ar":
            step.buf[me] = run.now[pl.ds(run.now_at, run.now_rows)]
        self.waiting.extend(step.copies.values())

    def finish(self, run, n):
        step = run.steps[n]
        axis, size = step.axis, SIZE[step.axis]
        me = self.place.at[axis]
        near = FAR[size][::-1]
        if step.kind == "rs":
            rows = run.now_rows // size
            total = run.now[pl.ds(pl.multiple_of(run.now_at + me * rows, 8), rows)]
            for d in near:
                step.copies[d].wait_recv()
                total = total + step.buf[d - 1]
            step.sum[...] = total
            run.now, run.now_at, run.now_rows = step.sum, 0, rows
            run.home = run.home + me * rows
        elif step.kind == "ar":
            for d in near:
                come = lax.rem(me + d, size)
                remote(
                    run.now.at[pl.ds(run.now_at, run.now_rows)],
                    step.buf.at[come],
                    self.send.at[step.sem + d],
                    self.recv.at[step.sem + come],
                    self.place.device(axis, come),
                ).wait_recv()
            total = step.buf[0]
            for j in range(1, size):
                total = total + step.buf[j]
            step.sum[...] = total
            run.now, run.now_at = step.sum, 0
        else:
            for d in near:
                step.copies[d].wait_recv()
            run.home = run.home - me * run.now_rows
            run.now_rows = run.now_rows * size
        if n + 1 < len(run.steps) and run.steps[n + 1].kind == "ag":
            run.home = pl.multiple_of(run.home, 8)
            if step.kind != "ag":
                self.out[self.place.core, pl.ds(run.home, run.now_rows)] = run.now[...]


def tica_kernel(
    codes_in, scale_in, valid_ref, white_out, koop_out, A, S, white, koop, out_sem, codes_ref, scale_ref, load_sem, lhs, frames, turned, weighted, trailing, acc, summed, *rest
):
    (frame_send, frame_recv), rest = rest[:2], rest[2:]
    n = sum(kind != "ag" for part in PARTS for kind, _ in all_steps(part))
    loads = [
        pltpu.make_async_copy(scale_in, scale_ref, load_sem.at[0]),
        pltpu.make_async_copy(codes_in, codes_ref, load_sem.at[1]),
    ]
    for load in loads:
        load.start()
    place = Place()
    core = place.core
    streams = []
    for s, out in enumerate((summed.at[0], summed.at[1])):
        bufs, sums, sems = rest[:n], rest[n : 2 * n], rest[2 * n : 2 * n + 4]
        rest = rest[2 * n + 4 :]
        streams.append(Stream(place, acc.at[s], out, bufs, sums, *sems))
    instant, lagged = streams

    chips = 32
    before = lax.rem(place.chip + chips - 1, chips)
    after = lax.rem(place.chip + 1, chips)
    barrier = pltpu.get_barrier_semaphore()
    greeted = [place.partner, (place.traj, after * 2)]
    for axis, size in SIZE.items():
        greeted += [place.device(axis, lax.rem(place.at[axis] + d, size)) for d in range(1, size)]
    for device in greeted:
        pl.semaphore_signal(barrier, inc=1, device_id=device, device_id_type=MESH)

    rows_of = lax.broadcasted_iota(jnp.int32, (128, 128), 0)
    lanes_of = lax.broadcasted_iota(jnp.int32, (128, 128), 1)
    bf16, f32 = jnp.bfloat16, jnp.float32
    mine = pl.multiple_of(core * 256, 256)
    for load in loads:
        load.wait()
    for i in range(2):
        scale = jnp.transpose(jnp.broadcast_to(scale_ref[:, 128 * i : 128 * i + 128], (128, 128)))
        at = pl.ds(pl.multiple_of(mine + 128 * i, 128), 128)
        for p in range(4):
            codes = codes_ref[128 * i : 128 * i + 128, 128 * p : 128 * p + 128]
            x = (codes.astype(f32) * scale).astype(bf16)
            frames[p, at, :] = x
            lhs[128 * i : 128 * i + 128, 128 * p : 128 * p + 128] = x

    pl.semaphore_wait(barrier, len(greeted) - 1 + 2 * (1 - core))
    own = frames.at[:, pl.ds(mine, 256), :]
    swap = remote(own, own, frame_send.at[0], frame_recv.at[0], place.partner)
    swap.start()
    first, halo = frames.at[:, pl.ds(0, LAG), :], frames.at[:, pl.ds(512, LAG), :]
    heads = [
        remote(first, halo, frame_send.at[1 + c], frame_recv.at[1], (place.traj, before * 2 + c)) for c in range(2)
    ]

    @pl.when(core == 0)
    def _():
        for c in heads:
            c.start()

    start = place.chip * 512
    valid = valid_ref[0]

    def rows_at(block):
        return pl.ds(pl.multiple_of(block * 128, 128), 128)

    def turn(block, panels):
        for p in panels:
            turned[p, block] = jnp.transpose(frames[p, rows_at(block), :].astype(f32)).astype(bf16)

    def prepare(block):
        t = rows_of + (start + block * 128)
        weight = jnp.where(t + LAG < valid, 1.0, 0.0) + jnp.where((t >= LAG) & (t < valid), 1.0, 0.0)
        for p in range(4):
            weighted[p, rows_at(block), :] = (frames[p, rows_at(block), :].astype(f32) * weight).astype(bf16)
        turn(block, (2 * core, 2 * core + 1))

    def product(a, *rights):
        left = jnp.concatenate([turned[a, i] for i in range(4)], axis=1)
        full = dot(left, jnp.concatenate([right[...] for right in rights], axis=1), ROWS, None)
        return [full[:, at_block(k)] for k in range(len(rights))]

    prepare(2 * core)
    prepare(2 * core + 1)
    swap.wait_recv()
    prepare(2 - 2 * core)
    prepare(3 - 2 * core)

    row8 = lax.broadcasted_iota(jnp.int32, (8, 128), 0)
    first_core = core == 0
    upper = product(2 * core, *[weighted.at[p] for p in range(4)])
    lower = product(2 * core + 1, weighted.at[1], weighted.at[3])
    acc[0, at_block(0)] = upper[1]
    acc[0, at_block(1)] = jnp.where(first_core, upper[2], upper[3])
    acc[0, at_block(2)] = jnp.where(first_core, upper[3], lower[0])
    on = [jnp.where(first_core, upper[0], upper[2]), jnp.where(first_core, lower[0], lower[1])]
    acc[0, 384:512] = jnp.where(rows_of <= lanes_of, on[0], on[1])
    diagonal = jnp.sum(jnp.where(rows_of == lanes_of, on[1], 0.0), axis=0, keepdims=True)
    ones = jnp.ones((16, 512), bf16)
    totals = jnp.concatenate(
        [jnp.zeros((4, 128), f32)] + [dot(ones, weighted[p], ROWS, None)[:1] for p in range(4)], axis=0
    )
    count = jnp.clip(valid - LAG - start, 0, 512).astype(f32) * 2.0
    extra = jnp.where(core == 0, totals, jnp.full((8, 128), count))
    acc[0, 512:520] = jnp.where(row8 == 0, diagonal, extra)
    acc[0, 520:HALF] = jnp.zeros((HALF - 520, 128), f32)
    instant.start()

    remote(first, halo, frame_send.at[1], frame_recv.at[1], (place.traj, after * 2)).wait_recv()
    for block in range(4):
        t = rows_of + (start + block * 128)
        for p in range(4):
            x = frames[p, 128 * block + LAG : 128 * block + LAG + 128, :].astype(f32)
            trailing[p, 128 * block : 128 * block + 128, :] = jnp.where(t + LAG < valid, x, 0.0).astype(bf16)
    for block in range(4):
        turn(block, (2 - 2 * core, 3 - 2 * core))
    full = [product(a, *[trailing.at[b] for b in range(4)]) for a in range(4)]
    for k in range(3):
        pair = [full[b][a] + jnp.transpose(full[a][b]) for a, b in BLOCKS[k]]
        acc[1, at_block(k)] = jnp.where(first_core, *pair)
    on = [jnp.where(first_core, full[i][i], full[i + 2][i + 2]) for i in range(2)]
    on = [x + jnp.transpose(x) for x in on]
    acc[1, 384:512] = jnp.where(rows_of >= lanes_of, on[0], on[1])
    diagonal = jnp.sum(jnp.where(rows_of == lanes_of, on[1], 0.0), axis=0, keepdims=True)
    acc[1, 512:520] = jnp.where(row8 == 0, diagonal, 0.0)
    acc[1, 520:HALF] = jnp.zeros((HALF - 520, 128), f32)

    instant.advance(0)
    lagged.start()
    instant.advance(1)
    instant.advance(2)
    lagged.advance(0)
    instant.advance(3)
    lagged.advance(1)
    instant.arrive()
    means = Means(summed.at[0], summed.at[1])
    means.instant_cov(A)
    D = A[at_block(0), at_block(0)]
    D = eliminate(A, 0, D)
    D = eliminate(A, 1, D, lambda: lagged.advance(2))
    D = eliminate(A, 2, D)
    eliminate(A, 3, D, lambda: lagged.advance(3))
    A[at_block(0), at_block(1)] = jnp.zeros((128, 128), f32)
    A[at_block(2), at_block(3)] = jnp.zeros((128, 128), f32)
    whiten(A, means.avg, lhs, white)
    out_white = pltpu.make_async_copy(white, white_out, out_sem.at[0])
    out_white.start()
    lagged.arrive()
    means.lagged_cov(S)
    out_koop = []

    def written(i):
        half = pl.ds(256 * i, 256)
        out_koop.append(pltpu.make_async_copy(koop.at[half], koop_out.at[half], out_sem.at[1 + i]))
        out_koop[-1].start()

    whiten_lagged(A, S, koop, written)
    instant.close()
    lagged.close()
    swap.wait_send()
    out_white.wait()
    for c in out_koop:
        c.wait()

    @pl.when(core == 0)
    def _():
        for c in heads:
            c.wait_send()


def sum_scratch():
    bufs, sums, sems = [], [], 0
    for part in PARTS:
        rows = part[1]
        for kind, axis in all_steps(part):
            size = SIZE[axis]
            sems += size
            if kind == "rs":
                rows //= size
                bufs.append(pltpu.VMEM((size - 1, rows, 128), jnp.float32))
                sums.append(pltpu.VMEM((rows, 128), jnp.float32))
            elif kind == "ar":
                bufs.append(pltpu.VMEM((size, rows, 128), jnp.float32))
                sums.append(pltpu.VMEM((rows, 128), jnp.float32))
    return [
        *bufs,
        *sums,
        pltpu.SemaphoreType.DMA((sems,)),
        pltpu.SemaphoreType.DMA((sems,)),
        pltpu.SemaphoreType.DMA((len(PARTS),)),
        pltpu.SemaphoreType.DMA((len(PARTS),)),
    ]


def tica(codes, row_scale, valid):
    hbm = pl.BlockSpec(memory_space=pltpu.HBM)
    square = jax.ShapeDtypeStruct((codes.shape[1], codes.shape[1]), jnp.float32)
    return pl.pallas_call(
        tica_kernel,
        out_shape=(jax.ShapeDtypeStruct(codes.shape, codes.dtype), square),
        in_specs=[hbm, hbm, pl.BlockSpec(memory_space=pltpu.SMEM)],
        out_specs=(hbm, hbm),
        scratch_shapes=[
            pltpu.VMEM(square.shape, square.dtype),
            pltpu.VMEM(square.shape, square.dtype),
            pltpu.VMEM(codes.shape, codes.dtype),
            pltpu.VMEM(square.shape, square.dtype),
            pltpu.SemaphoreType.DMA((3,)),
            pltpu.VMEM(codes.shape, codes.dtype),
            pltpu.VMEM(row_scale.shape, row_scale.dtype),
            pltpu.SemaphoreType.DMA((2,)),
            pltpu.VMEM((codes.shape[0] + 16, codes.shape[1]), jnp.bfloat16),
            pltpu.VMEM((4, 512 + LAG, 128), jnp.bfloat16),
            pltpu.VMEM((4, 4, 128, 128), jnp.bfloat16),
            pltpu.VMEM((4, 512, 128), jnp.bfloat16),
            pltpu.VMEM((4, 512, 128), jnp.bfloat16),
            pltpu.VMEM((2, HALF, 128), jnp.float32),
            pltpu.VMEM((2, 2, HALF, 128), jnp.float32),
            pltpu.SemaphoreType.DMA((3,)),
            pltpu.SemaphoreType.DMA((2,)),
            *sum_scratch(),
            *sum_scratch(),
        ],
        compiler_params=pltpu.CompilerParams(
            collective_id=0, has_side_effects=True, vmem_limit_bytes=58 * 2**20
        ),
        name="tica",
    )(codes, row_scale, valid)


HIGHEST = lax.Precision.HIGHEST
ROWS = (((1,), (0,)), ((), ()))
LANES = (((1,), (1,)), ((), ()))
SUBLANES = (((0,), (0,)), ((), ()))


def dot(left, right, dims, precision=HIGHEST):
    return lax.dot_general(left, right, dims, precision=precision, preferred_element_type=jnp.float32)


def one_row(x, k):
    return jnp.broadcast_to(x[k : k + 1, :], (8, 128))


def one_lane(x, k):
    return jnp.broadcast_to(x[:, k : k + 1], (8, 128))


def inverse_factor(block, halfway=None):
    rows = list(block)
    n, size = len(rows), 8
    sub = lax.broadcasted_iota(jnp.int32, (8, 128), 0)
    lane = lax.broadcasted_iota(jnp.int32, (8, 128), 1)
    even = (sub % 2) == 0
    for group in range(0, n, size):
        end = group + size
        coming = [one_lane(rows[group], 8 * group + k) for k in range(8)]
        pivots = []
        for r in range(group, end):
            first = 8 * r
            last = r == end - 1
            columns = [[coming[k]] + [one_lane(rows[q], first + k) for q in range(r + 1, end)] for k in range(8)]
            if not last:
                coming = [one_lane(rows[r + 1], first + 8 + k) for k in range(8)]
            inside = (lane >= first) & (lane < first + 8)
            panel = jnp.where(inside, jnp.where(lane - first == sub, 1.0, 0.0), rows[r])
            for q in range(r + 1, end):
                rows[q] = jnp.where(inside, 0.0, rows[q])
            for k in range(0, 8, 2):
                left, right = columns[k], columns[k + 1]
                a, b, d = one_row(left[0], k), one_row(left[0], k + 1), one_row(right[0], k + 1)
                det = a * d - b * b
                rough = pl.reciprocal(det, approx=True)
                mend = 2.0 - det * rough
                inv = rough * mend
                a_inv, b_inv, d_inv = a * inv, b * inv, d * inv
                low, high = jnp.where(sub > k + 1, left[0], 0.0), jnp.where(sub > k + 1, right[0], 0.0)
                g, h = low * d - high * b, high * a - low * b
                f0 = [g * inv] + [x * d_inv - y * b_inv for x, y in zip(left[1:], right[1:])]
                f1 = [h * inv] + [y * a_inv - x * b_inv for x, y in zip(left[1:], right[1:])]
                for m in range(k + 2, 8):
                    e0, e1 = one_row(left[0], m), one_row(right[0], m)
                    columns[m] = [columns[m][0] - ((g * e0 + h * e1) * rough) * mend] + [
                        x - (u * e0 + v * e1) for x, u, v in zip(columns[m][1:], f0[1:], f1[1:])
                    ]
                if not last:
                    coming = [
                        coming[m] - (f0[1] * one_row(left[1], m) + f1[1] * one_row(right[1], m)) for m in range(8)
                    ]
                row0, row1 = one_row(panel, k), one_row(panel, k + 1)
                panel = panel - (f0[0] * row0 + f1[0] * row1)
                for q in range(r + 1, end):
                    rows[q] = rows[q] - (f0[q - r] * row0 + f1[q - r] * row1)
                if k == 0:
                    pivot = (a, b, det)
                else:
                    pivot = tuple(jnp.where(sub >= k, x, y) for x, y in zip((a, b, det), pivot))
            rows[r] = panel
            pivots.append(pivot)
        for r in range(group, end):
            a, b, det = pivots[r - group]
            above = pltpu.roll(rows[r], 1, 0)
            rows[r] = jnp.where(even, rows[r], rows[r] * a - above * b) * lax.rsqrt(jnp.where(even, a, a * det))
        if end < n:
            done = jnp.concatenate(rows[group:end], axis=0)
            down = lax.broadcasted_iota(jnp.int32, done.shape, 0) + 8 * group
            along = lax.broadcasted_iota(jnp.int32, done.shape, 1)
            change = dot(done, jnp.where((along > down) & (along < 8 * end), 0.0, done), SUBLANES)
            inside = (lane >= 8 * group) & (lane < 8 * end)
            for q in range(end, n):
                rows[q] = jnp.where(inside, 0.0, rows[q]) - change[8 * q : 8 * q + 8]
            if halfway is not None:
                halfway()
    return [jnp.where(lane <= sub + 8 * q, rows[q], 0.0) for q in range(n)]


def split3(x):
    high = x.astype(jnp.bfloat16)
    rest = x - high.astype(jnp.float32)
    middle = rest.astype(jnp.bfloat16)
    return high, middle, (rest - middle.astype(jnp.float32)).astype(jnp.bfloat16)


def at_block(i):
    return slice(128 * i, 128 * i + 128)


def eliminate(A, k, D, halfway=None):
    W = jnp.concatenate(inverse_factor([D[8 * q : 8 * q + 8, :] for q in range(16)], halfway), axis=0)
    A[at_block(k), at_block(k)] = W
    if k < 3:
        near = dot(W, A[at_block(k), at_block(k + 1)], ROWS)
        D = A[at_block(k + 1), at_block(k + 1)] - dot(near, near, SUBLANES)
        A[at_block(k), at_block(k + 1)] = near
    for lo, hi in ((0, 128 * k), (128 * (k + 2), 512)):
        if lo < hi:
            A[at_block(k), lo:hi] = dot(W, A[at_block(k), lo:hi], ROWS)
    if k < 3:
        below = 128 * (k + 1)
        change = dot(A[at_block(k), below:], A[at_block(k), :], SUBLANES)
        A[below:, at_block(k)] = -change[:, at_block(k)]
        if k > 0:
            A[below:, 0 : 128 * k] = A[below:, 0 : 128 * k] - change[:, 0 : 128 * k]
        if k < 2:
            A[below:, below + 128 :] = A[below:, below + 128 :] - change[:, below + 128 :]
    return D


class Means:
    def __init__(self, inst_ref, lag_ref):
        self.inst, self.lag = inst_ref, lag_ref
        self.inv = 1.0 / inst_ref[1, 516:517, :]
        self.avg = [inst_ref[0, 516 + j : 517 + j, :] * self.inv for j in range(4)]
        self.down = [jnp.transpose(jnp.broadcast_to(a, (128, 128))) for a in self.avg]
        self.ri = lax.broadcasted_iota(jnp.int32, (128, 128), 0)
        self.ci = lax.broadcasted_iota(jnp.int32, (128, 128), 1)

    def on_diagonal(self, ref, i):
        stored = ref[i // 2, 384:512] * self.inv
        turned = jnp.transpose(stored)
        if i % 2 == 0:
            return stored, turned, stored
        return turned, stored, ref[i // 2, 512:513] * self.inv

    def instant_cov(self, A):
        for k, pair in enumerate(UPPER):
            for c, (i, j) in enumerate(pair):
                block = self.inst[c, at_block(k)] * self.inv - self.down[i] * self.avg[j]
                if i < j:
                    A[at_block(i), at_block(j)] = block
                else:
                    A[at_block(j), at_block(i)] = jnp.transpose(block)
        for i in range(4):
            own, turned, diagonal = self.on_diagonal(self.inst, i)
            whole = jnp.where(self.ri < self.ci, own, jnp.where(self.ri > self.ci, turned, diagonal))
            A[at_block(i), at_block(i)] = whole - self.down[i] * self.avg[i]

    def lagged_cov(self, S):
        zero = jnp.zeros((128, 128), jnp.float32)
        S[at_block(0), at_block(1)] = zero
        S[at_block(2), at_block(3)] = zero
        for k, pair in enumerate(BLOCKS):
            for c, (i, j) in enumerate(pair):
                S[at_block(j), at_block(i)] = self.lag[c, at_block(k)] * self.inv - self.down[j] * self.avg[i]
        for i in range(4):
            outer = self.down[i] * self.avg[i]
            own, _, diagonal = self.on_diagonal(self.lag, i)
            S[at_block(i), at_block(i)] = jnp.where(
                self.ri > self.ci, own - outer, jnp.where(self.ri == self.ci, 0.5 * (diagonal - outer), 0.0)
            )


def whiten(A, avg, lhs, white_ref):
    a = [A[0:256, 0:256], A[256:512, 0:256], A[256:512, 256:512]]
    am = [jnp.concatenate([t[m] for t in [split3(q) for q in avg]], axis=1) for m in range(3)]
    lhs[256:272, :] = jnp.concatenate(am + [jnp.zeros((13, 512), jnp.bfloat16)], axis=0)
    y = [None, None]
    for t in split3(a[0]):
        v = dot(lhs[:, 0:256], t, LANES, None)
        y[0] = v if y[0] is None else y[0] + v
    for t, u in zip(split3(a[1]), split3(a[2])):
        v = dot(lhs[:, 0:256], t, LANES, None) + dot(lhs[:, 256:512], u, LANES, None)
        y[1] = v if y[1] is None else y[1] + v
    for h in range(2):
        m = y[h][256:257] + y[h][257:258] + y[h][258:259]
        white_ref[:, 256*h:256*h+256] = (y[h][0:256] - m).astype(jnp.bfloat16)


def whiten_lagged(A, S, koop_ref, written):
    a = [A[0:256, 0:256], A[256:512, 0:256], A[256:512, 256:512]]
    s = [S[0:256, 0:256], S[256:512, 0:256], S[256:512, 256:512]]
    nn = ROWS; nt = LANES
    t00 = dot(a[0], s[0], nn)
    t10 = dot(a[1], s[0], nn) + dot(a[2], s[1], nn)
    t11 = dot(a[2], s[2], nn)
    k00 = dot(t00, a[0], nt)
    k01 = dot(t00, a[1], nt)
    k10 = dot(t10, a[0], nt)
    k11 = dot(t10, a[1], nt) + dot(t11, a[2], nt)
    k10 = k10 + jnp.transpose(k01)
    koop_ref[0:256, 0:256] = k00 + jnp.transpose(k00)
    koop_ref[0:256, 256:512] = jnp.transpose(k10)
    written(0)
    koop_ref[256:512, 0:256] = k10
    koop_ref[256:512, 256:512] = k11 + jnp.transpose(k11)
    written(1)


def hand_on_kernel(white_in, koop_in, white_out, koop_out, sems):
    copies = []
    for source, target, pieces in ((koop_in, koop_out, 4), (white_in, white_out, 2)):
        for i in range(pieces):
            rows = pl.ds(128 * i, 128)
            copies.append(pltpu.make_async_copy(source.at[rows], target.at[rows], sems.at[len(copies)]))
            copies[-1].start()
    for c in copies:
        c.wait()


def hand_on(whitened, koopman):
    hbm = pl.BlockSpec(memory_space=pltpu.HBM)
    return pl.pallas_call(
        hand_on_kernel,
        out_shape=tuple(jax.ShapeDtypeStruct(x.shape, x.dtype) for x in (whitened, koopman)),
        in_specs=[hbm, hbm],
        out_specs=(hbm, hbm),
        scratch_shapes=[pltpu.SemaphoreType.DMA((6,))],
        compiler_params=pltpu.CompilerParams(vmem_limit_bytes=58 * 2**20),
        name="hand_on",
    )(whitened, koopman)


def on_device(codes, row_scale, valid):
    projected, koopman = hand_on(*tica(codes[0], row_scale, valid))
    return (projected[None], koopman)


def solution(mesh):
    return jax.shard_map(
        on_device,
        mesh=mesh,
        in_specs=(P("traj", "blk", None), P("traj", "blk"), P("traj")),
        out_specs=(P("traj", "blk", None), P()),
        check_vma=False,
    )
```

```python
import jax
import jax.numpy as jnp
from jax import lax
from jax.experimental import pallas as pl
from jax.experimental.pallas import tpu as pltpu
from jax.sharding import PartitionSpec as P

MESH = pl.DeviceIdType.MESH
LAG = 64
HALF = 544
PARTS = (
    (0, 96, "x", (("ar", "y"), ("ar", "z"))),
    (96, 192, "y", (("ar", "z"), ("ar", "x"))),
    (288, 256, "z", (("ar", "x"), ("ar", "y"))),
)
SIZE = {"x": 4, "y": 8, "z": 8}
FAR = {4: (2, 1, 3), 8: (4, 3, 5, 2, 6, 1, 7)}
UPPER = (((0, 1), (2, 1)), ((0, 2), (2, 3)), ((0, 3), (3, 1)))
BLOCKS = (((0, 1), (1, 2)), ((0, 2), (1, 3)), ((0, 3), (2, 3)))


def all_steps(part):
    return (("rs", part[2]),) + part[3] + (("ag", part[2]),)


class Record:
    pass


class Place:
    def __init__(self):
        self.traj, self.blk = lax.axis_index("traj"), lax.axis_index("blk")
        self.core = lax.rem(self.blk, 2)
        self.chip = lax.div(self.blk, 2)
        self.at = {"x": lax.rem(self.chip, 4), "y": self.traj, "z": lax.div(self.blk, 8)}
        self.partner = (self.traj, self.blk + 1 - 2 * self.core)

    def device(self, axis, index):
        if axis == "x":
            return (self.traj, self.at["z"] * 8 + index * 2 + self.core)
        if axis == "y":
            return (index, self.blk)
        return (self.traj, index * 8 + self.at["x"] * 2 + self.core)


def remote(src, dst, send, recv, to):
    return pltpu.make_async_remote_copy(
        src_ref=src, dst_ref=dst, send_sem=send, recv_sem=recv, device_id=to, device_id_type=MESH
    )


class Stream:
    def __init__(self, place, acc, out, bufs, sums, send, recv, core_send, core_recv):
        self.place, self.acc, self.out = place, acc, out
        self.send, self.recv = send, recv
        self.core_send, self.core_recv = core_send, core_recv
        self.waiting, self.last, self.runs = [], [], []
        sem_at = buf_at = 0
        for part in PARTS:
            run = Record()
            run.base, run.rows = part[0], part[1]
            run.steps = []
            for kind, axis in all_steps(part):
                step = Record()
                step.kind, step.axis, step.sem = kind, axis, sem_at
                sem_at += SIZE[axis]
                if kind != "ag":
                    step.buf, step.sum = bufs[buf_at], sums[buf_at]
                    buf_at += 1
                run.steps.append(step)
            self.runs.append(run)
        self.n_steps = max(len(run.steps) for run in self.runs)

    def start(self):
        for run in self.runs:
            run.now, run.now_at, run.now_rows = self.acc, run.base, run.rows
            run.home = run.base
        for run in self.runs[::-1]:
            self.begin(run, 0)

    def advance(self, n):
        for k, run in enumerate(self.runs):
            if n < len(run.steps):
                self.finish(run, n)
                if n + 1 < len(run.steps):
                    self.begin(run, n + 1)
                else:
                    rows = self.out.at[self.place.core, pl.ds(run.base, run.rows)]
                    c = remote(rows, rows, self.core_send.at[k], self.core_recv.at[k], self.place.partner)
                    c.start()
                    self.last.append(c)

    def arrive(self):
        for c in self.last:
            c.wait_recv()

    def close(self):
        for c in self.waiting + self.last:
            c.wait_send()

    def begin(self, run, n):
        step = run.steps[n]
        axis, size = step.axis, SIZE[step.axis]
        me = self.place.at[axis]
        step.copies = {}
        for d in FAR[size]:
            to = lax.rem(me + d, size)
            if step.kind == "rs":
                rows = run.now_rows // size
                src = run.now.at[pl.ds(pl.multiple_of(run.now_at + to * rows, 8), rows)]
                dst, slot = step.buf.at[d - 1], d
            elif step.kind == "ar":
                src = run.now.at[pl.ds(run.now_at, run.now_rows)]
                dst, slot = step.buf.at[me], me
            else:
                src = dst = self.out.at[self.place.core, pl.ds(run.home, run.now_rows)]
                slot = d
            step.copies[d] = remote(
                src, dst, self.send.at[step.sem + d], self.recv.at[step.sem + slot], self.place.device(axis, to)
            )
            step.copies[d].start()
        if step.kind == "ar":
            step.buf[me] = run.now[pl.ds(run.now_at, run.now_rows)]
        self.waiting.extend(step.copies.values())

    def finish(self, run, n):
        step = run.steps[n]
        axis, size = step.axis, SIZE[step.axis]
        me = self.place.at[axis]
        near = FAR[size][::-1]
        if step.kind == "rs":
            rows = run.now_rows // size
            total = run.now[pl.ds(pl.multiple_of(run.now_at + me * rows, 8), rows)]
            for d in near:
                step.copies[d].wait_recv()
                total = total + step.buf[d - 1]
            step.sum[...] = total
            run.now, run.now_at, run.now_rows = step.sum, 0, rows
            run.home = run.home + me * rows
        elif step.kind == "ar":
            for d in near:
                come = lax.rem(me + d, size)
                remote(
                    run.now.at[pl.ds(run.now_at, run.now_rows)],
                    step.buf.at[come],
                    self.send.at[step.sem + d],
                    self.recv.at[step.sem + come],
                    self.place.device(axis, come),
                ).wait_recv()
            total = step.buf[0]
            for j in range(1, size):
                total = total + step.buf[j]
            step.sum[...] = total
            run.now, run.now_at = step.sum, 0
        else:
            for d in near:
                step.copies[d].wait_recv()
            run.home = run.home - me * run.now_rows
            run.now_rows = run.now_rows * size
        if n + 1 < len(run.steps) and run.steps[n + 1].kind == "ag":
            run.home = pl.multiple_of(run.home, 8)
            if step.kind != "ag":
                self.out[self.place.core, pl.ds(run.home, run.now_rows)] = run.now[...]


def tica_kernel(
    codes_in, scale_in, valid_ref, white_out, koop_out, A, S, white, koop, out_sem, codes_ref, scale_ref, load_sem, lhs, frames, turned, weighted, trailing, acc, summed, *rest
):
    (frame_send, frame_recv), rest = rest[:2], rest[2:]
    n = sum(kind != "ag" for part in PARTS for kind, _ in all_steps(part))
    loads = [
        pltpu.make_async_copy(scale_in, scale_ref, load_sem.at[0]),
        pltpu.make_async_copy(codes_in, codes_ref, load_sem.at[1]),
    ]
    for load in loads:
        load.start()
    place = Place()
    core = place.core
    streams = []
    for s, out in enumerate((summed.at[0], summed.at[1])):
        bufs, sums, sems = rest[:n], rest[n : 2 * n], rest[2 * n : 2 * n + 4]
        rest = rest[2 * n + 4 :]
        streams.append(Stream(place, acc.at[s], out, bufs, sums, *sems))
    instant, lagged = streams

    chips = 32
    before = lax.rem(place.chip + chips - 1, chips)
    after = lax.rem(place.chip + 1, chips)
    barrier = pltpu.get_barrier_semaphore()
    greeted = [place.partner, (place.traj, after * 2)]
    for axis, size in SIZE.items():
        greeted += [place.device(axis, lax.rem(place.at[axis] + d, size)) for d in range(1, size)]
    for device in greeted:
        pl.semaphore_signal(barrier, inc=1, device_id=device, device_id_type=MESH)

    rows_of = lax.broadcasted_iota(jnp.int32, (128, 128), 0)
    lanes_of = lax.broadcasted_iota(jnp.int32, (128, 128), 1)
    bf16, f32 = jnp.bfloat16, jnp.float32
    mine = pl.multiple_of(core * 256, 256)
    for load in loads:
        load.wait()
    for i in range(2):
        scale = jnp.transpose(jnp.broadcast_to(scale_ref[:, 128 * i : 128 * i + 128], (128, 128)))
        at = pl.ds(pl.multiple_of(mine + 128 * i, 128), 128)
        for p in range(4):
            codes = codes_ref[128 * i : 128 * i + 128, 128 * p : 128 * p + 128]
            x = (codes.astype(f32) * scale).astype(bf16)
            frames[p, at, :] = x
            lhs[128 * i : 128 * i + 128, 128 * p : 128 * p + 128] = x

    pl.semaphore_wait(barrier, len(greeted) - 1 + 2 * (1 - core))
    own = frames.at[:, pl.ds(mine, 256), :]
    swap = remote(own, own, frame_send.at[0], frame_recv.at[0], place.partner)
    swap.start()
    first, halo = frames.at[:, pl.ds(0, LAG), :], frames.at[:, pl.ds(512, LAG), :]
    heads = [
        remote(first, halo, frame_send.at[1 + c], frame_recv.at[1], (place.traj, before * 2 + c)) for c in range(2)
    ]

    @pl.when(core == 0)
    def _():
        for c in heads:
            c.start()

    start = place.chip * 512
    valid = valid_ref[0]

    def rows_at(block):
        return pl.ds(pl.multiple_of(block * 128, 128), 128)

    def turn(block, panels):
        for p in panels:
            turned[p, block] = jnp.transpose(frames[p, rows_at(block), :].astype(f32)).astype(bf16)

    def prepare(block):
        t = rows_of + (start + block * 128)
        weight = jnp.where(t + LAG < valid, 1.0, 0.0) + jnp.where((t >= LAG) & (t < valid), 1.0, 0.0)
        for p in range(4):
            weighted[p, rows_at(block), :] = (frames[p, rows_at(block), :].astype(f32) * weight).astype(bf16)
        turn(block, (2 * core, 2 * core + 1))

    def product(a, *rights):
        left = jnp.concatenate([turned[a, i] for i in range(4)], axis=1)
        full = dot(left, jnp.concatenate([right[...] for right in rights], axis=1), ROWS, None)
        return [full[:, at_block(k)] for k in range(len(rights))]

    prepare(2 * core)
    prepare(2 * core + 1)
    swap.wait_recv()
    prepare(2 - 2 * core)
    prepare(3 - 2 * core)

    row8 = lax.broadcasted_iota(jnp.int32, (8, 128), 0)
    first_core = core == 0
    upper = product(2 * core, *[weighted.at[p] for p in range(4)])
    lower = product(2 * core + 1, weighted.at[1], weighted.at[3])
    acc[0, at_block(0)] = upper[1]
    acc[0, at_block(1)] = jnp.where(first_core, upper[2], upper[3])
    acc[0, at_block(2)] = jnp.where(first_core, upper[3], lower[0])
    on = [jnp.where(first_core, upper[0], upper[2]), jnp.where(first_core, lower[0], lower[1])]
    acc[0, 384:512] = jnp.where(rows_of <= lanes_of, on[0], on[1])
    diagonal = jnp.sum(jnp.where(rows_of == lanes_of, on[1], 0.0), axis=0, keepdims=True)
    ones = jnp.ones((16, 512), bf16)
    totals = jnp.concatenate(
        [jnp.zeros((4, 128), f32)] + [dot(ones, weighted[p], ROWS, None)[:1] for p in range(4)], axis=0
    )
    count = jnp.clip(valid - LAG - start, 0, 512).astype(f32) * 2.0
    extra = jnp.where(core == 0, totals, jnp.full((8, 128), count))
    acc[0, 512:520] = jnp.where(row8 == 0, diagonal, extra)
    acc[0, 520:HALF] = jnp.zeros((HALF - 520, 128), f32)
    instant.start()

    remote(first, halo, frame_send.at[1], frame_recv.at[1], (place.traj, after * 2)).wait_recv()
    for block in range(4):
        t = rows_of + (start + block * 128)
        for p in range(4):
            x = frames[p, 128 * block + LAG : 128 * block + LAG + 128, :].astype(f32)
            trailing[p, 128 * block : 128 * block + 128, :] = jnp.where(t + LAG < valid, x, 0.0).astype(bf16)
    for block in range(4):
        turn(block, (2 - 2 * core, 3 - 2 * core))
    full = [product(a, *[trailing.at[b] for b in range(4)]) for a in range(4)]
    for k in range(3):
        pair = [full[b][a] + jnp.transpose(full[a][b]) for a, b in BLOCKS[k]]
        acc[1, at_block(k)] = jnp.where(first_core, *pair)
    on = [jnp.where(first_core, full[i][i], full[i + 2][i + 2]) for i in range(2)]
    on = [x + jnp.transpose(x) for x in on]
    acc[1, 384:512] = jnp.where(rows_of >= lanes_of, on[0], on[1])
    diagonal = jnp.sum(jnp.where(rows_of == lanes_of, on[1], 0.0), axis=0, keepdims=True)
    acc[1, 512:520] = jnp.where(row8 == 0, diagonal, 0.0)
    acc[1, 520:HALF] = jnp.zeros((HALF - 520, 128), f32)

    instant.advance(0)
    lagged.start()
    instant.advance(1)
    instant.advance(2)
    lagged.advance(0)
    instant.advance(3)
    lagged.advance(1)
    instant.arrive()
    means = Means(summed.at[0], summed.at[1])
    means.instant_cov(A)
    D = A[at_block(0), at_block(0)]
    D = eliminate(A, 0, D)
    D = eliminate(A, 1, D, lambda: lagged.advance(2))
    D = eliminate(A, 2, D)
    eliminate(A, 3, D, lambda: lagged.advance(3))
    A[at_block(0), at_block(1)] = jnp.zeros((128, 128), f32)
    A[at_block(2), at_block(3)] = jnp.zeros((128, 128), f32)
    whiten(A, means.avg, lhs, white)
    out_white = pltpu.make_async_copy(white, white_out, out_sem.at[0])
    out_white.start()
    lagged.arrive()
    means.lagged_cov(S)
    out_koop = []

    def written(i):
        half = pl.ds(256 * i, 256)
        out_koop.append(pltpu.make_async_copy(koop.at[half], koop_out.at[half], out_sem.at[1 + i]))
        out_koop[-1].start()

    whiten_lagged(A, S, koop, written)
    instant.close()
    lagged.close()
    swap.wait_send()
    out_white.wait()
    for c in out_koop:
        c.wait()

    @pl.when(core == 0)
    def _():
        for c in heads:
            c.wait_send()


def sum_scratch():
    bufs, sums, sems = [], [], 0
    for part in PARTS:
        rows = part[1]
        for kind, axis in all_steps(part):
            size = SIZE[axis]
            sems += size
            if kind == "rs":
                rows //= size
                bufs.append(pltpu.VMEM((size - 1, rows, 128), jnp.float32))
                sums.append(pltpu.VMEM((rows, 128), jnp.float32))
            elif kind == "ar":
                bufs.append(pltpu.VMEM((size, rows, 128), jnp.float32))
                sums.append(pltpu.VMEM((rows, 128), jnp.float32))
    return [
        *bufs,
        *sums,
        pltpu.SemaphoreType.DMA((sems,)),
        pltpu.SemaphoreType.DMA((sems,)),
        pltpu.SemaphoreType.DMA((len(PARTS),)),
        pltpu.SemaphoreType.DMA((len(PARTS),)),
    ]


def tica(codes, row_scale, valid):
    hbm = pl.BlockSpec(memory_space=pltpu.HBM)
    square = jax.ShapeDtypeStruct((codes.shape[1], codes.shape[1]), jnp.float32)
    return pl.pallas_call(
        tica_kernel,
        out_shape=(jax.ShapeDtypeStruct(codes.shape, codes.dtype), square),
        in_specs=[hbm, hbm, pl.BlockSpec(memory_space=pltpu.SMEM)],
        out_specs=(hbm, hbm),
        scratch_shapes=[
            pltpu.VMEM(square.shape, square.dtype),
            pltpu.VMEM(square.shape, square.dtype),
            pltpu.VMEM(codes.shape, codes.dtype),
            pltpu.VMEM(square.shape, square.dtype),
            pltpu.SemaphoreType.DMA((3,)),
            pltpu.VMEM(codes.shape, codes.dtype),
            pltpu.VMEM(row_scale.shape, row_scale.dtype),
            pltpu.SemaphoreType.DMA((2,)),
            pltpu.VMEM((codes.shape[0] + 16, codes.shape[1]), jnp.bfloat16),
            pltpu.VMEM((4, 512 + LAG, 128), jnp.bfloat16),
            pltpu.VMEM((4, 4, 128, 128), jnp.bfloat16),
            pltpu.VMEM((4, 512, 128), jnp.bfloat16),
            pltpu.VMEM((4, 512, 128), jnp.bfloat16),
            pltpu.VMEM((2, HALF, 128), jnp.float32),
            pltpu.VMEM((2, 2, HALF, 128), jnp.float32),
            pltpu.SemaphoreType.DMA((3,)),
            pltpu.SemaphoreType.DMA((2,)),
            *sum_scratch(),
            *sum_scratch(),
        ],
        compiler_params=pltpu.CompilerParams(
            collective_id=0, has_side_effects=True, vmem_limit_bytes=58 * 2**20
        ),
        name="tica",
    )(codes, row_scale, valid)


HIGHEST = lax.Precision.HIGHEST
ROWS = (((1,), (0,)), ((), ()))
LANES = (((1,), (1,)), ((), ()))
SUBLANES = (((0,), (0,)), ((), ()))


def dot(left, right, dims, precision=HIGHEST):
    return lax.dot_general(left, right, dims, precision=precision, preferred_element_type=jnp.float32)


def one_row(x, k):
    return jnp.broadcast_to(x[k : k + 1, :], (8, 128))


def one_lane(x, k):
    return jnp.broadcast_to(x[:, k : k + 1], (8, 128))


def inverse_factor(block, halfway=None):
    rows = list(block)
    n, size = len(rows), 8
    sub = lax.broadcasted_iota(jnp.int32, (8, 128), 0)
    lane = lax.broadcasted_iota(jnp.int32, (8, 128), 1)
    even = (sub % 2) == 0
    for group in range(0, n, size):
        end = group + size
        coming = [one_lane(rows[group], 8 * group + k) for k in range(8)]
        pivots = []
        for r in range(group, end):
            first = 8 * r
            last = r == end - 1
            columns = [[coming[k]] + [one_lane(rows[q], first + k) for q in range(r + 1, end)] for k in range(8)]
            if not last:
                coming = [one_lane(rows[r + 1], first + 8 + k) for k in range(8)]
            inside = (lane >= first) & (lane < first + 8)
            panel = jnp.where(inside, jnp.where(lane - first == sub, 1.0, 0.0), rows[r])
            for q in range(r + 1, end):
                rows[q] = jnp.where(inside, 0.0, rows[q])
            for k in range(0, 8, 2):
                left, right = columns[k], columns[k + 1]
                a, b, d = one_row(left[0], k), one_row(left[0], k + 1), one_row(right[0], k + 1)
                det = a * d - b * b
                rough = pl.reciprocal(det, approx=True)
                mend = 2.0 - det * rough
                inv = rough * mend
                a_inv, b_inv, d_inv = a * inv, b * inv, d * inv
                low, high = jnp.where(sub > k + 1, left[0], 0.0), jnp.where(sub > k + 1, right[0], 0.0)
                g, h = low * d - high * b, high * a - low * b
                f0 = [g * inv] + [x * d_inv - y * b_inv for x, y in zip(left[1:], right[1:])]
                f1 = [h * inv] + [y * a_inv - x * b_inv for x, y in zip(left[1:], right[1:])]
                for m in range(k + 2, 8):
                    e0, e1 = one_row(left[0], m), one_row(right[0], m)
                    columns[m] = [columns[m][0] - ((g * e0 + h * e1) * rough) * mend] + [
                        x - (u * e0 + v * e1) for x, u, v in zip(columns[m][1:], f0[1:], f1[1:])
                    ]
                if not last:
                    coming = [
                        coming[m] - (f0[1] * one_row(left[1], m) + f1[1] * one_row(right[1], m)) for m in range(8)
                    ]
                row0, row1 = one_row(panel, k), one_row(panel, k + 1)
                panel = panel - (f0[0] * row0 + f1[0] * row1)
                for q in range(r + 1, end):
                    rows[q] = rows[q] - (f0[q - r] * row0 + f1[q - r] * row1)
                if k == 0:
                    pivot = (a, b, det)
                else:
                    pivot = tuple(jnp.where(sub >= k, x, y) for x, y in zip((a, b, det), pivot))
            rows[r] = panel
            pivots.append(pivot)
        for r in range(group, end):
            a, b, det = pivots[r - group]
            above = pltpu.roll(rows[r], 1, 0)
            rows[r] = jnp.where(even, rows[r], rows[r] * a - above * b) * lax.rsqrt(jnp.where(even, a, a * det))
        if end < n:
            done = jnp.concatenate(rows[group:end], axis=0)
            down = lax.broadcasted_iota(jnp.int32, done.shape, 0) + 8 * group
            along = lax.broadcasted_iota(jnp.int32, done.shape, 1)
            change = dot(done, jnp.where((along > down) & (along < 8 * end), 0.0, done), SUBLANES)
            inside = (lane >= 8 * group) & (lane < 8 * end)
            for q in range(end, n):
                rows[q] = jnp.where(inside, 0.0, rows[q]) - change[8 * q : 8 * q + 8]
            if halfway is not None:
                halfway()
    return [jnp.where(lane <= sub + 8 * q, rows[q], 0.0) for q in range(n)]


def split3(x):
    high = x.astype(jnp.bfloat16)
    rest = x - high.astype(jnp.float32)
    middle = rest.astype(jnp.bfloat16)
    return high, middle, (rest - middle.astype(jnp.float32)).astype(jnp.bfloat16)


def at_block(i):
    return slice(128 * i, 128 * i + 128)


def eliminate(A, k, D, halfway=None):
    W = jnp.concatenate(inverse_factor([D[8 * q : 8 * q + 8, :] for q in range(16)], halfway), axis=0)
    A[at_block(k), at_block(k)] = W
    if k < 3:
        near = dot(W, A[at_block(k), at_block(k + 1)], ROWS)
        D = A[at_block(k + 1), at_block(k + 1)] - dot(near, near, SUBLANES)
        A[at_block(k), at_block(k + 1)] = near
    for lo, hi in ((0, 128 * k), (128 * (k + 2), 512)):
        if lo < hi:
            A[at_block(k), lo:hi] = dot(W, A[at_block(k), lo:hi], ROWS)
    if k < 3:
        below = 128 * (k + 1)
        change = dot(A[at_block(k), below:], A[at_block(k), :], SUBLANES)
        A[below:, at_block(k)] = -change[:, at_block(k)]
        if k > 0:
            A[below:, 0 : 128 * k] = A[below:, 0 : 128 * k] - change[:, 0 : 128 * k]
        if k < 2:
            A[below:, below + 128 :] = A[below:, below + 128 :] - change[:, below + 128 :]
    return D


class Means:
    def __init__(self, inst_ref, lag_ref):
        self.inst, self.lag = inst_ref, lag_ref
        self.inv = 1.0 / inst_ref[1, 516:517, :]
        self.avg = [inst_ref[0, 516 + j : 517 + j, :] * self.inv for j in range(4)]
        self.down = [jnp.transpose(jnp.broadcast_to(a, (128, 128))) for a in self.avg]
        self.ri = lax.broadcasted_iota(jnp.int32, (128, 128), 0)
        self.ci = lax.broadcasted_iota(jnp.int32, (128, 128), 1)

    def on_diagonal(self, ref, i):
        stored = ref[i // 2, 384:512] * self.inv
        turned = jnp.transpose(stored)
        if i % 2 == 0:
            return stored, turned, stored
        return turned, stored, ref[i // 2, 512:513] * self.inv

    def instant_cov(self, A):
        for k, pair in enumerate(UPPER):
            for c, (i, j) in enumerate(pair):
                block = self.inst[c, at_block(k)] * self.inv - self.down[i] * self.avg[j]
                if i < j:
                    A[at_block(i), at_block(j)] = block
                else:
                    A[at_block(j), at_block(i)] = jnp.transpose(block)
        for i in range(4):
            own, turned, diagonal = self.on_diagonal(self.inst, i)
            whole = jnp.where(self.ri < self.ci, own, jnp.where(self.ri > self.ci, turned, diagonal))
            A[at_block(i), at_block(i)] = whole - self.down[i] * self.avg[i]

    def lagged_cov(self, S):
        zero = jnp.zeros((128, 128), jnp.float32)
        S[at_block(0), at_block(1)] = zero
        S[at_block(2), at_block(3)] = zero
        for k, pair in enumerate(BLOCKS):
            for c, (i, j) in enumerate(pair):
                S[at_block(j), at_block(i)] = self.lag[c, at_block(k)] * self.inv - self.down[j] * self.avg[i]
        for i in range(4):
            outer = self.down[i] * self.avg[i]
            own, _, diagonal = self.on_diagonal(self.lag, i)
            S[at_block(i), at_block(i)] = jnp.where(
                self.ri > self.ci, own - outer, jnp.where(self.ri == self.ci, 0.5 * (diagonal - outer), 0.0)
            )


def whiten(A, avg, lhs, white_ref):
    a = [A[0:256, 0:256], A[256:512, 0:256], A[256:512, 256:512]]
    am = [jnp.concatenate([t[m] for t in [split3(q) for q in avg]], axis=1) for m in range(3)]
    lhs[256:272, :] = jnp.concatenate(am + [jnp.zeros((13, 512), jnp.bfloat16)], axis=0)
    y = [None, None]
    for t in split3(a[0]):
        v = dot(lhs[:, 0:256], t, LANES, None)
        y[0] = v if y[0] is None else y[0] + v
    for t, u in zip(split3(a[1]), split3(a[2])):
        v = dot(lhs[:, 0:256], t, LANES, None) + dot(lhs[:, 256:512], u, LANES, None)
        y[1] = v if y[1] is None else y[1] + v
    for h in range(2):
        m = y[h][256:257] + y[h][257:258] + y[h][258:259]
        white_ref[:, 256*h:256*h+256] = (y[h][0:256] - m).astype(jnp.bfloat16)


def whiten_lagged(A, S, koop_ref, written):
    a = [A[0:256, 0:256], A[256:512, 0:256], A[256:512, 256:512]]
    s = [S[0:256, 0:256], S[256:512, 0:256], S[256:512, 256:512]]
    nn = ROWS; nt = LANES
    t00 = dot(a[0], s[0], nn)
    t10 = dot(a[1], s[0], nn) + dot(a[2], s[1], nn)
    t11 = dot(a[2], s[2], nn)
    k00 = dot(t00, a[0], nt)
    k01 = dot(t00, a[1], nt)
    k10 = dot(t10, a[0], nt)
    k11 = dot(t10, a[1], nt) + dot(t11, a[2], nt)
    k10 = k10 + jnp.transpose(k01)
    koop_ref[0:256, 0:256] = k00 + jnp.transpose(k00)
    koop_ref[0:256, 256:512] = jnp.transpose(k10)
    written(0)
    koop_ref[256:512, 0:256] = k10
    koop_ref[256:512, 256:512] = k11 + jnp.transpose(k11)
    written(1)


def hand_on_kernel(white_in, koop_in, white_out, koop_out, white, koop, sems):
    pieces = [(koop_in, koop, koop_out, i) for i in range(4)] + [(white_in, white, white_out, i) for i in range(2)]
    loads, stores = [], []
    for k, (source, held, target, i) in enumerate(pieces):
        rows = pl.ds(128 * i, 128)
        loads.append(pltpu.make_async_copy(source.at[rows], held.at[rows], sems.at[0, k]))
        stores.append(pltpu.make_async_copy(held.at[rows], target.at[rows], sems.at[1, k]))
        loads[-1].start()
    for load, store in zip(loads, stores):
        load.wait()
        store.start()
    for store in stores:
        store.wait()


def hand_on(whitened, koopman):
    hbm = pl.BlockSpec(memory_space=pltpu.HBM)
    return pl.pallas_call(
        hand_on_kernel,
        out_shape=tuple(jax.ShapeDtypeStruct(x.shape, x.dtype) for x in (whitened, koopman)),
        in_specs=[hbm, hbm],
        out_specs=(hbm, hbm),
        scratch_shapes=[
            pltpu.VMEM(whitened.shape, whitened.dtype),
            pltpu.VMEM(koopman.shape, koopman.dtype),
            pltpu.SemaphoreType.DMA((2, 6)),
        ],
        compiler_params=pltpu.CompilerParams(vmem_limit_bytes=58 * 2**20),
        name="hand_on",
    )(whitened, koopman)


def on_device(codes, row_scale, valid):
    projected, koopman = hand_on(*tica(codes[0], row_scale, valid))
    return (projected[None], koopman)


def solution(mesh):
    return jax.shard_map(
        on_device,
        mesh=mesh,
        in_specs=(P("traj", "blk", None), P("traj", "blk"), P("traj")),
        out_specs=(P("traj", "blk", None), P()),
        check_vma=False,
    )
```

```python
import jax
import jax.numpy as jnp
from jax import lax
from jax.experimental import pallas as pl
from jax.experimental.pallas import tpu as pltpu
from jax.sharding import PartitionSpec as P

MESH = pl.DeviceIdType.MESH
LAG = 64
HALF = 544
PARTS = (
    (0, 96, "x", (("ar", "y"), ("ar", "z"))),
    (96, 192, "y", (("ar", "z"), ("ar", "x"))),
    (288, 256, "z", (("ar", "x"), ("ar", "y"))),
)
SIZE = {"x": 4, "y": 8, "z": 8}
FAR = {4: (2, 1, 3), 8: (4, 3, 5, 2, 6, 1, 7)}
UPPER = (((0, 1), (2, 1)), ((0, 2), (2, 3)), ((0, 3), (3, 1)))
BLOCKS = (((0, 1), (1, 2)), ((0, 2), (1, 3)), ((0, 3), (2, 3)))


def all_steps(part):
    return (("rs", part[2]),) + part[3] + (("ag", part[2]),)


class Record:
    pass


class Place:
    def __init__(self):
        self.traj, self.blk = lax.axis_index("traj"), lax.axis_index("blk")
        self.core = lax.rem(self.blk, 2)
        self.chip = lax.div(self.blk, 2)
        self.at = {"x": lax.rem(self.chip, 4), "y": self.traj, "z": lax.div(self.blk, 8)}
        self.partner = (self.traj, self.blk + 1 - 2 * self.core)

    def device(self, axis, index):
        if axis == "x":
            return (self.traj, self.at["z"] * 8 + index * 2 + self.core)
        if axis == "y":
            return (index, self.blk)
        return (self.traj, index * 8 + self.at["x"] * 2 + self.core)


def remote(src, dst, send, recv, to):
    return pltpu.make_async_remote_copy(
        src_ref=src, dst_ref=dst, send_sem=send, recv_sem=recv, device_id=to, device_id_type=MESH
    )


class Stream:
    def __init__(self, place, acc, out, bufs, sums, send, recv, core_send, core_recv):
        self.place, self.acc, self.out = place, acc, out
        self.send, self.recv = send, recv
        self.core_send, self.core_recv = core_send, core_recv
        self.waiting, self.last, self.runs = [], {}, []
        sem_at = buf_at = 0
        for part in PARTS:
            run = Record()
            run.base, run.rows = part[0], part[1]
            run.steps = []
            for kind, axis in all_steps(part):
                step = Record()
                step.kind, step.axis, step.sem = kind, axis, sem_at
                sem_at += SIZE[axis]
                if kind != "ag":
                    step.buf, step.sum = bufs[buf_at], sums[buf_at]
                    buf_at += 1
                run.steps.append(step)
            self.runs.append(run)
        self.n_steps = max(len(run.steps) for run in self.runs)

    def start(self):
        for run in self.runs:
            run.now, run.now_at, run.now_rows = self.acc, run.base, run.rows
            run.home = run.base
        for run in self.runs[::-1]:
            self.begin(run, 0)

    def advance(self, n, parts=(0, 1, 2)):
        for k in parts:
            run = self.runs[k]
            if n < len(run.steps):
                self.finish(run, n)
                if n + 1 < len(run.steps):
                    self.begin(run, n + 1)
                else:
                    rows = self.out.at[self.place.core, pl.ds(run.base, run.rows)]
                    c = remote(rows, rows, self.core_send.at[k], self.core_recv.at[k], self.place.partner)
                    c.start()
                    self.last[k] = c

    def arrive(self, parts=(0, 1, 2)):
        for k in parts:
            self.last[k].wait_recv()

    def close(self):
        for c in self.waiting + list(self.last.values()):
            c.wait_send()

    def begin(self, run, n):
        step = run.steps[n]
        axis, size = step.axis, SIZE[step.axis]
        me = self.place.at[axis]
        step.copies = {}
        for d in FAR[size]:
            to = lax.rem(me + d, size)
            if step.kind == "rs":
                rows = run.now_rows // size
                src = run.now.at[pl.ds(pl.multiple_of(run.now_at + to * rows, 8), rows)]
                dst, slot = step.buf.at[d - 1], d
            elif step.kind == "ar":
                src = run.now.at[pl.ds(run.now_at, run.now_rows)]
                dst, slot = step.buf.at[me], me
            else:
                src = dst = self.out.at[self.place.core, pl.ds(run.home, run.now_rows)]
                slot = d
            step.copies[d] = remote(
                src, dst, self.send.at[step.sem + d], self.recv.at[step.sem + slot], self.place.device(axis, to)
            )
            step.copies[d].start()
        if step.kind == "ar":
            step.buf[me] = run.now[pl.ds(run.now_at, run.now_rows)]
        self.waiting.extend(step.copies.values())

    def finish(self, run, n):
        step = run.steps[n]
        axis, size = step.axis, SIZE[step.axis]
        me = self.place.at[axis]
        near = FAR[size][::-1]
        if step.kind == "rs":
            rows = run.now_rows // size
            total = run.now[pl.ds(pl.multiple_of(run.now_at + me * rows, 8), rows)]
            for d in near:
                step.copies[d].wait_recv()
                total = total + step.buf[d - 1]
            step.sum[...] = total
            run.now, run.now_at, run.now_rows = step.sum, 0, rows
            run.home = run.home + me * rows
        elif step.kind == "ar":
            for d in near:
                come = lax.rem(me + d, size)
                remote(
                    run.now.at[pl.ds(run.now_at, run.now_rows)],
                    step.buf.at[come],
                    self.send.at[step.sem + d],
                    self.recv.at[step.sem + come],
                    self.place.device(axis, come),
                ).wait_recv()
            total = step.buf[0]
            for j in range(1, size):
                total = total + step.buf[j]
            step.sum[...] = total
            run.now, run.now_at = step.sum, 0
        else:
            for d in near:
                step.copies[d].wait_recv()
            run.home = run.home - me * run.now_rows
            run.now_rows = run.now_rows * size
        if n + 1 < len(run.steps) and run.steps[n + 1].kind == "ag":
            run.home = pl.multiple_of(run.home, 8)
            if step.kind != "ag":
                self.out[self.place.core, pl.ds(run.home, run.now_rows)] = run.now[...]


def moments_kernel(
    codes_in, scale_in, valid_ref, A, S, white_ref, codes_ref, scale_ref, load_sem, lhs, frames, turned, weighted, trailing, acc, summed, *rest
):
    (frame_send, frame_recv), rest = rest[:2], rest[2:]
    n = sum(kind != "ag" for part in PARTS for kind, _ in all_steps(part))
    loads = [
        pltpu.make_async_copy(scale_in, scale_ref, load_sem.at[0]),
        pltpu.make_async_copy(codes_in, codes_ref, load_sem.at[1]),
    ]
    for load in loads:
        load.start()
    place = Place()
    core = place.core
    streams = []
    for s, out in enumerate((summed.at[0], summed.at[1])):
        bufs, sums, sems = rest[:n], rest[n : 2 * n], rest[2 * n : 2 * n + 4]
        rest = rest[2 * n + 4 :]
        streams.append(Stream(place, acc.at[s], out, bufs, sums, *sems))
    instant, lagged = streams

    chips = 32
    before = lax.rem(place.chip + chips - 1, chips)
    after = lax.rem(place.chip + 1, chips)
    barrier = pltpu.get_barrier_semaphore()
    greeted = [place.partner, (place.traj, after * 2)]
    for axis, size in SIZE.items():
        greeted += [place.device(axis, lax.rem(place.at[axis] + d, size)) for d in range(1, size)]
    for device in greeted:
        pl.semaphore_signal(barrier, inc=1, device_id=device, device_id_type=MESH)

    rows_of = lax.broadcasted_iota(jnp.int32, (128, 128), 0)
    lanes_of = lax.broadcasted_iota(jnp.int32, (128, 128), 1)
    bf16, f32 = jnp.bfloat16, jnp.float32
    mine = pl.multiple_of(core * 256, 256)
    for load in loads:
        load.wait()
    for i in range(2):
        scale = jnp.transpose(jnp.broadcast_to(scale_ref[:, 128 * i : 128 * i + 128], (128, 128)))
        at = pl.ds(pl.multiple_of(mine + 128 * i, 128), 128)
        for p in range(4):
            codes = codes_ref[128 * i : 128 * i + 128, 128 * p : 128 * p + 128]
            x = (codes.astype(f32) * scale).astype(bf16)
            frames[p, at, :] = x
            lhs[128 * i : 128 * i + 128, 128 * p : 128 * p + 128] = x

    pl.semaphore_wait(barrier, len(greeted) - 1 + 2 * (1 - core))
    own = frames.at[:, pl.ds(mine, 256), :]
    swap = remote(own, own, frame_send.at[0], frame_recv.at[0], place.partner)
    swap.start()
    first, halo = frames.at[:, pl.ds(0, LAG), :], frames.at[:, pl.ds(512, LAG), :]
    heads = [
        remote(first, halo, frame_send.at[1 + c], frame_recv.at[1], (place.traj, before * 2 + c)) for c in range(2)
    ]

    @pl.when(core == 0)
    def _():
        for c in heads:
            c.start()

    start = place.chip * 512
    valid = valid_ref[0]

    def rows_at(block):
        return pl.ds(pl.multiple_of(block * 128, 128), 128)

    def turn(block, panels):
        for p in panels:
            turned[p, block] = jnp.transpose(frames[p, rows_at(block), :].astype(f32)).astype(bf16)

    def prepare(block):
        t = rows_of + (start + block * 128)
        weight = jnp.where(t + LAG < valid, 1.0, 0.0) + jnp.where((t >= LAG) & (t < valid), 1.0, 0.0)
        for p in range(4):
            weighted[p, rows_at(block), :] = (frames[p, rows_at(block), :].astype(f32) * weight).astype(bf16)
        turn(block, (2 * core, 2 * core + 1))

    def product(a, *rights):
        left = jnp.concatenate([turned[a, i] for i in range(4)], axis=1)
        full = dot(left, jnp.concatenate([right[...] for right in rights], axis=1), ROWS, None)
        return [full[:, at_block(k)] for k in range(len(rights))]

    prepare(2 * core)
    prepare(2 * core + 1)
    swap.wait_recv()
    prepare(2 - 2 * core)
    prepare(3 - 2 * core)

    row8 = lax.broadcasted_iota(jnp.int32, (8, 128), 0)
    first_core = core == 0
    upper = product(2 * core, *[weighted.at[p] for p in range(4)])
    lower = product(2 * core + 1, weighted.at[1], weighted.at[3])
    acc[0, at_block(0)] = upper[1]
    acc[0, at_block(1)] = jnp.where(first_core, upper[2], upper[3])
    acc[0, at_block(2)] = jnp.where(first_core, upper[3], lower[0])
    on = [jnp.where(first_core, upper[0], upper[2]), jnp.where(first_core, lower[0], lower[1])]
    acc[0, 384:512] = jnp.where(rows_of <= lanes_of, on[0], on[1])
    diagonal = jnp.sum(jnp.where(rows_of == lanes_of, on[1], 0.0), axis=0, keepdims=True)
    ones = jnp.ones((16, 512), bf16)
    totals = jnp.concatenate(
        [jnp.zeros((4, 128), f32)] + [dot(ones, weighted[p], ROWS, None)[:1] for p in range(4)], axis=0
    )
    count = jnp.clip(valid - LAG - start, 0, 512).astype(f32) * 2.0
    extra = jnp.where(core == 0, totals, jnp.full((8, 128), count))
    acc[0, 512:520] = jnp.where(row8 == 0, diagonal, extra)
    acc[0, 520:HALF] = jnp.zeros((HALF - 520, 128), f32)
    instant.start()

    remote(first, halo, frame_send.at[1], frame_recv.at[1], (place.traj, after * 2)).wait_recv()
    for block in range(4):
        t = rows_of + (start + block * 128)
        for p in range(4):
            x = frames[p, 128 * block + LAG : 128 * block + LAG + 128, :].astype(f32)
            trailing[p, 128 * block : 128 * block + 128, :] = jnp.where(t + LAG < valid, x, 0.0).astype(bf16)
    for block in range(4):
        turn(block, (2 - 2 * core, 3 - 2 * core))
    full = [product(a, *[trailing.at[b] for b in range(4)]) for a in range(4)]
    for k in range(3):
        pair = [full[b][a] + jnp.transpose(full[a][b]) for a, b in BLOCKS[k]]
        acc[1, at_block(k)] = jnp.where(first_core, *pair)
    on = [jnp.where(first_core, full[i][i], full[i + 2][i + 2]) for i in range(2)]
    on = [x + jnp.transpose(x) for x in on]
    acc[1, 384:512] = jnp.where(rows_of >= lanes_of, on[0], on[1])
    diagonal = jnp.sum(jnp.where(rows_of == lanes_of, on[1], 0.0), axis=0, keepdims=True)
    acc[1, 512:520] = jnp.where(row8 == 0, diagonal, 0.0)
    acc[1, 520:HALF] = jnp.zeros((HALF - 520, 128), f32)

    instant.advance(0)
    lagged.start()
    instant.advance(1)
    instant.advance(2)
    lagged.advance(0)
    instant.advance(3)
    lagged.advance(1)
    instant.arrive()
    means = Means(summed.at[0], summed.at[1])
    means.instant_cov(A)
    means.instant_diagonal(A)
    D = eliminate(A, 0, A[at_block(0), at_block(0)])
    D = eliminate(A, 1, D, lambda: lagged.advance(2))
    D = eliminate(A, 2, D)
    eliminate(A, 3, D, lambda: lagged.advance(3))
    A[at_block(0), at_block(1)] = jnp.zeros((128, 128), f32)
    A[at_block(2), at_block(3)] = jnp.zeros((128, 128), f32)
    whiten(A, means.avg, lhs, white_ref)
    lagged.arrive()
    means.lagged_cov(S)
    instant.close()
    lagged.close()
    swap.wait_send()

    @pl.when(core == 0)
    def _():
        for c in heads:
            c.wait_send()


def sum_scratch():
    bufs, sums, sems = [], [], 0
    for part in PARTS:
        rows = part[1]
        for kind, axis in all_steps(part):
            size = SIZE[axis]
            sems += size
            if kind == "rs":
                rows //= size
                bufs.append(pltpu.VMEM((size - 1, rows, 128), jnp.float32))
                sums.append(pltpu.VMEM((rows, 128), jnp.float32))
            elif kind == "ar":
                bufs.append(pltpu.VMEM((size, rows, 128), jnp.float32))
                sums.append(pltpu.VMEM((rows, 128), jnp.float32))
    return [
        *bufs,
        *sums,
        pltpu.SemaphoreType.DMA((sems,)),
        pltpu.SemaphoreType.DMA((sems,)),
        pltpu.SemaphoreType.DMA((len(PARTS),)),
        pltpu.SemaphoreType.DMA((len(PARTS),)),
    ]


def moments(codes, row_scale, valid):
    vmem = pl.BlockSpec(memory_space=pltpu.VMEM)
    hbm = pl.BlockSpec(memory_space=pltpu.HBM)
    square = jax.ShapeDtypeStruct((codes.shape[1], codes.shape[1]), jnp.float32)
    return pl.pallas_call(
        moments_kernel,
        out_shape=(square, square, jax.ShapeDtypeStruct(codes.shape, codes.dtype)),
        in_specs=[hbm, hbm, pl.BlockSpec(memory_space=pltpu.SMEM)],
        out_specs=(vmem,) * 3,
        scratch_shapes=[
            pltpu.VMEM(codes.shape, codes.dtype),
            pltpu.VMEM(row_scale.shape, row_scale.dtype),
            pltpu.SemaphoreType.DMA((2,)),
            pltpu.VMEM((codes.shape[0] + 16, codes.shape[1]), jnp.bfloat16),
            pltpu.VMEM((4, 512 + LAG, 128), jnp.bfloat16),
            pltpu.VMEM((4, 4, 128, 128), jnp.bfloat16),
            pltpu.VMEM((4, 512, 128), jnp.bfloat16),
            pltpu.VMEM((4, 512, 128), jnp.bfloat16),
            pltpu.VMEM((2, HALF, 128), jnp.float32),
            pltpu.VMEM((2, 2, HALF, 128), jnp.float32),
            pltpu.SemaphoreType.DMA((3,)),
            pltpu.SemaphoreType.DMA((2,)),
            *sum_scratch(),
            *sum_scratch(),
        ],
        compiler_params=pltpu.CompilerParams(
            collective_id=0, has_side_effects=True, vmem_limit_bytes=40 * 2**20
        ),
        name="moments",
    )(codes, row_scale, valid)


HIGHEST = lax.Precision.HIGHEST
ROWS = (((1,), (0,)), ((), ()))
LANES = (((1,), (1,)), ((), ()))
SUBLANES = (((0,), (0,)), ((), ()))


def dot(left, right, dims, precision=HIGHEST):
    return lax.dot_general(left, right, dims, precision=precision, preferred_element_type=jnp.float32)


def one_row(x, k):
    return jnp.broadcast_to(x[k : k + 1, :], (8, 128))


def one_lane(x, k):
    return jnp.broadcast_to(x[:, k : k + 1], (8, 128))


def inverse_factor(block, halfway=None):
    rows = list(block)
    n, size = len(rows), 8
    sub = lax.broadcasted_iota(jnp.int32, (8, 128), 0)
    lane = lax.broadcasted_iota(jnp.int32, (8, 128), 1)
    even = (sub % 2) == 0
    for group in range(0, n, size):
        end = group + size
        coming = [one_lane(rows[group], 8 * group + k) for k in range(8)]
        pivots = []
        for r in range(group, end):
            first = 8 * r
            last = r == end - 1
            columns = [[coming[k]] + [one_lane(rows[q], first + k) for q in range(r + 1, end)] for k in range(8)]
            if not last:
                coming = [one_lane(rows[r + 1], first + 8 + k) for k in range(8)]
            inside = (lane >= first) & (lane < first + 8)
            panel = jnp.where(inside, jnp.where(lane - first == sub, 1.0, 0.0), rows[r])
            for q in range(r + 1, end):
                rows[q] = jnp.where(inside, 0.0, rows[q])
            for k in range(0, 8, 2):
                left, right = columns[k], columns[k + 1]
                a, b, d = one_row(left[0], k), one_row(left[0], k + 1), one_row(right[0], k + 1)
                det = a * d - b * b
                rough = pl.reciprocal(det, approx=True)
                mend = 2.0 - det * rough
                inv = rough * mend
                a_inv, b_inv, d_inv = a * inv, b * inv, d * inv
                low, high = jnp.where(sub > k + 1, left[0], 0.0), jnp.where(sub > k + 1, right[0], 0.0)
                g, h = low * d - high * b, high * a - low * b
                f0 = [g * inv] + [x * d_inv - y * b_inv for x, y in zip(left[1:], right[1:])]
                f1 = [h * inv] + [y * a_inv - x * b_inv for x, y in zip(left[1:], right[1:])]
                for m in range(k + 2, 8):
                    e0, e1 = one_row(left[0], m), one_row(right[0], m)
                    columns[m] = [columns[m][0] - ((g * e0 + h * e1) * rough) * mend] + [
                        x - (u * e0 + v * e1) for x, u, v in zip(columns[m][1:], f0[1:], f1[1:])
                    ]
                if not last:
                    coming = [
                        coming[m] - (f0[1] * one_row(left[1], m) + f1[1] * one_row(right[1], m)) for m in range(8)
                    ]
                row0, row1 = one_row(panel, k), one_row(panel, k + 1)
                panel = panel - (f0[0] * row0 + f1[0] * row1)
                for q in range(r + 1, end):
                    rows[q] = rows[q] - (f0[q - r] * row0 + f1[q - r] * row1)
                if k == 0:
                    pivot = (a, b, det)
                else:
                    pivot = tuple(jnp.where(sub >= k, x, y) for x, y in zip((a, b, det), pivot))
            rows[r] = panel
            pivots.append(pivot)
        for r in range(group, end):
            a, b, det = pivots[r - group]
            above = pltpu.roll(rows[r], 1, 0)
            rows[r] = jnp.where(even, rows[r], rows[r] * a - above * b) * lax.rsqrt(jnp.where(even, a, a * det))
        if end < n:
            done = jnp.concatenate(rows[group:end], axis=0)
            down = lax.broadcasted_iota(jnp.int32, done.shape, 0) + 8 * group
            along = lax.broadcasted_iota(jnp.int32, done.shape, 1)
            change = dot(done, jnp.where((along > down) & (along < 8 * end), 0.0, done), SUBLANES)
            inside = (lane >= 8 * group) & (lane < 8 * end)
            for q in range(end, n):
                rows[q] = jnp.where(inside, 0.0, rows[q]) - change[8 * q : 8 * q + 8]
            if halfway is not None:
                halfway()
    return [jnp.where(lane <= sub + 8 * q, rows[q], 0.0) for q in range(n)]


def split3(x):
    high = x.astype(jnp.bfloat16)
    rest = x - high.astype(jnp.float32)
    middle = rest.astype(jnp.bfloat16)
    return high, middle, (rest - middle.astype(jnp.float32)).astype(jnp.bfloat16)


def at_block(i):
    return slice(128 * i, 128 * i + 128)


def eliminate(A, k, D, halfway=None):
    W = jnp.concatenate(inverse_factor([D[8 * q : 8 * q + 8, :] for q in range(16)], halfway), axis=0)
    A[at_block(k), at_block(k)] = W
    if k < 3:
        near = dot(W, A[at_block(k), at_block(k + 1)], ROWS)
        D = A[at_block(k + 1), at_block(k + 1)] - dot(near, near, SUBLANES)
        A[at_block(k), at_block(k + 1)] = near
    for lo, hi in ((0, 128 * k), (128 * (k + 2), 512)):
        if lo < hi:
            A[at_block(k), lo:hi] = dot(W, A[at_block(k), lo:hi], ROWS)
    if k < 3:
        below = 128 * (k + 1)
        change = dot(A[at_block(k), below:], A[at_block(k), :], SUBLANES)
        A[below:, at_block(k)] = -change[:, at_block(k)]
        if k > 0:
            A[below:, 0 : 128 * k] = A[below:, 0 : 128 * k] - change[:, 0 : 128 * k]
        if k < 2:
            A[below:, below + 128 :] = A[below:, below + 128 :] - change[:, below + 128 :]
    return D


class Means:
    def __init__(self, inst_ref, lag_ref):
        self.inst, self.lag = inst_ref, lag_ref
        self.inv = 1.0 / inst_ref[1, 516:517, :]
        self.avg = [inst_ref[0, 516 + j : 517 + j, :] * self.inv for j in range(4)]
        self.down = [jnp.transpose(jnp.broadcast_to(a, (128, 128))) for a in self.avg]
        self.ri = lax.broadcasted_iota(jnp.int32, (128, 128), 0)
        self.ci = lax.broadcasted_iota(jnp.int32, (128, 128), 1)

    def on_diagonal(self, ref, i):
        stored = ref[i // 2, 384:512] * self.inv
        turned = jnp.transpose(stored)
        if i % 2 == 0:
            return stored, turned, stored
        return turned, stored, ref[i // 2, 512:513] * self.inv

    def instant_cov(self, A):
        for k, pair in enumerate(UPPER):
            for c, (i, j) in enumerate(pair):
                block = self.inst[c, at_block(k)] * self.inv - self.down[i] * self.avg[j]
                if i < j:
                    A[at_block(i), at_block(j)] = block
                else:
                    A[at_block(j), at_block(i)] = jnp.transpose(block)

    def instant_diagonal(self, A):
        for i in range(4):
            own, turned, diagonal = self.on_diagonal(self.inst, i)
            whole = jnp.where(self.ri < self.ci, own, jnp.where(self.ri > self.ci, turned, diagonal))
            A[at_block(i), at_block(i)] = whole - self.down[i] * self.avg[i]

    def lagged_cov(self, S):
        zero = jnp.zeros((128, 128), jnp.float32)
        S[at_block(0), at_block(1)] = zero
        S[at_block(2), at_block(3)] = zero
        for k, pair in enumerate(BLOCKS):
            for c, (i, j) in enumerate(pair):
                S[at_block(j), at_block(i)] = self.lag[c, at_block(k)] * self.inv - self.down[j] * self.avg[i]
        for i in range(4):
            outer = self.down[i] * self.avg[i]
            own, _, diagonal = self.on_diagonal(self.lag, i)
            S[at_block(i), at_block(i)] = jnp.where(
                self.ri > self.ci, own - outer, jnp.where(self.ri == self.ci, 0.5 * (diagonal - outer), 0.0)
            )


def whiten(A, avg, lhs, white_ref):
    a = [A[0:256, 0:256], A[256:512, 0:256], A[256:512, 256:512]]
    am = [jnp.concatenate([t[m] for t in [split3(q) for q in avg]], axis=1) for m in range(3)]
    lhs[256:272, :] = jnp.concatenate(am + [jnp.zeros((13, 512), jnp.bfloat16)], axis=0)
    y = [None, None]
    for t in split3(a[0]):
        v = dot(lhs[:, 0:256], t, LANES, None)
        y[0] = v if y[0] is None else y[0] + v
    for t, u in zip(split3(a[1]), split3(a[2])):
        v = dot(lhs[:, 0:256], t, LANES, None) + dot(lhs[:, 256:512], u, LANES, None)
        y[1] = v if y[1] is None else y[1] + v
    for h in range(2):
        m = y[h][256:257] + y[h][257:258] + y[h][258:259]
        white_ref[:, 256*h:256*h+256] = (y[h][0:256] - m).astype(jnp.bfloat16)


def finish_kernel(A, S, white_in, white_ref, koop_ref, sem):
    handed_on = pltpu.make_async_copy(white_in, white_ref, sem)
    handed_on.start()
    a = [A[0:256, 0:256], A[256:512, 0:256], A[256:512, 256:512]]
    s = [S[0:256, 0:256], S[256:512, 0:256], S[256:512, 256:512]]
    nn = ROWS; nt = LANES
    t00 = dot(a[0], s[0], nn)
    t10 = dot(a[1], s[0], nn) + dot(a[2], s[1], nn)
    t11 = dot(a[2], s[2], nn)
    k00 = dot(t00, a[0], nt)
    k01 = dot(t00, a[1], nt)
    k10 = dot(t10, a[0], nt)
    k11 = dot(t10, a[1], nt) + dot(t11, a[2], nt)
    koop_ref[0:256, 0:256] = k00 + jnp.transpose(k00)
    koop_ref[256:512, 256:512] = k11 + jnp.transpose(k11)
    k10 = k10 + jnp.transpose(k01)
    koop_ref[256:512, 0:256] = k10
    koop_ref[0:256, 256:512] = jnp.transpose(k10)
    handed_on.wait()


def finish(whitener, lagged_cov, whitened):
    return pl.pallas_call(
        finish_kernel,
        out_shape=(
            jax.ShapeDtypeStruct(whitened.shape, whitened.dtype),
            jax.ShapeDtypeStruct(whitener.shape, jnp.float32),
        ),
        in_specs=[pl.BlockSpec(memory_space=pltpu.VMEM)] * 3,
        out_specs=(pl.BlockSpec(memory_space=pltpu.HBM), pl.BlockSpec(memory_space=pltpu.VMEM)),
        scratch_shapes=[pltpu.SemaphoreType.DMA],
        compiler_params=pltpu.CompilerParams(vmem_limit_bytes=40 * 2**20),
        name="finish",
    )(whitener, lagged_cov, whitened)


def on_device(codes, row_scale, valid):
    projected, koopman = finish(*moments(codes[0], row_scale, valid))
    return (projected[None], koopman)


def solution(mesh):
    return jax.shard_map(
        on_device,
        mesh=mesh,
        in_specs=(P("traj", "blk", None), P("traj", "blk"), P("traj")),
        out_specs=(P("traj", "blk", None), P()),
        check_vma=False,
    )
```
